32 devices in a mesh: dp: 8 (over y, x, core), copy: 4 (over z).
Axes of the slice: x: 2, y: 2, z: 4, core: 2. Of those that a mesh axis runs over, the one named last changes fastest.
Arguments:
- block_input: bfloat16 [2, 8, 384, 768], P(None, 'dp', 'copy'), may hold values from -6 to 6
- image_ids: int32 [2, 8, 384], P(None, 'dp'), may hold values from -1 to 3, as said below
- latents: float32 [2, 8, 384, 16], P(None, 'dp'), may hold values from -6 to 6
- noise: float32 [2, 4, 8, 384, 16], P(None, 'copy', 'dp'), may hold values from -6 to 6
- timesteps: int32 [2, 4, 8, 4], P(None, 'copy', 'dp'), may hold values from 0 to 999
- norm_gains: bfloat16 [2, 768], P(None, ('dp', 'copy')), may hold values from 0.5 to 1.5
- block_biases: bfloat16 [6, 768], P(None, ('dp', 'copy')), may hold values from -1.75 to 1.75
- w_qkv: bfloat16 [768, 2304], P(('dp', 'copy')), may hold values from -0.21875 to 0.21875
- w_proj: bfloat16 [768, 768], P(('dp', 'copy')), may hold values from -2.5 to 2.5
- w_up: bfloat16 [768, 3072], P(('dp', 'copy')), may hold values from -0.21875 to 0.21875
- up_bias: bfloat16 [3072], P(('dp', 'copy')), may hold values from -1.75 to 1.75
- w_down: bfloat16 [3072, 768], P(('dp', 'copy')), may hold values from -0.109375 to 0.109375
- head_gain: bfloat16 [1024], P(('dp', 'copy')), may hold values from 0.5 to 1.5
- head_biases: bfloat16 [12, 1024], P(None, ('dp', 'copy')), may hold values from -1.75 to 1.75
- w_cond: bfloat16 [768, 1024], P(('dp', 'copy')), may hold values from -0.21875 to 0.21875
- w_time1: bfloat16 [256, 1024], P(('dp', 'copy')), may hold values from -0.375 to 0.375
- w_time2: bfloat16 [1024, 1024], P(('dp', 'copy')), may hold values from -0.1875 to 0.1875
- w_input: bfloat16 [16, 1024], P(None, ('dp', 'copy')), may hold values from -1.5 to 1.5
- w_ada: bfloat16 [1024, 3072], P(('dp', 'copy')), may hold values from -0.1875 to 0.1875
- w_mlp1: bfloat16 [1024, 1024], P(('dp', 'copy')), may hold values from -0.1875 to 0.1875
- w_mlp2: bfloat16 [1024, 1024], P(('dp', 'copy')), may hold values from -0.1875 to 0.1875
- w_final: bfloat16 [1024, 2048], P(('dp', 'copy')), may hold values from -0.1875 to 0.1875
- w_output: bfloat16 [1024, 16], P(('dp', 'copy')), may hold values from -0.1875 to 0.1875
- output_bias: bfloat16 [16], replicated, may hold values from -1.75 to 1.75
Outputs:
- block_output: bfloat16 [2, 8, 384, 768], P(None, 'dp', 'copy')
- input_grad: float32 [2, 8, 384, 768], P(None, 'dp', 'copy')
- grad_norm_gains: float32 [2, 768], P(None, ('dp', 'copy'))
- grad_block_biases: float32 [6, 768], P(None, ('dp', 'copy'))
- grad_w_qkv: float32 [768, 2304], P(('dp', 'copy'))
- grad_w_proj: float32 [768, 768], P(('dp', 'copy'))
- grad_w_up: float32 [768, 3072], P(('dp', 'copy'))
- grad_up_bias: float32 [3072], P(('dp', 'copy'))
- grad_w_down: float32 [3072, 768], P(('dp', 'copy'))
- grad_head_gain: float32 [1024], P(('dp', 'copy'))
- grad_head_biases: float32 [12, 1024], P(None, ('dp', 'copy'))
- grad_w_cond: float32 [768, 1024], P(('dp', 'copy'))
- grad_w_time1: float32 [256, 1024], P(('dp', 'copy'))
- grad_w_time2: float32 [1024, 1024], P(('dp', 'copy'))
- grad_w_input: float32 [16, 1024], P(None, ('dp', 'copy'))
- grad_w_ada: float32 [1024, 3072], P(('dp', 'copy'))
- grad_w_mlp1: float32 [1024, 1024], P(('dp', 'copy'))
- grad_w_mlp2: float32 [1024, 1024], P(('dp', 'copy'))
- grad_w_final: float32 [1024, 2048], P(('dp', 'copy'))
- grad_w_output: float32 [1024, 16], P(('dp', 'copy'))
- grad_output_bias: float32 [16], replicated
The draws below stay inside these ranges and needn't reach their ends.
Inputs may be any that keep to these rules, and one draw needn't show every extreme that they name: `image_ids`: along a sequence the ids never fall; -1 marks padding, which comes only at a sequence's end.
All inputs are finite; a program needn't handle non-finite values.
Results may differ from the reference program's by a relative error of at most 0.013.
Values may be sent and summed in bfloat16 or wider, within the bound.
No kernel may reach another device: no remote copies, remote signals or barrier semaphores. Data moves between devices by JAX's collectives and lax.ppermute only.
A program may use at most 128 MiB of HBM per device.

```python
import math
import jax
import jax.numpy as jnp
from jax import lax

D = 768
HEADS = 12
HEAD_DIM = 64
FF = 3072
WIDTH = 1024
FREQ = 256
CHANNELS = 16
IMAGES = 4
MICRO = 2
TOK_DEV = 96
SEQ = 384
SEQS = 8
N_COPY = 4


def draw_image_ids(key, part):
    key = jax.random.fold_in(key, 11)
    count = MICRO * SEQS
    lead = jax.random.randint(jax.random.fold_in(key, 1), (count,), 1, TOK_DEV // 2)
    tail = jax.random.randint(jax.random.fold_in(key, 2), (count,), TOK_DEV // 4 + 2, TOK_DEV // 2 + 2)
    padding = jax.random.randint(jax.random.fold_in(key, 3), (count,), 0, 1 << 20) % (tail // 2) + 1
    remain = tail - padding
    split_at = jax.random.randint(jax.random.fold_in(key, 4), (count,), 0, 1 << 20) % (remain - 1) + 1
    position = jnp.arange(SEQ, dtype=jnp.int32)[None, :]
    long_end = (SEQ - tail)[:, None]
    image_ids = jnp.where(position < lead[:, None], 0, jnp.where(position < long_end, 1, jnp.where(position < long_end + split_at[:, None], 2, jnp.where(position < (SEQ - padding)[:, None], 3, -1))))
    return image_ids.reshape(MICRO, SEQS, SEQ).astype(jnp.int32)


def place_ends(result, stream_key, smallest, top_value):
    dims = result.shape
    place = [jax.random.randint(jax.random.fold_in(stream_key, axis), (), 0, dims[axis]) for axis in range(len(dims))]
    result = result.at[tuple(place)].set(smallest)
    longest = dims.index(max(dims))
    place[longest] = (place[longest] + 1) % dims[longest]
    return result.at[tuple(place)].set(top_value)


def level_of(rng, dims, split, least, high):
    factor_of = 1.0
    for dim, shards_of in split:
        heights = jax.random.uniform(jax.random.fold_in(jax.random.fold_in(rng, 6), dim), (shards_of,), jnp.float32, least / len(split), high / len(split))
        factor_of = factor_of * jnp.repeat(jnp.exp(heights), dims[dim] // shards_of).reshape((-1,) + (1,) * (len(dims) - 1 - dim))
    return factor_of


def scatter_about(own_key, shape, spread, limit, split=(), kind=jnp.bfloat16):
    gain = level_of(own_key, shape, split, -0.22, 0.18) if split else 1.0
    drawn = jax.random.normal(own_key, shape, jnp.float32) * spread * gain
    return jnp.minimum(jnp.maximum(drawn, -limit), limit).astype(kind)


def setup_inputs(seed: int = 0) -> dict:
    keys = jax.random.split(jax.random.key(seed), 25)
    block_input = scatter_about(keys[0], (MICRO, SEQS, SEQ, D), 1.0, 6.0, ((1, 8), (2, 4)))
    image_ids = draw_image_ids(jax.random.fold_in(keys[24], 71), 0)
    latents = scatter_about(keys[2], (MICRO, SEQS, SEQ, CHANNELS), 1.0, 6.0, ((1, 8),), jnp.float32)
    noise = scatter_about(keys[3], (MICRO, N_COPY, SEQS, SEQ, CHANNELS), 1.0, 6.0, ((1, 4), (2, 8)), jnp.float32)
    timesteps = place_ends(jax.random.randint(keys[4], (MICRO, N_COPY, SEQS, IMAGES), 0, 1000), jax.random.fold_in(keys[4], 1), 0, 999).astype(jnp.int32)
    norm_gains = jnp.clip(1.0 + 0.1 * jax.random.normal(keys[5], (2, D), jnp.float32), 0.5, 1.5).astype(jnp.bfloat16)
    block_biases = scatter_about(keys[6], (6, D), 0.3, 1.75, ((1, 32),))
    w_qkv = scatter_about(keys[7], (D, 3 * D), D ** -0.5, 0.21875, ((0, 32),))
    w_proj = scatter_about(keys[8], (D, D), (max(D // 128, 1)) ** -0.5, 2.5, ((0, 32),))
    w_up = scatter_about(keys[9], (D, FF), D ** -0.5, 0.21875, ((0, 32),))
    up_bias = scatter_about(keys[10], (FF,), 0.3, 1.75, ((0, 32),))
    w_down = scatter_about(keys[11], (FF, D), FF ** -0.5, 0.109375, ((0, 32),))
    head_gain = jnp.clip(1.0 + 0.1 * jax.random.normal(keys[12], (WIDTH,), jnp.float32), 0.5, 1.5).astype(jnp.bfloat16)
    head_biases = scatter_about(keys[13], (12, WIDTH), 0.3, 1.75, ((1, 32),))
    w_cond = scatter_about(keys[14], (D, WIDTH), D ** -0.5, 0.21875, ((0, 32),))
    w_time1 = scatter_about(keys[15], (FREQ, WIDTH), FREQ ** -0.5, 0.375, ((0, 32),))
    w_time2 = scatter_about(keys[16], (WIDTH, WIDTH), WIDTH ** -0.5, 0.1875, ((0, 32),))
    w_input = scatter_about(keys[17], (CHANNELS, WIDTH), CHANNELS ** -0.5, 1.5, ((1, 32),))
    w_ada = scatter_about(keys[18], (WIDTH, 3 * WIDTH), WIDTH ** -0.5, 0.1875, ((0, 32),))
    w_mlp1 = scatter_about(keys[19], (WIDTH, WIDTH), WIDTH ** -0.5, 0.1875, ((0, 32),))
    w_mlp2 = scatter_about(keys[20], (WIDTH, WIDTH), WIDTH ** -0.5, 0.1875, ((0, 32),))
    w_final = scatter_about(keys[21], (WIDTH, 2 * WIDTH), WIDTH ** -0.5, 0.1875, ((0, 32),))
    w_output = scatter_about(keys[22], (WIDTH, CHANNELS), WIDTH ** -0.5, 0.1875, ((0, 32),))
    output_bias = scatter_about(keys[23], (CHANNELS,), 0.3, 1.75)
    return {"block_input": block_input, "image_ids": image_ids, "latents": latents, "noise": noise, "timesteps": timesteps, "norm_gains": norm_gains, "block_biases": block_biases, "w_qkv": w_qkv, "w_proj": w_proj, "w_up": w_up, "up_bias": up_bias, "w_down": w_down, "head_gain": head_gain, "head_biases": head_biases, "w_cond": w_cond, "w_time1": w_time1, "w_time2": w_time2, "w_input": w_input, "w_ada": w_ada, "w_mlp1": w_mlp1, "w_mlp2": w_mlp2, "w_final": w_final, "w_output": w_output, "output_bias": output_bias}


@jax.custom_vjp
def low(v):
    return lax.optimization_barrier(v.astype(jnp.bfloat16)).astype(jnp.float32)

@jax.custom_vjp
def low_back(v):
    return v

def low_keep(v):
    return (low(v), None)

def low_pass(kept, grad):
    return (grad,)

def back_keep(v):
    return (v, None)

def back_low(kept, grad):
    return (low(grad),)
low.defvjp(low_keep, low_pass)
low_back.defvjp(back_keep, back_low)
epsilon = 1e-06
highest = lax.Precision.HIGHEST

def matmul(left_side, right_side):
    return jnp.dot(left_side, right_side, precision=highest, preferred_element_type=jnp.float32)

def layer_norm(values):
    center = values - lax.optimization_barrier(jnp.mean(values, axis=-1, keepdims=True))
    return center * lax.rsqrt(lax.optimization_barrier(jnp.mean(center * center, axis=-1, keepdims=True)) + epsilon)

def sinusoid(step_vals):
    half_width = FREQ // 2
    rates = jnp.exp(-math.log(10000.0) * jnp.arange(half_width, dtype=jnp.float32) / half_width)
    angles = step_vals[:, None] * rates[None, :]
    return jnp.concatenate([jnp.cos(angles), jnp.sin(angles)], axis=1)

def plan(step_vals):
    anchor = math.cos(0.008 / 1.008 * math.pi / 2.0) ** 2
    angle_now = ((step_vals + 1.0) / 1000.0 + 0.008) / 1.008 * (math.pi / 2.0)
    signal = jnp.cos(angle_now) ** 2 / anchor
    return jnp.stack([jnp.sqrt(signal), jnp.sqrt(1.0 - signal)], axis=1)

def block_and_head(params, rows, image_row, latent_rows, noise_rows, step_rows):
    norm_gains, block_biases, w_qkv, w_proj, w_up, up_bias, w_down, head_gain, head_biases, w_cond, w_time1, w_time2, w_input, w_ada, w_mlp1, w_mlp2, w_final, w_output, output_bias = params
    length = rows.shape[0]
    score_scale = HEAD_DIM ** (-0.5)
    first_in = low(layer_norm(rows) * norm_gains[0] + block_biases[0])
    zeros_key = jnp.zeros((D,), jnp.float32)
    projected = matmul(first_in, w_qkv) + jnp.concatenate([block_biases[1], zeros_key, block_biases[2]])
    projected = low(low_back(projected))
    queries = projected[:, :D].reshape(length, HEADS, HEAD_DIM)
    key_rows = projected[:, D:2 * D].reshape(length, HEADS, HEAD_DIM)
    value_rows = projected[:, 2 * D:].reshape(length, HEADS, HEAD_DIM)
    scores = low_back(jnp.einsum('qhd,khd->hqk', queries, key_rows, precision=highest) * score_scale)
    same_image = image_row[:, None] == image_row[None, :]
    scores = jnp.where(same_image[None], scores, -1e+30)
    attn_weights = low(jax.nn.softmax(scores, axis=-1))
    mixed = jnp.einsum('hqk,khd->qhd', attn_weights, value_rows, precision=highest).reshape(length, D)
    mixed = low(low_back(mixed))
    middle = rows + low_back(matmul(mixed, w_proj) + block_biases[3])
    second_in = low(layer_norm(middle) * norm_gains[1] + block_biases[4])
    hidden = low_back(matmul(second_in, w_up) + up_bias)
    active = low(jax.nn.gelu(hidden, approximate=False))
    output = middle + low_back(matmul(active, w_down) + block_biases[5])
    condition = low(output)
    valid_rows = (image_row >= 0).astype(jnp.float32)
    image_onehot = (image_row[:, None] == jnp.arange(IMAGES, dtype=jnp.int32)[None, :]).astype(jnp.float32)
    cond_part = low_back(matmul(condition, w_cond) + head_biases[0])
    ada_bias = head_biases[7:10].reshape(3 * WIDTH)
    final_bias = head_biases[10:12].reshape(2 * WIDTH)
    total = jnp.zeros((), jnp.float32)
    for noise_copy in range(N_COPY):
        step_vals = step_rows[noise_copy].astype(jnp.float32)
        sinusoid_in = low(sinusoid(step_vals))
        time_one = low_back(matmul(sinusoid_in, w_time1) + head_biases[1])
        time_act = low(jax.nn.silu(time_one))
        embedded = low_back(matmul(time_act, w_time2) + head_biases[2])
        cond_all = cond_part + matmul(image_onehot, embedded)
        gated = low(jax.nn.silu(cond_all))
        modulation = low_back(matmul(gated, w_ada) + ada_bias)
        shift_rows = modulation[:, :WIDTH]
        scale_rows = modulation[:, WIDTH:2 * WIDTH]
        gate_rows = modulation[:, 2 * WIDTH:]
        mixing = matmul(image_onehot, plan(step_vals))
        noisy = latent_rows * mixing[:, 0:1] + noise_rows[noise_copy] * mixing[:, 1:2]
        entry_rows = low_back(matmul(low(noisy), w_input) + head_biases[3])
        affine = layer_norm(entry_rows) * head_gain + head_biases[4]
        mlp_in = low(affine * (1.0 + scale_rows) + shift_rows)
        inner_one = low_back(matmul(mlp_in, w_mlp1) + head_biases[5])
        inner_two = low_back(matmul(low(jax.nn.silu(inner_one)), w_mlp2) + head_biases[6])
        residual = entry_rows + gate_rows * inner_two
        final_mod = low_back(matmul(gated, w_final) + final_bias)
        final_in = low(layer_norm(residual) * (1.0 + final_mod[:, WIDTH:]) + final_mod[:, :WIDTH])
        predicted = low_back(matmul(final_in, w_output) + output_bias)
        error = predicted - noise_rows[noise_copy]
        total = total + 0.5 * jnp.sum(valid_rows[:, None] * error * error)
    return (total, output)

def reference(block_input, image_ids, latents, noise, timesteps, norm_gains, block_biases, w_qkv, w_proj, w_up, up_bias, w_down, head_gain, head_biases, w_cond, w_time1, w_time2, w_input, w_ada, w_mlp1, w_mlp2, w_final, w_output, output_bias):
    params = tuple((item.astype(jnp.float32) for item in (norm_gains, block_biases, w_qkv, w_proj, w_up, up_bias, w_down, head_gain, head_biases, w_cond, w_time1, w_time2, w_input, w_ada, w_mlp1, w_mlp2, w_final, w_output, output_bias)))
    count = MICRO * SEQS
    rows_all = block_input.astype(jnp.float32).reshape(count, SEQ, D)
    ids_all = image_ids.reshape(count, SEQ).astype(jnp.int32)
    latent_all = latents.astype(jnp.float32).reshape(count, SEQ, CHANNELS)
    noise_all = jnp.swapaxes(noise.astype(jnp.float32), 1, 2).reshape(count, N_COPY, SEQ, CHANNELS)
    steps_all = jnp.swapaxes(timesteps, 1, 2).reshape(count, N_COPY, IMAGES)

    def one_sequence(carry, item):
        rows, image_row, latent_rows, noise_rows, step_rows = item

        def objective(weights, inputs):
            return block_and_head(weights, inputs, image_row, latent_rows, noise_rows, step_rows)
        loss, pullback, output = jax.vjp(objective, params, rows, has_aux=True)
        weight_grads, row_grads = pullback(jnp.ones_like(loss))
        carry = jax.tree.map(jnp.add, carry, weight_grads)
        return (carry, (output.astype(jnp.bfloat16), row_grads))
    start = jax.tree.map(jnp.zeros_like, params)
    totals, (outputs, row_grads) = lax.scan(one_sequence, start, (rows_all, ids_all, latent_all, noise_all, steps_all))
    block_output = outputs.reshape(MICRO, SEQS, SEQ, D)
    input_grad = row_grads.reshape(MICRO, SEQS, SEQ, D)
    return (block_output, input_grad, totals[0], totals[1], totals[2], totals[3], totals[4], totals[5], totals[6], totals[7], totals[8], totals[9], totals[10], totals[11], totals[12], totals[13], totals[14], totals[15], totals[16], totals[17], totals[18])
```

```python
import math

import jax
import jax.numpy as jnp
from jax import lax
from jax.sharding import PartitionSpec as P

D = 768
HEADS = 12
HEAD_DIM = 64
WIDTH = 1024
FREQ = 256
CHANNELS = 16
IMAGES = 4


epsilon = 1e-06
highest = lax.Precision.HIGHEST


def product(left_side, right_side):
    return jnp.dot(left_side, right_side, preferred_element_type=jnp.float32)


def weight_grad(left_side, right_side):
    return lax.dot_general(
        left_side, right_side, (((0,), (0,)), ((), ())), preferred_element_type=jnp.float32
    )


def input_back(gradient, weight):
    return lax.dot_general(
        gradient, weight, (((1,), (1,)), ((), ())), preferred_element_type=jnp.float32
    )


def column_sum(values):
    return jnp.sum(values.astype(jnp.float32), axis=0)


def normalize(values):
    center = values - jnp.mean(values, axis=-1, keepdims=True)
    inverse = lax.rsqrt(jnp.mean(center * center, axis=-1, keepdims=True) + epsilon)
    return (center * inverse, inverse)


def norm_back(gradient, normed, inverse):
    return inverse * (
        gradient
        - jnp.mean(gradient, axis=-1, keepdims=True)
        - normed * jnp.mean(gradient * normed, axis=-1, keepdims=True)
    )


def silu_slope(values):
    sigma = jax.nn.sigmoid(values)
    return sigma * (1.0 + values * (1.0 - sigma))


def gelu_slope(values):
    return 0.5 * (1.0 + lax.erf(values * 2.0 ** (-0.5))) + values * jnp.exp(
        -0.5 * values * values
    ) * (2.0 * math.pi) ** (-0.5)


def sinusoid(step_vals):
    half_width = FREQ // 2
    rates = jnp.exp(-math.log(10000.0) * jnp.arange(half_width, dtype=jnp.float32) / half_width)
    angles = step_vals[:, None] * rates[None, :]
    return jnp.concatenate([jnp.cos(angles), jnp.sin(angles)], axis=1)


def plan(step_vals):
    anchor = math.cos(0.008 / 1.008 * math.pi / 2.0) ** 2
    angle_now = ((step_vals + 1.0) / 1000.0 + 0.008) / 1.008 * (math.pi / 2.0)
    signal = jnp.cos(angle_now) ** 2 / anchor
    return jnp.stack([jnp.sqrt(signal), jnp.sqrt(1.0 - signal)], axis=1)


def tdot(left_side, right_side):
    return lax.dot_general(
        left_side, right_side, (((0,), (0,)), ((), ())), preferred_element_type=jnp.float32
    )


def swap_bit(values, size, bit):
    return lax.ppermute(values, "dp", [(i, i ^ (1 << bit)) for i in range(size)])


def shift_copy(values, size, shift):
    return lax.ppermute(values, "copy", [(i, (i + shift) % size) for i in range(size)])


def copy_gather(values, size):
    parts = [values] + [shift_copy(values, size, size - j) for j in range(1, size)]
    return jnp.stack(parts)


def copy_reduce(chunks, size):
    total = chunks[0].astype(jnp.float32)
    for j in range(1, size):
        total = total + shift_copy(chunks[j], size, j).astype(jnp.float32)
    return total


def pick(values, index, axis):
    return lax.dynamic_index_in_dim(values, index, axis, keepdims=False)


def scatter_bits(values, me, size, bits):
    for bit in bits:
        mine = (me >> bit) & 1
        send = pick(values, 1 - mine, 0).astype(jnp.bfloat16)
        keep = pick(values, mine, 0)
        got = swap_bit(send, size, bit)
        values = (keep.astype(jnp.float32) + got.astype(jnp.float32)).astype(jnp.bfloat16)
    return values


def reduce_dp(values, size):
    me = lax.axis_index("dp")
    levels = size.bit_length() - 1
    rows, width = values.shape[1:]
    cube = values.reshape((2,) * levels + (rows, width))
    cube = jnp.moveaxis(cube, levels - 1, 0)
    cube = scatter_bits(cube, me, size, [0])
    rest = list(range(levels - 1, 0, -1))
    half = rows // 2 // 8 * 8
    first = scatter_bits(cube[..., :half, :], me, size, rest)
    second_cube = cube[..., half:, :]
    second_cube = jnp.transpose(
        second_cube, tuple(range(levels - 1))[::-1] + (levels - 1, levels)
    )
    second = scatter_bits(second_cube, me, size, rest[::-1])
    return jnp.concatenate([first, second], axis=0)


def reduce_all(values, dp_size, copy_size):
    rows, width = values.shape[2:]
    got = reduce_dp(values.reshape(dp_size, copy_size * rows, width), dp_size)
    got = got.reshape(copy_size, rows, width)
    me = lax.axis_index("copy")
    chunks = [pick(got, lax.rem(me + j, copy_size), 0) for j in range(copy_size)]
    return copy_reduce(chunks, copy_size)


def shards(
    block_input,
    image_ids,
    latents,
    noise,
    timesteps,
    norm_gains,
    block_biases,
    w_qkv,
    w_proj,
    w_up,
    up_bias,
    w_down,
    head_gain,
    head_biases,
    w_cond,
    w_time1,
    w_time2,
    w_input,
    w_ada,
    w_mlp1,
    w_mlp2,
    w_final,
    w_output,
    output_bias,
):
    bf16, f32 = jnp.bfloat16, jnp.float32
    dp_size, copy_size = lax.axis_size("dp"), lax.axis_size("copy")
    world = dp_size * copy_size
    place = lax.axis_index("copy")
    micros, _, own, _ = block_input.shape
    length = image_ids.shape[2]
    total = micros * length
    k_d, k_ff, k_w, k_t = D // world, w_down.shape[0], WIDTH // world, w_time1.shape[0]
    ff = k_ff * world
    score_scale = HEAD_DIM ** (-0.5)

    def cut(matrix, width):
        return [matrix[:, i : i + width] for i in range(0, matrix.shape[1], width)]

    def pad_flat(parts, width):
        flat = jnp.concatenate([p.reshape(-1) for p in parts])
        count = -(-flat.shape[0] // (8 * width)) * 8 * width
        return jnp.pad(flat, (0, count - flat.shape[0])).reshape(-1, width)

    block_parts = (
        cut(w_qkv, D)
        + [w_proj]
        + cut(w_up, D)
        + [w_down, pad_flat([norm_gains, block_biases, up_bias], D)]
    )
    head_parts = (
        [w_cond]
        + cut(w_ada, WIDTH)
        + [w_mlp1, w_mlp2]
        + cut(w_final, WIDTH)
        + [w_time1, w_time2, pad_flat([w_input, w_output, head_gain, head_biases], WIDTH)]
    )
    block_pack = lax.all_gather(jnp.concatenate(block_parts, 0), ("dp", "copy"), axis=0)
    head_pack = lax.all_gather(jnp.concatenate(head_parts, 0), ("dp", "copy"), axis=0)

    rows = jnp.moveaxis(copy_gather(block_input[:, 0], copy_size), 0, 1)
    rows = rows.reshape(total, D).astype(f32)

    def turned(values):
        twice = jnp.concatenate([values, values], axis=1)
        return lax.dynamic_slice_in_dim(twice, place * own, length, 1)

    ids = turned(image_ids[:, 0])
    latent_rows = turned(latents[:, 0]).reshape(total, CHANNELS)
    noise_rows = turned(noise[:, 0, 0]).reshape(total, CHANNELS)

    def unpack(pack, parts):
        out, at = [], 0
        for part in parts:
            out.append(pack[:, at : at + part.shape[0]].reshape(-1, pack.shape[2]))
            at += part.shape[0]
        return out

    block_full = unpack(block_pack, block_parts)
    w_q, w_k, w_v, w_proj_full = block_full[:4]
    w_up_full = jnp.concatenate(block_full[4:8], axis=1)
    w_down_full = block_full[8]
    small = block_full[9].reshape(world, -1)
    gains = small[:, : 2 * k_d].reshape(world, 2, k_d)
    gains = jnp.moveaxis(gains, 0, 1).reshape(2, D).astype(f32)
    biases = small[:, 2 * k_d : 8 * k_d].reshape(world, 6, k_d)
    biases = jnp.moveaxis(biases, 0, 1).reshape(6, D).astype(f32)
    up_bias_full = small[:, 8 * k_d : 8 * k_d + k_ff].reshape(ff).astype(f32)

    norm_one, inv_one = normalize(rows)
    first_in = (norm_one * gains[0] + biases[0]).astype(bf16)
    queries = (product(first_in, w_q) + biases[1]).astype(bf16)
    key_rows = product(first_in, w_k).astype(bf16)
    value_rows = (product(first_in, w_v) + biases[2]).astype(bf16)
    queries = queries.reshape(micros, length, HEADS, HEAD_DIM)
    key_rows = key_rows.reshape(micros, length, HEADS, HEAD_DIM)
    value_rows = value_rows.reshape(micros, length, HEADS, HEAD_DIM)
    same_image = (ids[:, :, None] == ids[:, None, :])[:, None]

    def attention_scores():
        scores = jnp.einsum("bqhd,bkhd->bhqk", queries, key_rows, preferred_element_type=f32)
        return jnp.where(same_image, scores * score_scale, -1e30)

    scores = attention_scores()
    row_max = jnp.max(scores, axis=-1, keepdims=True)
    exp_scores = jnp.exp(scores - row_max)
    row_total = jnp.sum(exp_scores, axis=-1, keepdims=True)
    log_total = row_max + jnp.log(row_total)
    attn_weights = (exp_scores / row_total).astype(bf16)
    mixed = jnp.einsum("bhqk,bkhd->bqhd", attn_weights, value_rows, preferred_element_type=f32)
    mixed = mixed.reshape(total, D).astype(bf16)
    middle = rows + product(mixed, w_proj_full) + biases[3]
    norm_two, inv_two = normalize(middle)
    second_in = (norm_two * gains[1] + biases[4]).astype(bf16)
    hidden = product(second_in, w_up_full) + up_bias_full
    active = jax.nn.gelu(hidden, approximate=False).astype(bf16)
    output = middle + product(active, w_down_full) + biases[5]
    condition = output.astype(bf16)

    head_full = unpack(head_pack, head_parts)
    w_cond_full, w_shift, w_scale, w_gate, w_one, w_two, w_fshift, w_fscale = head_full[:8]
    w_time1_full, w_time2_full = head_full[8:10]
    small = head_full[10].reshape(world, -1)
    at = CHANNELS * k_w
    w_input_full = small[:, :at].reshape(world, CHANNELS, k_w)
    w_input_full = jnp.moveaxis(w_input_full, 0, 1).reshape(CHANNELS, WIDTH)
    w_output_full = small[:, at : 2 * at].reshape(WIDTH, CHANNELS)
    head_gain_f = small[:, 2 * at : 2 * at + k_w].reshape(WIDTH).astype(f32)
    head_bias = small[:, 2 * at + k_w : 2 * at + 13 * k_w].reshape(world, 12, k_w)
    head_bias = jnp.moveaxis(head_bias, 0, 1).reshape(12, WIDTH).astype(f32)

    valid_rows = (ids >= 0).astype(f32).reshape(total, 1)
    slots = jnp.arange(micros * IMAGES, dtype=jnp.int32)
    row_slot = ids + IMAGES * jnp.arange(micros, dtype=jnp.int32)[:, None]
    row_slot = jnp.where(ids >= 0, row_slot, -1).reshape(total, 1)
    image_onehot = (row_slot == slots[None, :]).astype(f32)
    step_vals = timesteps[:, 0, 0].reshape(micros * IMAGES).astype(f32)
    sinusoid_in = sinusoid(step_vals).astype(bf16)
    time_one = product(sinusoid_in, w_time1_full) + head_bias[1]
    time_act = jax.nn.silu(time_one).astype(bf16)
    embedded = product(time_act, w_time2_full) + head_bias[2]
    cond_all = (
        product(condition, w_cond_full)
        + head_bias[0]
        + jnp.dot(image_onehot, embedded, precision=highest, preferred_element_type=f32)
    )
    gated = jax.nn.silu(cond_all).astype(bf16)
    shift_rows = product(gated, w_shift) + head_bias[7]
    scale_rows = product(gated, w_scale) + head_bias[8]
    gate_rows = product(gated, w_gate) + head_bias[9]
    mixing = jnp.dot(image_onehot, plan(step_vals), precision=highest, preferred_element_type=f32)
    noisy = (latent_rows * mixing[:, 0:1] + noise_rows * mixing[:, 1:2]).astype(bf16)
    entry_rows = product(noisy, w_input_full) + head_bias[3]
    norm_head, inv_head = normalize(entry_rows)
    affine = norm_head * head_gain_f + head_bias[4]
    mlp_in = (affine * (1.0 + scale_rows) + shift_rows).astype(bf16)
    inner_one = product(mlp_in, w_one) + head_bias[5]
    inner_act = jax.nn.silu(inner_one).astype(bf16)
    inner_two = product(inner_act, w_two) + head_bias[6]
    residual = entry_rows + gate_rows * inner_two
    fshift_rows = product(gated, w_fshift) + head_bias[10]
    fscale_rows = product(gated, w_fscale) + head_bias[11]
    norm_final, inv_final = normalize(residual)
    final_in = (norm_final * (1.0 + fscale_rows) + fshift_rows).astype(bf16)
    predicted = product(final_in, w_output_full) + output_bias.astype(f32)

    grad_pred = ((predicted - noise_rows) * valid_rows).astype(bf16)
    grad_out_bias = lax.psum(column_sum(grad_pred), ("dp", "copy"))
    grad_w_output = weight_grad(final_in, grad_pred)
    grad_final_in = input_back(grad_pred, w_output_full)
    grad_fshift = grad_final_in.astype(bf16)
    grad_fscale = (grad_final_in * norm_final).astype(bf16)
    grad_residual = norm_back(grad_final_in * (1.0 + fscale_rows), norm_final, inv_final)
    grad_gated = input_back(grad_fshift, w_fshift) + input_back(grad_fscale, w_fscale)
    grad_inner_two = (grad_residual * gate_rows).astype(bf16)
    grad_inner_one = (input_back(grad_inner_two, w_two) * silu_slope(inner_one)).astype(bf16)
    grad_mlp_in = input_back(grad_inner_one, w_one)
    grad_shift = grad_mlp_in.astype(bf16)
    grad_scale = (grad_mlp_in * affine).astype(bf16)
    grad_gate = (grad_residual * inner_two).astype(bf16)
    grad_affine = grad_mlp_in * (1.0 + scale_rows)
    grad_head_gain = jnp.sum(grad_affine * norm_head, axis=0)
    grad_entry = grad_residual + norm_back(grad_affine * head_gain_f, norm_head, inv_head)
    grad_entry = grad_entry.astype(bf16)
    grad_w_input = weight_grad(noisy, grad_entry)
    grad_gated = (
        grad_gated
        + input_back(grad_shift, w_shift)
        + input_back(grad_scale, w_scale)
        + input_back(grad_gate, w_gate)
    )
    grad_cond = grad_gated * silu_slope(cond_all)
    grad_cond_low = grad_cond.astype(bf16)
    grad_condition = input_back(grad_cond_low, w_cond_full).astype(bf16)

    chunks = grad_condition.reshape(micros, copy_size, own, D)
    grad_z_own = copy_reduce([chunks[:, j] for j in range(copy_size)], copy_size).astype(bf16)

    grad_embedded = lax.dot_general(
        image_onehot,
        grad_cond,
        (((0,), (0,)), ((), ())),
        precision=highest,
        preferred_element_type=f32,
    ).astype(bf16)
    grad_time_one = (input_back(grad_embedded, w_time2_full) * silu_slope(time_one)).astype(bf16)

    def grad_pack(pieces, width):
        split = [p.astype(bf16).reshape(dp_size, copy_size, -1, width) for p in pieces]
        return jnp.concatenate(split, axis=2)

    def split_pack(pack, parts):
        out, at = [], 0
        for rows_of in parts:
            out.append(pack[at : at + rows_of])
            at += rows_of
        return out

    pack_one = grad_pack(
        [
            weight_grad(gated, grad_fshift),
            weight_grad(gated, grad_fscale),
            weight_grad(inner_act, grad_inner_two),
            weight_grad(mlp_in, grad_inner_one),
        ],
        WIDTH,
    )
    own_fshift, own_fscale, own_two, own_one = split_pack(
        reduce_all(pack_one, dp_size, copy_size), [k_w] * 4
    )
    head_bias_grad = jnp.stack(
        [
            column_sum(grad_cond_low),
            column_sum(grad_time_one),
            column_sum(grad_embedded),
            column_sum(grad_entry),
            jnp.sum(grad_affine, axis=0),
            column_sum(grad_inner_one),
            column_sum(grad_inner_two),
            column_sum(grad_shift),
            column_sum(grad_scale),
            column_sum(grad_gate),
            column_sum(grad_fshift),
            column_sum(grad_fscale),
        ]
    )

    def owned(values, count):
        return jnp.moveaxis(values.reshape(count, world, -1), 1, 0).reshape(world, -1)

    small_grads = jnp.concatenate(
        [
            owned(grad_w_input, CHANNELS),
            grad_w_output.reshape(world, -1),
            owned(grad_head_gain[None], 1),
            owned(head_bias_grad, 12),
        ],
        axis=1,
    )
    small_rows = -(-small_grads.shape[1] // (8 * WIDTH)) * 8
    small_grads = jnp.pad(
        small_grads, ((0, 0), (0, small_rows * WIDTH - small_grads.shape[1]))
    ).reshape(world * small_rows, WIDTH)
    pack_two = grad_pack(
        [
            weight_grad(gated, grad_shift),
            weight_grad(gated, grad_scale),
            weight_grad(gated, grad_gate),
            weight_grad(condition, grad_cond_low),
            weight_grad(time_act, grad_embedded),
            weight_grad(sinusoid_in, grad_time_one),
            small_grads,
        ],
        WIDTH,
    )
    own_shift, own_scale, own_gate, own_cond, own_time2, own_time1, own_small = split_pack(
        reduce_all(pack_two, dp_size, copy_size), [k_w] * 3 + [k_d, k_w, k_t, small_rows]
    )
    own_small = own_small.reshape(-1)
    own_w_input = own_small[:at].reshape(CHANNELS, k_w)
    own_w_output = own_small[at : 2 * at].reshape(k_w, CHANNELS)
    own_head_gain = own_small[2 * at : 2 * at + k_w]
    own_head_biases = own_small[2 * at + k_w : 2 * at + 13 * k_w].reshape(12, k_w)

    grad_z = jnp.moveaxis(copy_gather(grad_z_own, copy_size), 0, 1).reshape(total, D)
    grad_down = grad_z
    grad_hidden = (input_back(grad_down, w_down_full) * gelu_slope(hidden)).astype(bf16)
    grad_second = input_back(grad_hidden, w_up_full)
    grad_middle = grad_z.astype(f32) + norm_back(grad_second * gains[1], norm_two, inv_two)
    grad_branch = grad_middle.astype(bf16)
    grad_mixed = input_back(grad_branch, w_proj_full).astype(bf16)
    grad_mixed = grad_mixed.reshape(micros, length, HEADS, HEAD_DIM)
    probs = jnp.exp(attention_scores() - log_total)
    grad_probs = jnp.einsum("bqhd,bkhd->bhqk", grad_mixed, value_rows, preferred_element_type=f32)
    delta = jnp.sum(grad_probs * probs, axis=-1, keepdims=True)
    grad_scores = (probs * (grad_probs - delta)).astype(bf16)
    grad_queries = (
        jnp.einsum("bhqk,bkhd->bqhd", grad_scores, key_rows, preferred_element_type=f32)
        * score_scale
    )
    grad_keys = (
        jnp.einsum("bhqk,bqhd->bkhd", grad_scores, queries, preferred_element_type=f32)
        * score_scale
    )
    grad_values = jnp.einsum(
        "bhqk,bqhd->bkhd", probs.astype(bf16), grad_mixed, preferred_element_type=f32
    )
    grad_q = grad_queries.astype(bf16).reshape(total, D)
    grad_k = grad_keys.astype(bf16).reshape(total, D)
    grad_v = grad_values.astype(bf16).reshape(total, D)
    grad_first = input_back(grad_q, w_q) + input_back(grad_k, w_k) + input_back(grad_v, w_v)

    def chosen(values):
        width = values.shape[1]
        k = width // world
        source = jnp.arange(width, dtype=jnp.int32)[:, None]
        target = jnp.arange(dp_size * k, dtype=jnp.int32)[None, :]
        wanted = (target // k * copy_size + place) * k + target % k
        return product(values, (source == wanted).astype(bf16)).astype(bf16)

    def block_pack_of(pieces, width):
        split = [p.astype(bf16).reshape(dp_size, -1, width) for p in pieces]
        return jnp.concatenate(split, axis=1)

    second_z = chosen(second_in)
    grads_up = [weight_grad(second_z, g) for g in cut(grad_hidden, D)]
    pack_three = block_pack_of(grads_up + [weight_grad(chosen(active), grad_down)], D)
    own_up_down = reduce_dp(pack_three, dp_size).astype(f32)
    own_up = jnp.concatenate(split_pack(own_up_down, [k_d] * 4), axis=1)
    own_down = own_up_down[4 * k_d :]

    first_z = chosen(first_in)
    mixed_z = chosen(mixed)
    block_small = jnp.concatenate(
        [
            owned(
                jnp.stack(
                    [jnp.sum(grad_first * norm_one, axis=0), jnp.sum(grad_second * norm_two, axis=0)]
                ),
                2,
            ),
            owned(
                jnp.stack(
                    [
                        jnp.sum(grad_first, axis=0),
                        column_sum(grad_q),
                        column_sum(grad_v),
                        column_sum(grad_branch),
                        jnp.sum(grad_second, axis=0),
                        column_sum(grad_down),
                    ]
                ),
                6,
            ),
            owned(column_sum(grad_hidden)[None], 1),
        ],
        axis=1,
    )
    block_small = pick(block_small.reshape(dp_size, copy_size, -1), place, 1)
    block_rows = -(-block_small.shape[1] // (8 * D)) * 8
    block_small = jnp.pad(
        block_small, ((0, 0), (0, block_rows * D - block_small.shape[1]))
    ).reshape(dp_size * block_rows, D)
    pack_four = block_pack_of(
        [
            weight_grad(first_z, grad_q),
            weight_grad(first_z, grad_k),
            weight_grad(first_z, grad_v),
            weight_grad(mixed_z, grad_branch),
            block_small,
        ],
        D,
    )
    own_four = reduce_dp(pack_four, dp_size).astype(f32)
    own_q, own_k, own_v, own_proj, own_rest = split_pack(own_four, [k_d] * 4 + [block_rows])
    own_rest = own_rest.reshape(-1)
    own_gains = own_rest[: 2 * k_d].reshape(2, k_d)
    own_biases = own_rest[2 * k_d : 8 * k_d].reshape(6, k_d)
    own_up_bias = own_rest[8 * k_d : 8 * k_d + k_ff]

    mine = grad_first.reshape(micros, length, D)[:, :own].reshape(micros * own, D)
    mine_norm = norm_one.reshape(micros, length, D)[:, :own].reshape(micros * own, D)
    mine_inv = inv_one.reshape(micros, length, 1)[:, :own].reshape(micros * own, 1)
    mine_middle = grad_middle.reshape(micros, length, D)[:, :own].reshape(micros * own, D)
    input_grad = mine_middle + norm_back(mine * gains[0], mine_norm, mine_inv)
    input_grad = input_grad.reshape(micros, 1, own, D)
    block_output = condition.reshape(micros, length, D)[:, :own].reshape(micros, 1, own, D)
    return (
        block_output,
        input_grad,
        own_gains,
        own_biases,
        jnp.concatenate([own_q, own_k, own_v], axis=1),
        own_proj,
        own_up,
        own_up_bias,
        own_down,
        own_head_gain,
        own_head_biases,
        own_cond,
        own_time1,
        own_time2,
        own_w_input,
        jnp.concatenate([own_shift, own_scale, own_gate], axis=1),
        own_one,
        own_two,
        jnp.concatenate([own_fshift, own_fscale], axis=1),
        own_w_output,
        grad_out_bias,
    )


def solution(mesh):
    in_specs = (
        P(None, "dp", "copy", None),
        P(None, "dp", None),
        P(None, "dp", None, None),
        P(None, "copy", "dp", None, None),
        P(None, "copy", "dp", None),
        P(None, ("dp", "copy")),
        P(None, ("dp", "copy")),
        P(("dp", "copy"), None),
        P(("dp", "copy"), None),
        P(("dp", "copy"), None),
        P(("dp", "copy")),
        P(("dp", "copy"), None),
        P(("dp", "copy")),
        P(None, ("dp", "copy")),
        P(("dp", "copy"), None),
        P(("dp", "copy"), None),
        P(("dp", "copy"), None),
        P(None, ("dp", "copy")),
        P(("dp", "copy"), None),
        P(("dp", "copy"), None),
        P(("dp", "copy"), None),
        P(("dp", "copy"), None),
        P(("dp", "copy"), None),
        P(),
    )
    out_specs = (
        P(None, "dp", "copy", None),
        P(None, "dp", "copy", None),
        P(None, ("dp", "copy")),
        P(None, ("dp", "copy")),
        P(("dp", "copy"), None),
        P(("dp", "copy"), None),
        P(("dp", "copy"), None),
        P(("dp", "copy")),
        P(("dp", "copy"), None),
        P(("dp", "copy")),
        P(None, ("dp", "copy")),
        P(("dp", "copy"), None),
        P(("dp", "copy"), None),
        P(("dp", "copy"), None),
        P(None, ("dp", "copy")),
        P(("dp", "copy"), None),
        P(("dp", "copy"), None),
        P(("dp", "copy"), None),
        P(("dp", "copy"), None),
        P(("dp", "copy"), None),
        P(),
    )
    return jax.shard_map(shards, mesh=mesh, in_specs=in_specs, out_specs=out_specs, check_vma=False)
```

```python
import functools
import math

import jax
import jax.numpy as jnp
from jax import lax
from jax.experimental import pallas as pl
from jax.experimental.pallas import tpu as pltpu
from jax.sharding import PartitionSpec as P

D = 768
HEADS = 12
HEAD_DIM = 64
WIDTH = 1024
FREQ = 256
CHANNELS = 16
IMAGES = 4


epsilon = 1e-06
highest = lax.Precision.HIGHEST


def product(left_side, right_side):
    return jnp.dot(left_side, right_side, preferred_element_type=jnp.float32)


def weight_grad(left_side, right_side):
    return lax.dot_general(
        left_side, right_side, (((0,), (0,)), ((), ())), preferred_element_type=jnp.float32
    )


def input_back(gradient, weight):
    return lax.dot_general(
        gradient, weight, (((1,), (1,)), ((), ())), preferred_element_type=jnp.float32
    )


def column_sum(values):
    return jnp.sum(values.astype(jnp.float32), axis=0)


def normalize(values):
    center = values - jnp.mean(values, axis=-1, keepdims=True)
    inverse = lax.rsqrt(jnp.mean(center * center, axis=-1, keepdims=True) + epsilon)
    return (center * inverse, inverse)


def norm_back(gradient, normed, inverse):
    return inverse * (
        gradient
        - jnp.mean(gradient, axis=-1, keepdims=True)
        - normed * jnp.mean(gradient * normed, axis=-1, keepdims=True)
    )


def silu_slope(values):
    sigma = jax.nn.sigmoid(values)
    return sigma * (1.0 + values * (1.0 - sigma))


def gelu_slope(values):
    return 0.5 * (1.0 + lax.erf(values * 2.0 ** (-0.5))) + values * jnp.exp(
        -0.5 * values * values
    ) * (2.0 * math.pi) ** (-0.5)


def sinusoid(step_vals):
    half_width = FREQ // 2
    rates = jnp.exp(-math.log(10000.0) * jnp.arange(half_width, dtype=jnp.float32) / half_width)
    angles = step_vals[:, None] * rates[None, :]
    return jnp.concatenate([jnp.cos(angles), jnp.sin(angles)], axis=1)


def plan(step_vals):
    anchor = math.cos(0.008 / 1.008 * math.pi / 2.0) ** 2
    angle_now = ((step_vals + 1.0) / 1000.0 + 0.008) / 1.008 * (math.pi / 2.0)
    signal = jnp.cos(angle_now) ** 2 / anchor
    return jnp.stack([jnp.sqrt(signal), jnp.sqrt(1.0 - signal)], axis=1)


def tdot(left_side, right_side):
    return lax.dot_general(
        left_side, right_side, (((0,), (0,)), ((), ())), preferred_element_type=jnp.float32
    )


def swap_bit(values, size, bit):
    return lax.ppermute(values, "dp", [(i, i ^ (1 << bit)) for i in range(size)])


def shift_copy(values, size, shift):
    return lax.ppermute(values, "copy", [(i, (i + shift) % size) for i in range(size)])


def swap_copy(values, size, shift):
    return lax.ppermute(values, "copy", [(i, i ^ shift) for i in range(size)])


def pick(values, index, axis):
    return lax.dynamic_index_in_dim(values, index, axis, keepdims=False)


def tie(*values):
    return lax.optimization_barrier(values)


MIB = 1 << 20
LIGHT = pl.CostEstimate(flops=10**6, bytes_accessed=10**5, transcendentals=0)


def dot0(left_side, right_side):
    return lax.dot_general(
        left_side, right_side, (((0,), (0,)), ((), ())), preferred_element_type=jnp.float32
    )


def dot1(left_side, right_side):
    return lax.dot_general(
        left_side, right_side, (((1,), (1,)), ((), ())), preferred_element_type=jnp.float32
    )


def small_call(body, outs, scalars, ins):
    size = sum(math.prod(o.shape) * o.dtype.itemsize for o in outs)
    size += sum(math.prod(v.shape) * v.dtype.itemsize for v in ins)
    return pl.pallas_call(
        body,
        out_shape=outs,
        in_specs=[pl.BlockSpec(memory_space=pltpu.SMEM)]
        + [pl.BlockSpec(memory_space=pltpu.VMEM)] * len(ins),
        out_specs=[pl.BlockSpec(memory_space=pltpu.VMEM)] * len(outs),
        compiler_params=pltpu.CompilerParams(vmem_limit_bytes=2 * size + 16 * MIB),
        cost_estimate=LIGHT,
    )(jnp.stack([jnp.asarray(v, jnp.int32) for v in scalars]), *ins)


def low_shape(*dims):
    return jax.ShapeDtypeStruct(dims, jnp.bfloat16)


def add_up(one, two):
    return one.astype(jnp.float32) + two.astype(jnp.float32)


def cut_first(keep, got, rows, bits, kernels):
    count, mids, total, width = keep.shape
    half = count // 2

    if not kernels:
        sums = add_up(keep, got).astype(jnp.bfloat16)
        first = sums[:, :, :rows].reshape(2, half, mids, rows, width)
        second = sums[:, :, rows:].reshape(half, 2, mids, total - rows, width)
        return [
            pick(first, 1 - bits[0], 0),
            pick(first, bits[0], 0),
            pick(second, 1 - bits[1], 1),
            pick(second, bits[1], 1),
        ]

    def body(at, keep_ref, got_ref, *outs):
        for out, bit, top in zip(outs, (1 - at[0], at[0], 1 - at[1], at[1]), (0, 0, 1, 1)):
            cut = pl.ds(rows, total - rows) if top else pl.ds(0, rows)
            for i in range(half):
                p = 2 * i + bit if top else bit * half + i
                out[i] = add_up(keep_ref[p, :, cut], got_ref[p, :, cut]).astype(jnp.bfloat16)

    outs = [low_shape(half, mids, n, width) for n in (rows, rows, total - rows, total - rows)]
    return small_call(body, outs, bits, [keep, got])


def cut_next(keeps, gots, bits, kernels):
    count, mids, _, width = keeps[0].shape
    half = count // 2
    sizes = [k.shape[2] for k in keeps]
    if not kernels:
        sums = [add_up(k, g).astype(jnp.bfloat16) for k, g in zip(keeps, gots)]
        first = sums[0].reshape(2, half, mids, sizes[0], width)
        second = sums[1].reshape(half, 2, mids, sizes[1], width)
        return [
            pick(first, 1 - bits[0], 0),
            pick(first, bits[0], 0),
            pick(second, 1 - bits[1], 1),
            pick(second, bits[1], 1),
        ]

    def body(at, keep_one, got_one, keep_two, got_two, *outs):
        for out, bit, top in zip(outs, (1 - at[0], at[0], 1 - at[1], at[1]), (0, 0, 1, 1)):
            keep, got = (keep_two, got_two) if top else (keep_one, got_one)
            for i in range(half):
                p = 2 * i + bit if top else bit * half + i
                out[i] = add_up(keep[p], got[p]).astype(jnp.bfloat16)

    outs = [low_shape(half, mids, n, width) for n in (sizes[0], sizes[0], sizes[1], sizes[1])]
    return small_call(body, outs, bits, [keeps[0], gots[0], keeps[1], gots[1]])


def cut_copies(keeps, gots, place, copy_size, kernels):
    _, mids, _, width = keeps[0].shape
    sizes = [k.shape[2] for k in keeps]
    total = sum(sizes)
    if not kernels:
        sums = jnp.concatenate([add_up(k, g)[0] for k, g in zip(keeps, gots)], axis=1)
        sums = sums.astype(jnp.bfloat16).reshape(2, copy_size, total, width)
        return [pick(sums, lax.rem(place + j, copy_size), 1) for j in range(copy_size)]

    def body(at, keep_one, got_one, keep_two, got_two, *outs):
        for j in range(copy_size):
            z = lax.rem(at[0] + j, copy_size)
            for c in range(2):
                m = c * copy_size + z
                top = add_up(keep_one[0, m], got_one[0, m]).astype(jnp.bfloat16)
                low = add_up(keep_two[0, m], got_two[0, m]).astype(jnp.bfloat16)
                outs[j][c, : sizes[0]] = top
                outs[j][c, sizes[0] :] = low

    outs = [low_shape(2, total, width)] * copy_size
    return small_call(body, outs, [place], [keeps[0], gots[0], keeps[1], gots[1]])


def own_and_other(parts, scalars, kernels):
    place, core = scalars
    count = len(parts)
    _, total, width = parts[0].shape
    if not kernels:
        stacked = jnp.stack(parts).astype(jnp.float32)
        sums = 0.0
        for i in range(count):
            sums = sums + pick(stacked, lax.rem(place + count - i, count), 0)
        sums = sums.astype(jnp.bfloat16)
        return [pick(sums, 1 - core, 0), pick(sums, core, 0)]

    def body(at, *refs):
        for out, c in zip(refs[count:], (1 - at[1], at[1])):
            values = [r[c].astype(jnp.float32) for r in refs[:count]]
            sums = None
            for i in range(count):
                turn = lax.rem(at[0] + count - i, count)
                value = values[0]
                for j in range(1, count):
                    value = jnp.where(turn == j, values[j], value)
                sums = value if sums is None else sums + value
            out[...] = sums.astype(jnp.bfloat16)

    return small_call(body, [low_shape(total, width)] * 2, scalars, parts)


class Reduction:
    def __init__(self, send, keep, rows, size, kernels):
        self.size, self.rows, self.kernels = size, rows, kernels
        self.left = size.bit_length() - 2
        self.me = lax.axis_index("dp")
        self.sent, self.kept, self.bits = [send], [keep], [0]

    def receive(self):
        self.got = [swap_bit(v, self.size, bit) for v, bit in zip(self.sent, self.bits)]
        return self

    def advance(self):
        if len(self.sent) == 1:
            self.bits = [self.left, 1]
            bits = [(self.me >> b) & 1 for b in self.bits]
            cuts = cut_first(self.kept[0], self.got[0], self.rows, bits, self.kernels)
        else:
            self.bits = [self.bits[0] - 1, self.bits[1] + 1]
            bits = [(self.me >> b) & 1 for b in self.bits]
            cuts = cut_next(self.kept, self.got, bits, self.kernels)
        self.left -= 1
        self.sent, self.kept = [cuts[0], cuts[2]], [cuts[1], cuts[3]]
        return self


def attend(ids_col, ids_row, q, k, lanes, head, scale):
    wanted = (lanes >= HEAD_DIM) if head else (lanes < HEAD_DIM)
    scores = dot1(jnp.where(wanted, q, 0), k) * scale
    scores = jnp.where(ids_col == ids_row, scores, -1e30)
    exps = jnp.exp(scores - jnp.max(scores, axis=-1, keepdims=True))
    return wanted, exps / jnp.sum(exps, axis=-1, keepdims=True)


def attention_specs(micros, length):
    wide = pl.BlockSpec((length, 2 * HEAD_DIM), lambda m, h: (m, h))
    col = pl.BlockSpec((length, 1), lambda m, h: (m, 0))
    row = pl.BlockSpec((1, 1, length), lambda m, h: (m, 0, 0))
    return wide, col, row


def attention(queries, key_rows, value_rows, ids):
    micros, length = ids.shape
    scale = HEAD_DIM ** (-0.5)
    wide, col, row = attention_specs(micros, length)

    def body(col_ref, row_ref, q_ref, k_ref, v_ref, out_ref):
        lanes = lax.broadcasted_iota(jnp.int32, (1, 2 * HEAD_DIM), 1)
        outs = []
        for head in range(2):
            _, probs = attend(
                col_ref[...], row_ref[0], q_ref[...], k_ref[...], lanes, head, scale
            )
            outs.append(
                jnp.dot(
                    probs.astype(jnp.bfloat16), v_ref[...], preferred_element_type=jnp.float32
                )
            )
        out_ref[...] = jnp.where(lanes < HEAD_DIM, outs[0], outs[1]).astype(jnp.bfloat16)

    return pl.pallas_call(
        body,
        grid=(micros, HEADS // 2),
        out_shape=low_shape(micros * length, D),
        in_specs=[col, row, wide, wide, wide],
        out_specs=wide,
        compiler_params=pltpu.CompilerParams(vmem_limit_bytes=24 * MIB),
        cost_estimate=LIGHT,
    )(ids.reshape(-1, 1), ids[:, None], queries, key_rows, value_rows)


def attention_back(queries, key_rows, value_rows, grad_mixed, ids):
    micros, length = ids.shape
    scale = HEAD_DIM ** (-0.5)
    wide, col, row = attention_specs(micros, length)

    def body(col_ref, row_ref, q_ref, k_ref, v_ref, g_ref, gq_ref, gk_ref, gv_ref):
        lanes = lax.broadcasted_iota(jnp.int32, (1, 2 * HEAD_DIM), 1)
        q, k, v, g = q_ref[...], k_ref[...], v_ref[...], g_ref[...]
        parts = []
        for head in range(2):
            wanted, probs = attend(col_ref[...], row_ref[0], q, k, lanes, head, scale)
            grad_probs = dot1(jnp.where(wanted, g, 0), v)
            delta = jnp.sum(grad_probs * probs, axis=-1, keepdims=True)
            grad_scores = (probs * (grad_probs - delta)).astype(jnp.bfloat16)
            parts.append(
                (
                    jnp.dot(grad_scores, k, preferred_element_type=jnp.float32) * scale,
                    dot0(grad_scores, q) * scale,
                    dot0(probs.astype(jnp.bfloat16), g),
                )
            )
        for out, one, two in zip((gq_ref, gk_ref, gv_ref), *parts):
            out[...] = jnp.where(lanes < HEAD_DIM, one, two).astype(jnp.bfloat16)

    return pl.pallas_call(
        body,
        grid=(micros, HEADS // 2),
        out_shape=[low_shape(micros * length, D)] * 3,
        in_specs=[col, row, wide, wide, wide, wide],
        out_specs=[wide] * 3,
        compiler_params=pltpu.CompilerParams(vmem_limit_bytes=32 * MIB),
        cost_estimate=LIGHT,
    )(ids.reshape(-1, 1), ids[:, None], queries, key_rows, value_rows, grad_mixed)


def pack_head_grads(pairs, core, dp_size, copy_size, kernels):
    world = dp_size * copy_size
    count, mids = dp_size // 2, 2 * copy_size
    width = pairs[0][1].shape[1]
    half = width // 2
    sizes = [p[0].shape[1] // world for p in pairs]
    total = sum(sizes)
    if not kernels:
        packs = []
        for c in (1 - core, core):
            parts = []
            for left_side, right_side in pairs:
                part = lax.dynamic_slice_in_dim(right_side, c * half, half, 1)
                part = weight_grad(left_side, part).astype(jnp.bfloat16)
                parts.append(part.reshape(count, mids, -1, half))
            packs.append(jnp.concatenate(parts, axis=2))
        return packs + [jnp.stack([column_sum(p[1]) for p in pairs])]

    lefts, which = [], []
    for left_side, _ in pairs:
        seen = [i for i, other in enumerate(lefts) if other is left_side]
        which.append(seen[0] if seen else len(lefts))
        lefts += [] if seen else [left_side]
    rights = [p[1] for p in pairs]
    narrow = [v.shape[1] // count % 128 == 0 for v in lefts]
    held = [i for i, w in enumerate(which) if not narrow[w]]

    def body(at, *refs):
        left_refs = refs[: len(lefts)]
        right_refs = refs[len(lefts) : len(lefts) + len(rights)]
        sent, kept, sums = refs[len(lefts) + len(rights) :][:3]
        scratch = refs[len(lefts) + len(rights) + 3 :]
        first = at[0] == 0
        step = pl.program_id(0)

        @pl.when(step == 0)
        def _():
            for i, right in enumerate(right_refs):
                ones = jnp.ones((8, right.shape[0]), jnp.bfloat16)
                row = jnp.dot(ones, right[...], preferred_element_type=jnp.float32)
                sums[i : i + 1] = row[:1]
            for i, buffer in zip(held, scratch):
                buffer[...] = dot0(left_refs[which[i]][...], right_refs[i][...])

        at_row = 0
        for i, n in enumerate(sizes):
            if i in held:
                rows = mids * n
                whole = scratch[held.index(i)][pl.ds(pl.multiple_of(step * rows, 8), rows)]
            else:
                whole = dot0(left_refs[which[i]][...], right_refs[i][...])
            left, right = whole[:, :half], whole[:, half:]
            for out, part in (
                (sent, jnp.where(first, right, left)),
                (kept, jnp.where(first, left, right)),
            ):
                out[0, :, at_row : at_row + n] = part.reshape(mids, n, half).astype(jnp.bfloat16)
            at_row += n

    in_specs = [pl.BlockSpec(memory_space=pltpu.SMEM)]
    for v, cut_up in zip(lefts, narrow):
        if cut_up:
            in_specs.append(pl.BlockSpec((v.shape[0], v.shape[1] // count), lambda p: (0, p)))
        else:
            in_specs.append(pl.BlockSpec(v.shape, lambda p: (0, 0)))
    in_specs += [pl.BlockSpec(v.shape, lambda p: (0, 0)) for v in rights]
    out_spec = pl.BlockSpec((1, mids, total, half), lambda p: (p, 0, 0, 0))
    return pl.pallas_call(
        body,
        grid=(count,),
        out_shape=[low_shape(count, mids, total, half)] * 2
        + [jax.ShapeDtypeStruct((len(pairs), width), jnp.float32)],
        in_specs=in_specs,
        out_specs=[out_spec] * 2 + [pl.BlockSpec((len(pairs), width), lambda p: (0, 0))],
        scratch_shapes=[
            pltpu.VMEM((lefts[which[i]].shape[1], width), jnp.float32) for i in held
        ],
        compiler_params=pltpu.CompilerParams(vmem_limit_bytes=44 * MIB),
        cost_estimate=LIGHT,
    )(jnp.asarray(core, jnp.int32)[None], *lefts, *rights)


def assemble(pieces, scalars, copy_size, rows):
    width = pieces[0][0].shape[-1]
    total = rows

    def body(at, *refs):
        ins, out, sems = refs[: len(pieces)], refs[len(pieces)], refs[len(pieces) + 1]
        copies = []
        for ref, (value, first, flip, vary) in zip(ins, pieces):
            for d in range(2):
                for j in range(copy_size):
                    dp = at[0] ^ (flip | (vary if d else 0))
                    owner = dp * copy_size + lax.rem(at[1] + j, copy_size)
                    copy = pltpu.make_async_copy(
                        ref.at[d, j],
                        out.at[owner, pl.ds(first, value.shape[2])],
                        sems.at[len(copies)],
                    )
                    copy.start()
                    copies.append(copy)
        for copy in copies:
            copy.wait()

    return pl.pallas_call(
        body,
        out_shape=low_shape(8 * copy_size, total, width),
        in_specs=[pl.BlockSpec(memory_space=pltpu.SMEM)]
        + [pl.BlockSpec(memory_space=pl.ANY)] * len(pieces),
        out_specs=pl.BlockSpec(memory_space=pl.ANY),
        scratch_shapes=[pltpu.SemaphoreType.DMA((len(pieces) * 2 * copy_size,))],
        compiler_params=pltpu.CompilerParams(vmem_limit_bytes=4 * MIB),
        cost_estimate=LIGHT,
    )(jnp.stack([jnp.asarray(v, jnp.int32) for v in scalars]), *[p[0] for p in pieces])


def gather(pack, rows, arrived):
    total = pack.shape[0]
    along = [pack, *arrived]
    pieces = []
    for first, last, bits in ((0, rows, (2, 1)), (rows, total, (1, 2))):
        held = jnp.stack([v[first:last] for v in along])
        held = jnp.stack([held, swap_bit(held, 8, bits[0])])
        got = swap_bit(held, 8, bits[1])
        vary = 1 << bits[0]
        other = 1 << bits[1]
        pieces += [(held, first, 0, vary), (got, first, other, vary)]
        pieces += [
            (swap_bit(held, 8, 0), first, 1, vary),
            (swap_bit(got, 8, 0), first, other | 1, vary),
        ]
    return assemble(pieces, (lax.axis_index("dp"), lax.axis_index("copy")), 4, total)


def spread(packed, count, k):
    world = packed.shape[0]
    width = world * k
    padded = -(-count // 8) * 8
    lanes = -(-count * k // 128) * 128
    if 128 % k or packed.shape[1] < lanes:
        values = packed[:, : count * k].reshape(world, count, k)
        return jnp.moveaxis(values, 0, 1).reshape(count, width).astype(jnp.float32)
    group = 128 // k

    def body(packed_ref, out_ref):
        column = lax.broadcasted_iota(jnp.int32, (128, width), 1)
        row = lax.broadcasted_iota(jnp.int32, (128, width), 0)
        owner = lax.broadcasted_iota(jnp.int32, (world, width), 0)
        own = owner == lax.broadcasted_iota(jnp.int32, (world, width), 1) // k
        for j in range(group):
            tile = (row == j * k + column % k).astype(jnp.bfloat16)
            for i in range(j, count, group):
                block = packed_ref[:, i // group * 128 : (i // group + 1) * 128]
                values = jnp.dot(block, tile, preferred_element_type=jnp.float32)
                out_ref[i : i + 1] = jnp.sum(jnp.where(own, values, 0.0), axis=0, keepdims=True)

    return pl.pallas_call(
        body,
        out_shape=jax.ShapeDtypeStruct((padded, width), jnp.float32),
        in_specs=[pl.BlockSpec(memory_space=pltpu.VMEM)],
        out_specs=pl.BlockSpec(memory_space=pltpu.VMEM),
        compiler_params=pltpu.CompilerParams(vmem_limit_bytes=16 * MIB),
        cost_estimate=LIGHT,
    )(packed[:, :lanes])[:count]


def entry_back(grad_affine, grad_residual, norm_head, inv_head, gain, noisy):
    rows, width = grad_affine.shape
    step = 256

    def body(ga_ref, gr_ref, norm_ref, inv_ref, gain_ref, noisy_ref, out_ref):
        grad, norm = ga_ref[...], norm_ref[...]
        back = norm_back(grad * gain_ref[...], norm, inv_ref[...])
        entry = (gr_ref[...] + back).astype(jnp.bfloat16)
        part = jnp.concatenate(
            [
                dot0(noisy_ref[...], entry),
                jnp.sum(grad * norm, axis=0, keepdims=True),
                jnp.sum(entry.astype(jnp.float32), axis=0, keepdims=True),
                jnp.sum(grad, axis=0, keepdims=True),
                jnp.zeros((5, width), jnp.float32),
            ],
            axis=0,
        )

        @pl.when(pl.program_id(0) == 0)
        def _():
            out_ref[...] = part

        @pl.when(pl.program_id(0) > 0)
        def _():
            out_ref[...] += part

    tall = pl.BlockSpec((step, width), lambda i: (i, 0))
    return pl.pallas_call(
        body,
        grid=(rows // step,),
        out_shape=jax.ShapeDtypeStruct((CHANNELS + 8, width), jnp.float32),
        in_specs=[
            tall,
            tall,
            tall,
            pl.BlockSpec((step, 1), lambda i: (i, 0)),
            pl.BlockSpec((1, width), lambda i: (0, 0)),
            pl.BlockSpec((step, CHANNELS), lambda i: (i, 0)),
        ],
        out_specs=pl.BlockSpec((CHANNELS + 8, width), lambda i: (0, 0)),
        compiler_params=pltpu.CompilerParams(vmem_limit_bytes=32 * MIB),
        cost_estimate=LIGHT,
    )(grad_affine, grad_residual, norm_head, inv_head, gain[None], noisy)


def feed_back(gradient, slope, w_up_full, w_down_full):
    rows, ff = slope.shape
    step = 512

    def body(g_ref, slope_ref, up_ref, down_ref, out_ref, sums_ref, second_ref):
        grad_hidden = dot1(g_ref[...], down_ref[...]) * slope_ref[...].astype(jnp.float32)
        grad_hidden = grad_hidden.astype(jnp.bfloat16)
        out_ref[...] = grad_hidden
        ones = jnp.ones((8, rows), jnp.bfloat16)
        sums_ref[...] = jnp.dot(ones, grad_hidden, preferred_element_type=jnp.float32)
        part = dot1(grad_hidden, up_ref[...])

        @pl.when(pl.program_id(0) == 0)
        def _():
            second_ref[...] = part

        @pl.when(pl.program_id(0) > 0)
        def _():
            second_ref[...] += part

    full = pl.BlockSpec((rows, D), lambda j: (0, 0))
    across = pl.BlockSpec((rows, step), lambda j: (0, j))
    grad_hidden, sums, second = pl.pallas_call(
        body,
        grid=(ff // step,),
        out_shape=[
            low_shape(rows, ff),
            jax.ShapeDtypeStruct((8, ff), jnp.float32),
            jax.ShapeDtypeStruct((rows, D), jnp.float32),
        ],
        in_specs=[
            full,
            across,
            pl.BlockSpec((D, step), lambda j: (0, j)),
            pl.BlockSpec((step, D), lambda j: (j, 0)),
        ],
        out_specs=[across, pl.BlockSpec((8, step), lambda j: (0, j)), full],
        compiler_params=pltpu.CompilerParams(vmem_limit_bytes=32 * MIB),
        cost_estimate=LIGHT,
    )(gradient, slope, w_up_full, w_down_full)
    return grad_hidden, sums[0], second


def pack_block_grads(pairs, ready, core, dp_size, kernels):
    count = dp_size // 2
    half = D // 2
    pieces = [(i, j) for i, p in enumerate(pairs) for j in range(p[1].shape[1] // D)]
    sizes = [pairs[i][0].shape[1] // dp_size for i, _ in pieces]
    sizes += [r.shape[0] // dp_size for r in ready]
    total = sum(sizes)

    if not kernels:
        packs = []
        for c in (1 - core, core):
            parts = []
            for i, j in pieces:
                part = lax.dynamic_slice_in_dim(pairs[i][1], j * D + c * half, half, 1)
                parts.append(weight_grad(pairs[i][0], part))
            for gradient in ready:
                parts.append(lax.dynamic_slice_in_dim(gradient, c * half, half, 1))
            parts = [p.astype(jnp.bfloat16).reshape(count, 2, -1, half) for p in parts]
            packs.append(jnp.concatenate(parts, axis=2))
        return packs

    def body(at, *refs):
        sent, kept = refs[-2:]
        first = at[0] == 0
        at_row = 0
        for piece, n in enumerate(sizes):
            if piece < len(pieces):
                i, j = pieces[piece]
                whole = dot0(refs[2 * i][...], refs[2 * i + 1][:, j * D : (j + 1) * D])
            else:
                whole = refs[2 * len(pairs) + piece - len(pieces)][...].astype(jnp.float32)
            left, right = whole[:, :half], whole[:, half:]
            for out, part in (
                (sent, jnp.where(first, right, left)),
                (kept, jnp.where(first, left, right)),
            ):
                part = part.reshape(count, 2, n, half).astype(jnp.bfloat16)
                out[:, :, at_row : at_row + n] = part
            at_row += n

    flat = [v for p in pairs for v in p] + list(ready)
    return small_call(body, [low_shape(count, 2, total, half)] * 2, [core], flat)


def shards(
    block_input,
    image_ids,
    latents,
    noise,
    timesteps,
    norm_gains,
    block_biases,
    w_qkv,
    w_proj,
    w_up,
    up_bias,
    w_down,
    head_gain,
    head_biases,
    w_cond,
    w_time1,
    w_time2,
    w_input,
    w_ada,
    w_mlp1,
    w_mlp2,
    w_final,
    w_output,
    output_bias,
):
    bf16, f32 = jnp.bfloat16, jnp.float32
    dp_size, copy_size = lax.axis_size("dp"), lax.axis_size("copy")
    world = dp_size * copy_size
    place = lax.axis_index("copy")
    micros, _, own, _ = block_input.shape
    length = image_ids.shape[2]
    total = micros * length
    k_d, k_ff, k_w, k_t = D // world, w_down.shape[0], WIDTH // world, w_time1.shape[0]
    ff = k_ff * world
    kernels = k_d % 8 == 0 and k_w % 16 == 0 and k_t % 8 == 0
    score_scale = HEAD_DIM ** (-0.5)

    def cut(matrix, width):
        return [matrix[:, i : i + width] for i in range(0, matrix.shape[1], width)]

    def pad_flat(parts, width):
        flat = jnp.concatenate([p.reshape(-1) for p in parts])
        count = -(-flat.shape[0] // (16 * width)) * 16 * width
        return jnp.pad(flat, (0, count - flat.shape[0])).reshape(-1, width)

    groups = [
        (cut(w_qkv, D) + [w_proj, pad_flat([norm_gains, block_biases, up_bias], D)], 2),
        (cut(w_up, D) + [w_down], 4),
        (
            cut(w_ada, WIDTH)
            + [w_time2, w_cond, w_time1]
            + [pad_flat([w_input, w_output.T, head_gain, head_biases], WIDTH)],
            3,
        ),
        ([w_mlp1, w_mlp2] + cut(w_final, WIDTH), 2),
    ]

    def everyone(pack):
        return [shift_copy(pack, copy_size, copy_size - j) for j in range(1, copy_size)]

    def unpack(pack, parts):
        out, at = [], 0
        for part in parts:
            out.append(pack[:, at : at + part.shape[0]].reshape(-1, pack.shape[2]))
            at += part.shape[0]
        return out

    own_rows = block_input[:, 0]
    packs = [jnp.concatenate(parts, 0) for parts, _ in groups]
    if kernels and dp_size == 8 and copy_size == 4:
        head_own = jnp.concatenate(packs[2:])
        arrived = [everyone(packs[0])]
        *arrived[0], packs[1] = tie(*arrived[0], packs[1])
        arrived.append(everyone(packs[1]))
        *arrived[1], own_rows, head_own = tie(*arrived[1], own_rows, head_own)
        rows_arrived = everyone(own_rows)
        full = [
            gather(pack, sum(p.shape[0] for p in parts[:n]), got)
            for pack, (parts, n), got in zip(packs[:2], groups[:2], arrived[:2])
        ]
        head = lax.all_gather(head_own, ("dp", "copy"), axis=0)
        full += [head[:, : packs[2].shape[0]], head[:, packs[2].shape[0] :]]
    else:
        rows_arrived = everyone(own_rows)
        full = [lax.all_gather(pack, ("dp", "copy"), axis=0) for pack in packs]
    full = [unpack(pack, parts) for pack, (parts, _) in zip(full, groups)]

    rows = jnp.stack([own_rows, *rows_arrived], axis=1).reshape(total, D).astype(f32)

    def turned(values):
        twice = jnp.concatenate([values, values], axis=1)
        return lax.dynamic_slice_in_dim(twice, place * own, length, 1)

    ids = turned(image_ids[:, 0])
    latent_rows = turned(latents[:, 0]).reshape(total, CHANNELS)
    noise_rows = turned(noise[:, 0, 0]).reshape(total, CHANNELS)

    w_q, w_k, w_v, w_proj_full, small = full[0]
    w_up_full = jnp.concatenate(full[1][:4], axis=1)
    w_down_full = full[1][4]
    small = small.reshape(world, -1)
    up_bias_full = small[:, 8 * k_d : 8 * k_d + k_ff].reshape(ff).astype(f32)
    gains = small[:, : 2 * k_d].reshape(world, 2, k_d)
    gains = jnp.moveaxis(gains, 0, 1).reshape(2, D).astype(f32)
    biases = small[:, 2 * k_d : 8 * k_d].reshape(world, 6, k_d)
    biases = jnp.moveaxis(biases, 0, 1).reshape(6, D).astype(f32)

    norm_one, inv_one = normalize(rows)
    first_in = (norm_one * gains[0] + biases[0]).astype(bf16)
    queries = (product(first_in, w_q) + biases[1]).astype(bf16)
    key_rows = product(first_in, w_k).astype(bf16)
    value_rows = (product(first_in, w_v) + biases[2]).astype(bf16)
    mixed = attention(queries, key_rows, value_rows, ids)
    middle = rows + product(mixed, w_proj_full) + biases[3]
    norm_two, inv_two = normalize(middle)
    second_in = (norm_two * gains[1] + biases[4]).astype(bf16)
    hidden = product(second_in, w_up_full) + up_bias_full
    active = jax.nn.gelu(hidden, approximate=False).astype(bf16)
    slope = gelu_slope(hidden).astype(bf16)
    output = middle + product(active, w_down_full) + biases[5]
    condition = output.astype(bf16)

    def chosen(values):
        width = values.shape[1]
        k = width // world
        source = jnp.arange(width, dtype=jnp.int32)[:, None]
        target = jnp.arange(dp_size * k, dtype=jnp.int32)[None, :]
        wanted = (target // k * copy_size + place) * k + target % k
        return product(values, (source == wanted).astype(bf16)).astype(bf16)

    condition, first_z, mixed_z, second_z, active_z, slope = tie(
        condition, chosen(first_in), chosen(mixed), chosen(second_in), chosen(active), slope
    )
    core = lax.axis_index("dp") & 1

    def split_pack(pack, parts):
        out, at = [], 0
        for rows_of in parts:
            out.append(pack[at : at + rows_of])
            at += rows_of
        return out

    def advance(reduction, others):
        tied = tie(*reduction.got, *others)
        reduction.got = list(tied[: len(reduction.got)])
        others = tied[len(reduction.got) :]
        reduction.advance()
        count = len(reduction.sent)
        tied = tie(*reduction.sent, *reduction.kept, *others)
        reduction.sent = list(tied[:count])
        reduction.kept = list(tied[count : 2 * count])
        reduction.receive()
        return tied[2 * count :]

    def to_copies(reduction, others):
        tied = tie(*reduction.got, *others)
        reduction.got = list(tied[: len(reduction.got)])
        others = tied[len(reduction.got) :]
        chunks = cut_copies(reduction.kept, reduction.got, place, copy_size, kernels)
        tied = tie(*chunks, *others)
        chunks = list(tied[:copy_size])
        arriving = [shift_copy(chunks[j], copy_size, j) for j in range(1, copy_size)]
        return [chunks[0], *arriving], tied[copy_size:]

    def whole(other, mine):
        got = swap_bit(other, dp_size, 0)
        left = jnp.where(core == 0, mine, got)
        right = jnp.where(core == 0, got, mine)
        return jnp.concatenate([left, right], axis=1).astype(f32)

    def landed(parts):
        return whole(*own_and_other(parts, (place, core), kernels))

    def finish(reduction):
        while reduction.left:
            reduction.advance().receive()
        parts = [
            jnp.concatenate([v[0] for v in values], axis=1)
            for values in (reduction.kept, reduction.got)
        ]
        return whole(*own_and_other(parts, (0, core), kernels))

    w_shift, w_scale, w_gate, w_time2_full, w_cond_full, w_time1_full, small = full[2]
    w_one, w_two, w_fshift, w_fscale = full[3]
    small = small.reshape(world, -1)
    small = spread(small, 2 * CHANNELS + 13, k_w)
    w_input_full = small[:CHANNELS].astype(bf16)
    w_output_t = small[CHANNELS : 2 * CHANNELS].astype(bf16)
    head_gain_f = small[2 * CHANNELS]
    head_bias = small[2 * CHANNELS + 1 :]

    valid_rows = (ids >= 0).astype(f32).reshape(total, 1)
    slots = jnp.arange(micros * IMAGES, dtype=jnp.int32)
    row_slot = ids + IMAGES * jnp.arange(micros, dtype=jnp.int32)[:, None]
    row_slot = jnp.where(ids >= 0, row_slot, -1).reshape(total, 1)
    image_onehot = (row_slot == slots[None, :]).astype(f32)
    step_vals = timesteps[:, 0, 0].reshape(micros * IMAGES).astype(f32)
    sinusoid_in = sinusoid(step_vals).astype(bf16)
    time_one = product(sinusoid_in, w_time1_full) + head_bias[1]
    time_act = jax.nn.silu(time_one).astype(bf16)
    embedded = product(time_act, w_time2_full) + head_bias[2]
    cond_all = (
        product(condition, w_cond_full)
        + head_bias[0]
        + jnp.dot(image_onehot, embedded, precision=highest, preferred_element_type=f32)
    )
    gated = jax.nn.silu(cond_all).astype(bf16)
    shift_rows = product(gated, w_shift) + head_bias[7]
    scale_rows = product(gated, w_scale) + head_bias[8]
    gate_rows = product(gated, w_gate) + head_bias[9]
    mixing = jnp.dot(image_onehot, plan(step_vals), precision=highest, preferred_element_type=f32)
    noisy = (latent_rows * mixing[:, 0:1] + noise_rows * mixing[:, 1:2]).astype(bf16)
    entry_rows = product(noisy, w_input_full) + head_bias[3]
    norm_head, inv_head = normalize(entry_rows)
    affine = norm_head * head_gain_f + head_bias[4]
    mlp_in = (affine * (1.0 + scale_rows) + shift_rows).astype(bf16)
    inner_one = product(mlp_in, w_one) + head_bias[5]
    inner_act = jax.nn.silu(inner_one).astype(bf16)
    inner_two = product(inner_act, w_two) + head_bias[6]
    residual = entry_rows + gate_rows * inner_two
    fshift_rows = product(gated, w_fshift) + head_bias[10]
    fscale_rows = product(gated, w_fscale) + head_bias[11]
    norm_final, inv_final = normalize(residual)
    final_in = (norm_final * (1.0 + fscale_rows) + fshift_rows).astype(bf16)
    predicted = input_back(final_in, w_output_t) + output_bias.astype(f32)

    grad_pred = ((predicted - noise_rows) * valid_rows).astype(bf16)
    grad_out_bias = column_sum(grad_pred)
    grad_w_output = weight_grad(grad_pred, final_in)
    grad_final_in = product(grad_pred, w_output_t)
    grad_fshift = grad_final_in.astype(bf16)
    grad_fscale = (grad_final_in * norm_final).astype(bf16)
    grad_residual = norm_back(grad_final_in * (1.0 + fscale_rows), norm_final, inv_final)
    grad_gated = input_back(grad_fshift, w_fshift) + input_back(grad_fscale, w_fscale)
    grad_inner_two = (grad_residual * gate_rows).astype(bf16)
    grad_inner_one = (input_back(grad_inner_two, w_two) * silu_slope(inner_one)).astype(bf16)
    send, keep, sums_one = pack_head_grads(
        [
            (gated, grad_fshift),
            (gated, grad_fscale),
            (inner_act, grad_inner_two),
            (mlp_in, grad_inner_one),
        ],
        core,
        dp_size,
        copy_size,
        kernels,
    )
    grad_inner_one, send, keep = tie(grad_inner_one, send, keep)
    pack_one = Reduction(send, keep, 2 * k_w, dp_size, kernels).receive()
    grad_mlp_in = input_back(grad_inner_one, w_one)
    (grad_mlp_in,) = advance(pack_one, [grad_mlp_in])
    grad_shift = grad_mlp_in.astype(bf16)
    grad_scale = (grad_mlp_in * affine).astype(bf16)
    grad_gate = (grad_residual * inner_two).astype(bf16)
    grad_affine = grad_mlp_in * (1.0 + scale_rows)
    grad_gated = (
        grad_gated
        + input_back(grad_shift, w_shift)
        + input_back(grad_scale, w_scale)
        + input_back(grad_gate, w_gate)
    )
    grad_cond = grad_gated * silu_slope(cond_all)
    grad_cond_low = grad_cond.astype(bf16)
    grad_condition = input_back(grad_cond_low, w_cond_full).astype(bf16)

    chunks = grad_condition.reshape(micros, copy_size, own, D)
    chunks = [chunks[:, j] for j in range(copy_size)]
    tied = advance(pack_one, [*chunks, grad_affine, grad_cond, grad_cond_low])
    chunks = tied[:copy_size]
    grad_affine, grad_cond, grad_cond_low = tied[copy_size:]
    arriving = [shift_copy(chunks[j], copy_size, j) for j in range(1, copy_size)]
    grad_embedded = lax.dot_general(
        image_onehot,
        grad_cond,
        (((0,), (0,)), ((), ())),
        precision=highest,
        preferred_element_type=f32,
    ).astype(bf16)
    grad_time_one = (input_back(grad_embedded, w_time2_full) * silu_slope(time_one)).astype(bf16)
    send, keep, sums_two = pack_head_grads(
        [
            (gated, grad_shift),
            (gated, grad_scale),
            (gated, grad_gate),
            (time_act, grad_embedded),
            (condition, grad_cond_low),
            (sinusoid_in, grad_time_one),
        ],
        core,
        dp_size,
        copy_size,
        kernels,
    )
    send, keep, *arriving = tie(send, keep, *arriving)
    pack_two = Reduction(send, keep, 3 * k_w, dp_size, kernels).receive()
    grad_z_own = chunks[0].astype(f32)
    for part in arriving:
        grad_z_own = grad_z_own + part.astype(f32)
    grad_z_own = grad_z_own.astype(bf16)
    (grad_z_own,) = advance(pack_two, [grad_z_own])
    arriving = [shift_copy(grad_z_own, copy_size, copy_size - j) for j in range(1, copy_size)]
    grad_affine, grad_z_own = tie(grad_affine, grad_z_own)
    if kernels:
        from_entry = entry_back(
            grad_affine, grad_residual, norm_head, inv_head, head_gain_f, noisy
        )
    else:
        grad_entry = grad_residual + norm_back(grad_affine * head_gain_f, norm_head, inv_head)
        grad_entry = grad_entry.astype(bf16)
        from_entry = jnp.concatenate(
            [
                weight_grad(noisy, grad_entry),
                jnp.sum(grad_affine * norm_head, axis=0)[None],
                column_sum(grad_entry)[None],
                jnp.sum(grad_affine, axis=0)[None],
            ]
        )
    from_entry, *arriving = tie(from_entry, *arriving)
    one_parts, (grad_z_own, *arriving) = to_copies(pack_one, [grad_z_own, *arriving])

    grad_z = jnp.stack([grad_z_own, *arriving], axis=1).reshape(total, D)
    grad_down = grad_z
    if kernels:
        grad_hidden, sums_hidden, grad_second = feed_back(grad_down, slope, w_up_full, w_down_full)
    else:
        grad_hidden = input_back(grad_down, w_down_full) * slope.astype(f32)
        grad_hidden = grad_hidden.astype(bf16)
        sums_hidden = column_sum(grad_hidden)
        grad_second = input_back(grad_hidden, w_up_full)
    grad_middle = grad_z.astype(f32) + norm_back(grad_second * gains[1], norm_two, inv_two)
    grad_branch = grad_middle.astype(bf16)
    grad_mixed = input_back(grad_branch, w_proj_full).astype(bf16)
    send, keep = pack_block_grads(
        [(second_z, grad_hidden), (active_z, grad_down)], [], core, dp_size, kernels
    )
    pack_three = Reduction(send, keep, 4 * k_d, dp_size, kernels)
    grad_mixed, pack_three.sent[0], pack_three.kept[0] = tie(grad_mixed, send, keep)
    pack_three.receive()
    (grad_mixed,) = advance(pack_two, [grad_mixed])
    small_grads = jnp.concatenate(
        [
            from_entry[:CHANNELS],
            grad_w_output,
            from_entry[CHANNELS : CHANNELS + 1],
            sums_two[4:6],
            sums_two[3:4],
            from_entry[CHANNELS + 1 : CHANNELS + 3],
            sums_one[3:4],
            sums_one[2:3],
            sums_two[:3],
            sums_one[:2],
            jnp.pad(grad_out_bias, (0, WIDTH - CHANNELS))[None],
            jnp.zeros((2, WIDTH), f32),
        ],
        axis=0,
    )
    swaps = [functools.partial(swap_bit, size=dp_size, bit=b) for b in range(dp_size.bit_length() - 1)]
    swaps += [functools.partial(swap_copy, size=copy_size, shift=n) for n in (1, 2)]

    def add_swapped(values, swap, *others):
        return tie(values + swap(values), *others)

    small_grads, grad_mixed = tie(small_grads, grad_mixed)
    small_grads, grad_mixed = add_swapped(small_grads, swaps[0], grad_mixed)
    grad_q, grad_k, grad_v = attention_back(queries, key_rows, value_rows, grad_mixed, ids)
    small_grads, grad_q = add_swapped(small_grads, swaps[1], grad_q)
    send, keep = pack_block_grads(
        [(first_z, grad_q), (first_z, grad_k), (first_z, grad_v), (mixed_z, grad_branch)],
        [],
        core,
        dp_size,
        kernels,
    )
    pack_four = Reduction(send, keep, 2 * k_d, dp_size, kernels)
    grad_q, pack_four.sent[0], pack_four.kept[0] = tie(grad_q, send, keep)
    pack_four.receive()
    two_parts, (grad_q,) = to_copies(pack_two, [grad_q])
    (grad_q,) = advance(pack_three, [grad_q])
    (grad_q,) = advance(pack_four, [grad_q])
    own_one_parts = own_and_other(one_parts, (place, core), kernels)
    small_grads, grad_q, *own_one_parts = add_swapped(small_grads, swaps[2], grad_q, *own_one_parts)
    for swap in swaps[3:]:
        small_grads = small_grads + swap(small_grads)

    grad_first = input_back(grad_q, w_q) + input_back(grad_k, w_k) + input_back(grad_v, w_v)

    own_up_down = finish(pack_three)
    own_up = jnp.concatenate(split_pack(own_up_down, [k_d] * 4), axis=1)
    own_down = own_up_down[4 * k_d :]

    block_small = jnp.concatenate(
        [
            jnp.stack(
                [
                    jnp.sum(grad_first * norm_one, axis=0),
                    jnp.sum(grad_second * norm_two, axis=0),
                    jnp.sum(grad_first, axis=0),
                    column_sum(grad_q),
                    column_sum(grad_v),
                    column_sum(grad_branch),
                    jnp.sum(grad_second, axis=0),
                    column_sum(grad_down),
                ]
            ),
            sums_hidden.reshape(-1, D),
        ],
        axis=0,
    )
    for bit in range(dp_size.bit_length() - 1):
        block_small = block_small + swap_bit(block_small, dp_size, bit)
    own_four = finish(pack_four)
    own_q, own_k, own_v, own_proj = split_pack(own_four, [k_d] * 4)
    own_fshift, own_fscale, own_two, own_one = split_pack(
        whole(*own_one_parts), [k_w] * 4
    )
    own_shift, own_scale, own_gate, own_time2, own_cond, own_time1 = split_pack(
        landed(two_parts), [k_w] * 4 + [k_d, k_t]
    )
    me = lax.axis_index("dp") * copy_size + place
    own_rest = lax.dynamic_slice_in_dim(block_small[:8], me * k_d, k_d, 1)
    own_gains, own_biases = own_rest[:2], own_rest[2:]
    own_up_bias = lax.dynamic_slice_in_dim(block_small[8:].reshape(ff), me * k_ff, k_ff)
    own_small = lax.dynamic_slice_in_dim(small_grads, me * k_w, k_w, 1)
    own_w_input = own_small[:CHANNELS]
    own_w_output = own_small[CHANNELS : 2 * CHANNELS].T
    own_head_gain = own_small[2 * CHANNELS]
    own_head_biases = own_small[2 * CHANNELS + 1 : 2 * CHANNELS + 13]
    grad_out_bias = small_grads[2 * CHANNELS + 13, :CHANNELS]

    mine = grad_first.reshape(micros, length, D)[:, :own].reshape(micros * own, D)
    mine_norm = norm_one.reshape(micros, length, D)[:, :own].reshape(micros * own, D)
    mine_inv = inv_one.reshape(micros, length, 1)[:, :own].reshape(micros * own, 1)
    mine_middle = grad_middle.reshape(micros, length, D)[:, :own].reshape(micros * own, D)
    input_grad = mine_middle + norm_back(mine * gains[0], mine_norm, mine_inv)
    input_grad = input_grad.reshape(micros, 1, own, D)
    block_output = condition.reshape(micros, length, D)[:, :own].reshape(micros, 1, own, D)
    return (
        block_output,
        input_grad,
        own_gains,
        own_biases,
        jnp.concatenate([own_q, own_k, own_v], axis=1),
        own_proj,
        own_up,
        own_up_bias,
        own_down,
        own_head_gain,
        own_head_biases,
        own_cond,
        own_time1,
        own_time2,
        own_w_input,
        jnp.concatenate([own_shift, own_scale, own_gate], axis=1),
        own_one,
        own_two,
        jnp.concatenate([own_fshift, own_fscale], axis=1),
        own_w_output,
        grad_out_bias,
    )


def solution(mesh):
    in_specs = (
        P(None, "dp", "copy", None),
        P(None, "dp", None),
        P(None, "dp", None, None),
        P(None, "copy", "dp", None, None),
        P(None, "copy", "dp", None),
        P(None, ("dp", "copy")),
        P(None, ("dp", "copy")),
        P(("dp", "copy"), None),
        P(("dp", "copy"), None),
        P(("dp", "copy"), None),
        P(("dp", "copy")),
        P(("dp", "copy"), None),
        P(("dp", "copy")),
        P(None, ("dp", "copy")),
        P(("dp", "copy"), None),
        P(("dp", "copy"), None),
        P(("dp", "copy"), None),
        P(None, ("dp", "copy")),
        P(("dp", "copy"), None),
        P(("dp", "copy"), None),
        P(("dp", "copy"), None),
        P(("dp", "copy"), None),
        P(("dp", "copy"), None),
        P(),
    )
    out_specs = (
        P(None, "dp", "copy", None),
        P(None, "dp", "copy", None),
        P(None, ("dp", "copy")),
        P(None, ("dp", "copy")),
        P(("dp", "copy"), None),
        P(("dp", "copy"), None),
        P(("dp", "copy"), None),
        P(("dp", "copy")),
        P(("dp", "copy"), None),
        P(("dp", "copy")),
        P(None, ("dp", "copy")),
        P(("dp", "copy"), None),
        P(("dp", "copy"), None),
        P(("dp", "copy"), None),
        P(None, ("dp", "copy")),
        P(("dp", "copy"), None),
        P(("dp", "copy"), None),
        P(("dp", "copy"), None),
        P(("dp", "copy"), None),
        P(("dp", "copy"), None),
        P(),
    )
    return jax.shard_map(shards, mesh=mesh, in_specs=in_specs, out_specs=out_specs, check_vma=False)
```

```python
import functools
import math

import jax
import jax.numpy as jnp
from jax import lax
from jax.experimental import pallas as pl
from jax.experimental.pallas import tpu as pltpu
from jax.sharding import PartitionSpec as P

D = 768
HEADS = 12
HEAD_DIM = 64
WIDTH = 1024
FREQ = 256
CHANNELS = 16
IMAGES = 4


epsilon = 1e-06
highest = lax.Precision.HIGHEST


def product(left_side, right_side):
    return jnp.dot(left_side, right_side, preferred_element_type=jnp.float32)


def weight_grad(left_side, right_side):
    return lax.dot_general(
        left_side, right_side, (((0,), (0,)), ((), ())), preferred_element_type=jnp.float32
    )


def input_back(gradient, weight):
    return lax.dot_general(
        gradient, weight, (((1,), (1,)), ((), ())), preferred_element_type=jnp.float32
    )


def column_sum(values):
    return jnp.sum(values.astype(jnp.float32), axis=0)


def normalize(values):
    center = values - jnp.mean(values, axis=-1, keepdims=True)
    inverse = lax.rsqrt(jnp.mean(center * center, axis=-1, keepdims=True) + epsilon)
    return (center * inverse, inverse)


def norm_back(gradient, normed, inverse):
    return inverse * (
        gradient
        - jnp.mean(gradient, axis=-1, keepdims=True)
        - normed * jnp.mean(gradient * normed, axis=-1, keepdims=True)
    )


def silu_slope(values):
    sigma = jax.nn.sigmoid(values)
    return sigma * (1.0 + values * (1.0 - sigma))


def gelu_slope(values):
    return 0.5 * (1.0 + lax.erf(values * 2.0 ** (-0.5))) + values * jnp.exp(
        -0.5 * values * values
    ) * (2.0 * math.pi) ** (-0.5)


def sinusoid(step_vals):
    half_width = FREQ // 2
    rates = jnp.exp(-math.log(10000.0) * jnp.arange(half_width, dtype=jnp.float32) / half_width)
    angles = step_vals[:, None] * rates[None, :]
    return jnp.concatenate([jnp.cos(angles), jnp.sin(angles)], axis=1)


def plan(step_vals):
    anchor = math.cos(0.008 / 1.008 * math.pi / 2.0) ** 2
    angle_now = ((step_vals + 1.0) / 1000.0 + 0.008) / 1.008 * (math.pi / 2.0)
    signal = jnp.cos(angle_now) ** 2 / anchor
    return jnp.stack([jnp.sqrt(signal), jnp.sqrt(1.0 - signal)], axis=1)


def tdot(left_side, right_side):
    return lax.dot_general(
        left_side, right_side, (((0,), (0,)), ((), ())), preferred_element_type=jnp.float32
    )


def swap_bit(values, size, bit):
    return lax.ppermute(values, "dp", [(i, i ^ (1 << bit)) for i in range(size)])


def shift_copy(values, size, shift):
    return lax.ppermute(values, "copy", [(i, (i + shift) % size) for i in range(size)])


def swap_copy(values, size, shift):
    return lax.ppermute(values, "copy", [(i, i ^ shift) for i in range(size)])


def pick(values, index, axis):
    return lax.dynamic_index_in_dim(values, index, axis, keepdims=False)


def tie(*values):
    return lax.optimization_barrier(values)


MIB = 1 << 20


LIGHT = pl.CostEstimate(flops=10**6, bytes_accessed=10**5, transcendentals=0)


def dot0(left_side, right_side):
    return lax.dot_general(
        left_side, right_side, (((0,), (0,)), ((), ())), preferred_element_type=jnp.float32
    )


def dot1(left_side, right_side):
    return lax.dot_general(
        left_side, right_side, (((1,), (1,)), ((), ())), preferred_element_type=jnp.float32
    )


def small_call(body, outs, scalars, ins):
    size = sum(math.prod(o.shape) * o.dtype.itemsize for o in outs)
    size += sum(math.prod(v.shape) * v.dtype.itemsize for v in ins)
    return pl.pallas_call(
        body,
        out_shape=outs,
        in_specs=[pl.BlockSpec(memory_space=pltpu.SMEM)]
        + [pl.BlockSpec(memory_space=pltpu.VMEM)] * len(ins),
        out_specs=[pl.BlockSpec(memory_space=pltpu.VMEM)] * len(outs),
        compiler_params=pltpu.CompilerParams(vmem_limit_bytes=60 * MIB),
        cost_estimate=LIGHT,
    )(jnp.stack([jnp.asarray(v, jnp.int32) for v in scalars]), *ins)


def low_shape(*dims):
    return jax.ShapeDtypeStruct(dims, jnp.bfloat16)


def add_up(one, two):
    return one.astype(jnp.float32) + two.astype(jnp.float32)


def cut_first(keeps, gots, rows, bits, kernels):
    count, mids, _, width = keeps[0].shape
    half = count // 2
    sizes = [k.shape[2] for k in keeps]
    total = sum(sizes)

    if not kernels:
        sums = jnp.concatenate([add_up(k, g) for k, g in zip(keeps, gots)], axis=2)
        sums = sums.astype(jnp.bfloat16)
        first = sums[:, :, :rows].reshape(2, half, mids, rows, width)
        second = sums[:, :, rows:].reshape(half, 2, mids, total - rows, width)
        return [
            pick(first, 1 - bits[0], 0),
            pick(first, bits[0], 0),
            pick(second, 1 - bits[1], 1),
            pick(second, bits[1], 1),
        ]

    def body(at, *refs):
        keep_refs, got_refs = refs[: len(keeps)], refs[len(keeps) : 2 * len(keeps)]
        outs = refs[2 * len(keeps) :]
        for out, bit, low in zip(outs, (1 - at[0], at[0], 1 - at[1], at[1]), (0, 0, 1, 1)):
            begin, end = (rows, total) if low else (0, rows)
            at_row = 0
            for keep, got, n in zip(keep_refs, got_refs, sizes):
                top, bottom = max(begin, at_row), min(end, at_row + n)
                if top < bottom:
                    cut = pl.ds(top - at_row, bottom - top)
                    for i in range(half):
                        p = 2 * i + bit if low else bit * half + i
                        value = add_up(keep[p, :, cut], got[p, :, cut]).astype(jnp.bfloat16)
                        out[i, :, top - begin : bottom - begin] = value
                at_row += n

    outs = [low_shape(half, mids, n, width) for n in (rows, rows, total - rows, total - rows)]
    return small_call(body, outs, bits, [*keeps, *gots])


def cut_next(keeps, gots, bits, kernels):
    count, mids, _, width = keeps[0].shape
    half = count // 2
    sizes = [k.shape[2] for k in keeps]
    if not kernels:
        sums = [add_up(k, g).astype(jnp.bfloat16) for k, g in zip(keeps, gots)]
        first = sums[0].reshape(2, half, mids, sizes[0], width)
        second = sums[1].reshape(half, 2, mids, sizes[1], width)
        return [
            pick(first, 1 - bits[0], 0),
            pick(first, bits[0], 0),
            pick(second, 1 - bits[1], 1),
            pick(second, bits[1], 1),
        ]

    def body(at, keep_one, got_one, keep_two, got_two, *outs):
        for out, bit, top in zip(outs, (1 - at[0], at[0], 1 - at[1], at[1]), (0, 0, 1, 1)):
            keep, got = (keep_two, got_two) if top else (keep_one, got_one)
            for i in range(half):
                p = 2 * i + bit if top else bit * half + i
                out[i] = add_up(keep[p], got[p]).astype(jnp.bfloat16)

    outs = [low_shape(half, mids, n, width) for n in (sizes[0], sizes[0], sizes[1], sizes[1])]
    return small_call(body, outs, bits, [keeps[0], gots[0], keeps[1], gots[1]])


def cut_copies(keeps, gots, place, copy_size, kernels):
    _, mids, _, width = keeps[0].shape
    sizes = [k.shape[2] for k in keeps]
    total = sum(sizes)
    if not kernels:
        sums = jnp.concatenate([add_up(k, g)[0] for k, g in zip(keeps, gots)], axis=1)
        sums = sums.astype(jnp.bfloat16).reshape(2, copy_size, total, width)
        return [pick(sums, lax.rem(place + j, copy_size), 1) for j in range(copy_size)]

    def body(at, keep_one, got_one, keep_two, got_two, *outs):
        for j in range(copy_size):
            z = lax.rem(at[0] + j, copy_size)
            for c in range(2):
                m = c * copy_size + z
                top = add_up(keep_one[0, m], got_one[0, m]).astype(jnp.bfloat16)
                low = add_up(keep_two[0, m], got_two[0, m]).astype(jnp.bfloat16)
                outs[j][c, : sizes[0]] = top
                outs[j][c, sizes[0] :] = low

    outs = [low_shape(2, total, width)] * copy_size
    return small_call(body, outs, [place], [keeps[0], gots[0], keeps[1], gots[1]])


def sum_low(parts, kernels):
    if not kernels:
        return sum(p.astype(jnp.float32) for p in parts).astype(jnp.bfloat16)

    def body(at, *refs):
        total = refs[0][...].astype(jnp.float32)
        for ref in refs[1:-1]:
            total = total + ref[...].astype(jnp.float32)
        refs[-1][...] = total.astype(jnp.bfloat16)

    return small_call(body, [low_shape(*parts[0].shape)], [0], parts)[0]


def own_and_other(parts, scalars, kernels):
    place, core = scalars
    count = len(parts)
    _, total, width = parts[0].shape
    if not kernels:
        stacked = jnp.stack(parts).astype(jnp.float32)
        sums = 0.0
        for i in range(count):
            sums = sums + pick(stacked, lax.rem(place + count - i, count), 0)
        sums = sums.astype(jnp.bfloat16)
        return [pick(sums, 1 - core, 0), pick(sums, core, 0)]

    def body(at, *refs):
        for out, c in zip(refs[count:], (1 - at[1], at[1])):
            values = [r[c].astype(jnp.float32) for r in refs[:count]]
            sums = None
            for i in range(count):
                turn = lax.rem(at[0] + count - i, count)
                value = values[0]
                for j in range(1, count):
                    value = jnp.where(turn == j, values[j], value)
                sums = value if sums is None else sums + value
            out[...] = sums.astype(jnp.bfloat16)

    return small_call(body, [low_shape(total, width)] * 2, scalars, parts)


class Reduction:
    def __init__(self, sent, kept, rows, size, kernels):
        self.size, self.rows, self.kernels = size, rows, kernels
        self.left = size.bit_length() - 2
        self.me = lax.axis_index("dp")
        self.sent, self.kept, self.bits = list(sent), list(kept), [0] * len(sent)
        self.first = True

    def receive(self):
        self.got = [swap_bit(v, self.size, bit) for v, bit in zip(self.sent, self.bits)]
        return self

    def advance(self):
        if self.first:
            self.bits = [self.left, 1]
            bits = [(self.me >> b) & 1 for b in self.bits]
            cuts = cut_first(self.kept, self.got, self.rows, bits, self.kernels)
        else:
            self.bits = [self.bits[0] - 1, self.bits[1] + 1]
            bits = [(self.me >> b) & 1 for b in self.bits]
            cuts = cut_next(self.kept, self.got, bits, self.kernels)
        self.first = False
        self.left -= 1
        self.sent, self.kept = [cuts[0], cuts[2]], [cuts[1], cuts[3]]
        return self


def attend(ids_col, ids_row, q, k, lanes, head, scale):
    wanted = (lanes >= HEAD_DIM) if head else (lanes < HEAD_DIM)
    scores = dot1(jnp.where(wanted, q, 0), k) * scale
    scores = jnp.where(ids_col == ids_row, scores, -1e30)
    exps = jnp.exp(scores - jnp.max(scores, axis=-1, keepdims=True))
    return wanted, exps / jnp.sum(exps, axis=-1, keepdims=True)


def attention_specs(micros, length, first=0):
    wide = pl.BlockSpec((length, 2 * HEAD_DIM), lambda m, h: (m + first, h))
    col = pl.BlockSpec((length, 1), lambda m, h: (m + first, 0))
    row = pl.BlockSpec((1, 1, length), lambda m, h: (m + first, 0, 0))
    return wide, col, row


def attention(queries, key_rows, value_rows, ids):
    micros, length = ids.shape
    scale = HEAD_DIM ** (-0.5)
    wide, col, row = attention_specs(micros, length)

    def body(col_ref, row_ref, q_ref, k_ref, v_ref, out_ref):
        lanes = lax.broadcasted_iota(jnp.int32, (1, 2 * HEAD_DIM), 1)
        outs = []
        for head in range(2):
            _, probs = attend(
                col_ref[...], row_ref[0], q_ref[...], k_ref[...], lanes, head, scale
            )
            outs.append(
                jnp.dot(
                    probs.astype(jnp.bfloat16), v_ref[...], preferred_element_type=jnp.float32
                )
            )
        out_ref[...] = jnp.where(lanes < HEAD_DIM, outs[0], outs[1]).astype(jnp.bfloat16)

    return pl.pallas_call(
        body,
        grid=(micros, HEADS // 2),
        out_shape=low_shape(micros * length, D),
        in_specs=[col, row, wide, wide, wide],
        out_specs=wide,
        compiler_params=pltpu.CompilerParams(vmem_limit_bytes=24 * MIB),
        cost_estimate=LIGHT,
    )(ids.reshape(-1, 1), ids[:, None], queries, key_rows, value_rows)


def attention_back(queries, key_rows, value_rows, grad_mixed, ids, which, before):
    micros, length = ids.shape
    scale = HEAD_DIM ** (-0.5)
    wide, col, row = attention_specs(micros, length, which)

    def body(col_ref, row_ref, q_ref, k_ref, v_ref, g_ref, *outs):
        lanes = lax.broadcasted_iota(jnp.int32, (1, 2 * HEAD_DIM), 1)
        q, k, v, g = q_ref[...], k_ref[...], v_ref[...], g_ref[...]
        parts = []
        for head in range(2):
            wanted, probs = attend(col_ref[...], row_ref[0], q, k, lanes, head, scale)
            grad_probs = dot1(jnp.where(wanted, g, 0), v)
            delta = jnp.sum(grad_probs * probs, axis=-1, keepdims=True)
            grad_scores = (probs * (grad_probs - delta)).astype(jnp.bfloat16)
            parts.append(
                (
                    jnp.dot(grad_scores, k, preferred_element_type=jnp.float32) * scale,
                    dot0(grad_scores, q) * scale,
                    dot0(probs.astype(jnp.bfloat16), g),
                )
            )
        for out, one, two in zip(outs[-3:], *parts):
            out[...] = jnp.where(lanes < HEAD_DIM, one, two).astype(jnp.bfloat16)

    return pl.pallas_call(
        body,
        grid=(1, HEADS // 2),
        out_shape=[low_shape(micros * length, D)] * 3,
        in_specs=[col, row, wide, wide, wide, wide]
        + [pl.BlockSpec(memory_space=pl.ANY)] * len(before or ()),
        out_specs=[wide] * 3,
        input_output_aliases={6 + i: i for i in range(len(before or ()))},
        compiler_params=pltpu.CompilerParams(vmem_limit_bytes=60 * MIB),
        cost_estimate=LIGHT,
    )(ids.reshape(-1, 1), ids[:, None], queries, key_rows, value_rows, grad_mixed, *(before or ()))


def pack_head_grads(pairs, core, dp_size, copy_size, kernels, others=(), plan=None):
    world = dp_size * copy_size
    count, mids = dp_size // 2, 2 * copy_size
    width = pairs[0][1].shape[1]
    half = width // 2
    sizes = [p[0].shape[1] // world for p in pairs]
    total = sum(sizes)
    if not kernels:
        packs = []
        for c in (1 - core, core):
            parts = []
            for left_side, right_side in pairs:
                part = lax.dynamic_slice_in_dim(right_side, c * half, half, 1)
                part = weight_grad(left_side, part).astype(jnp.bfloat16)
                parts.append(part.reshape(count, mids, -1, half))
            packs.append(jnp.concatenate(parts, axis=2))
        given = [jnp.stack([column_sum(p[1]) for p in pairs]), *others]
        if plan is None:
            return packs + given
        return packs + [jnp.concatenate([given[i][at : at + n] for i, at, n in plan])]

    lefts, which = [], []
    for left_side, _ in pairs:
        seen = [i for i, other in enumerate(lefts) if other is left_side]
        which.append(seen[0] if seen else len(lefts))
        lefts += [] if seen else [left_side]
    rights = [p[1] for p in pairs]
    narrow = [v.shape[1] // count % 128 == 0 for v in lefts]
    held = [i for i, w in enumerate(which) if not narrow[w]]

    where, height = list(range(len(pairs))), len(pairs)
    if plan is not None:
        at_row = 0
        for source, row, n in plan:
            if not source:
                where[row : row + n] = range(at_row, at_row + n)
            at_row += n
        height = at_row

    def body(at, *refs):
        left_refs = refs[: len(lefts)]
        right_refs = refs[len(lefts) : len(lefts) + len(rights)]
        other_refs, refs = refs[len(lefts) + len(rights) :][: len(others)], refs[len(others) :]
        sent, kept, sums = refs[len(lefts) + len(rights) :][:3]
        scratch = refs[len(lefts) + len(rights) + 3 :]
        first = at[0] == 0
        step = pl.program_id(0)

        @pl.when(step == 0)
        def _():
            for i, right in enumerate(right_refs):
                ones = jnp.ones((8, right.shape[0]), jnp.bfloat16)
                row = jnp.dot(ones, right[...], preferred_element_type=jnp.float32)
                sums[where[i] : where[i] + 1] = row[:1]
            at = 0
            for source, row, n in plan or ():
                if source:
                    sums[at : at + n] = other_refs[source - 1][row : row + n]
                at += n
            for i, buffer in zip(held, scratch):
                buffer[...] = dot0(left_refs[which[i]][...], right_refs[i][...])

        at_row = 0
        for i, n in enumerate(sizes):
            if i in held:
                rows = mids * n
                whole = scratch[held.index(i)][pl.ds(pl.multiple_of(step * rows, 8), rows)]
            else:
                whole = dot0(left_refs[which[i]][...], right_refs[i][...])
            left, right = whole[:, :half], whole[:, half:]
            for out, part in (
                (sent, jnp.where(first, right, left)),
                (kept, jnp.where(first, left, right)),
            ):
                out[0, :, at_row : at_row + n] = part.reshape(mids, n, half).astype(jnp.bfloat16)
            at_row += n

    in_specs = [pl.BlockSpec(memory_space=pltpu.SMEM)]
    for v, cut_up in zip(lefts, narrow):
        if cut_up:
            in_specs.append(pl.BlockSpec((v.shape[0], v.shape[1] // count), lambda p: (0, p)))
        else:
            in_specs.append(pl.BlockSpec(v.shape, lambda p: (0, 0)))
    in_specs += [pl.BlockSpec(v.shape, lambda p: (0, 0)) for v in [*rights, *others]]
    out_spec = pl.BlockSpec((1, mids, total, half), lambda p: (p, 0, 0, 0))
    return pl.pallas_call(
        body,
        grid=(count,),
        out_shape=[low_shape(count, mids, total, half)] * 2
        + [jax.ShapeDtypeStruct((height, width), jnp.float32)],
        in_specs=in_specs,
        out_specs=[out_spec] * 2 + [pl.BlockSpec((height, width), lambda p: (0, 0))],
        scratch_shapes=[
            pltpu.VMEM((lefts[which[i]].shape[1], width), jnp.float32) for i in held
        ],
        compiler_params=pltpu.CompilerParams(vmem_limit_bytes=60 * MIB),
        cost_estimate=LIGHT,
    )(jnp.asarray(core, jnp.int32)[None], *lefts, *rights, *others)


def assemble(pieces, scalars, copy_size, rows):
    width = pieces[0][0].shape[-1]
    total = rows

    def body(at, *refs):
        ins, out, sems = refs[: len(pieces)], refs[len(pieces)], refs[len(pieces) + 1]
        copies = []
        for ref, (value, first, flip, vary) in zip(ins, pieces):
            for d in range(2):
                for j in range(copy_size):
                    dp = at[0] ^ (flip | (vary if d else 0))
                    owner = dp * copy_size + lax.rem(at[1] + j, copy_size)
                    copy = pltpu.make_async_copy(
                        ref.at[d, j],
                        out.at[owner, pl.ds(first, value.shape[2])],
                        sems.at[len(copies)],
                    )
                    copy.start()
                    copies.append(copy)
        for copy in copies:
            copy.wait()

    return pl.pallas_call(
        body,
        out_shape=low_shape(8 * copy_size, total, width),
        in_specs=[pl.BlockSpec(memory_space=pltpu.SMEM)]
        + [pl.BlockSpec(memory_space=pl.ANY)] * len(pieces),
        out_specs=pl.BlockSpec(memory_space=pl.ANY),
        scratch_shapes=[pltpu.SemaphoreType.DMA((len(pieces) * 2 * copy_size,))],
        compiler_params=pltpu.CompilerParams(vmem_limit_bytes=4 * MIB),
        cost_estimate=LIGHT,
    )(jnp.stack([jnp.asarray(v, jnp.int32) for v in scalars]), *[p[0] for p in pieces])


def gather(pack, rows, arrived):
    total = pack.shape[0]
    along = [pack, *arrived]
    pieces = []
    for first, last, bits in ((0, rows, (2, 1)), (rows, total, (1, 2))):
        held = jnp.stack([v[first:last] for v in along])
        held = jnp.stack([held, swap_bit(held, 8, bits[0])])
        got = swap_bit(held, 8, bits[1])
        vary = 1 << bits[0]
        other = 1 << bits[1]
        pieces += [(held, first, 0, vary), (got, first, other, vary)]
        pieces += [
            (swap_bit(held, 8, 0), first, 1, vary),
            (swap_bit(got, 8, 0), first, other | 1, vary),
        ]
    return assemble(pieces, (lax.axis_index("dp"), lax.axis_index("copy")), 4, total)


LANES = 128


def padded_lanes(values):
    return jnp.pad(values, ((0, 0), (0, LANES - values.shape[1]))).reshape(-1)


def spread(packed, sizes):
    world = packed.shape[0]
    total = sum(count for count, _ in sizes)

    def body(packed_ref, *outs):
        at = 0
        for (count, k), out in zip(sizes, outs):
            width = world * k
            column = lax.broadcasted_iota(jnp.int32, (LANES, width), 1)
            row = lax.broadcasted_iota(jnp.int32, (LANES, width), 0)
            tile = (row == column % k).astype(jnp.bfloat16)
            owner = lax.broadcasted_iota(jnp.int32, (world, width), 0)
            own = owner == lax.broadcasted_iota(jnp.int32, (world, width), 1) // k
            for i in range(count):
                block = packed_ref[:, (at + i) * LANES : (at + i + 1) * LANES]
                values = jnp.dot(block, tile, preferred_element_type=jnp.float32)
                out[i : i + 1] = jnp.sum(jnp.where(own, values, 0.0), axis=0, keepdims=True)
            at += count

    return pl.pallas_call(
        body,
        out_shape=[
            jax.ShapeDtypeStruct((count, world * k), jnp.float32) for count, k in sizes
        ],
        in_specs=[pl.BlockSpec(memory_space=pltpu.VMEM)],
        out_specs=[pl.BlockSpec(memory_space=pltpu.VMEM)] * len(sizes),
        compiler_params=pltpu.CompilerParams(vmem_limit_bytes=16 * MIB),
        cost_estimate=LIGHT,
    )(packed[:, : total * LANES])


def head_step(weight, head_bias, gain, out_bias, embedded, values):
    bf16, f32 = jnp.bfloat16, jnp.float32
    condition, noisy, noise, slot = values
    out, sums = {}, {}
    valid = (slot >= 0).astype(f32)
    cond = product(condition, weight("cond")) + head_bias(0)
    chosen = jnp.zeros_like(cond)
    for i in range(embedded.shape[0]):
        chosen = jnp.where(slot == i, embedded[i : i + 1], chosen)
    cond = cond + chosen
    gated = jax.nn.silu(cond).astype(bf16)
    out["gated"] = gated
    entry = product(noisy, weight("input")) + head_bias(3)
    norm_head, inv_head = normalize(entry)
    affine = norm_head * gain + head_bias(4)
    shift = product(gated, weight("shift")) + head_bias(7)
    scale = product(gated, weight("scale")) + head_bias(8)
    mlp_in = (affine * (1.0 + scale) + shift).astype(bf16)
    out["mlp_in"] = mlp_in
    inner_one = product(mlp_in, weight("one")) + head_bias(5)
    inner_act = jax.nn.silu(inner_one).astype(bf16)
    out["inner_act"] = inner_act
    inner_two = product(inner_act, weight("two")) + head_bias(6)
    gate = product(gated, weight("gate")) + head_bias(9)
    residual = entry + gate * inner_two
    fshift = product(gated, weight("fshift")) + head_bias(10)
    fscale = product(gated, weight("fscale")) + head_bias(11)
    norm_final, inv_final = normalize(residual)
    final_in = (norm_final * (1.0 + fscale) + fshift).astype(bf16)
    predicted = input_back(final_in, weight("output")) + out_bias
    grad_pred = ((predicted - noise) * valid).astype(bf16)
    sums["output"] = weight_grad(grad_pred, final_in)
    sums["out_bias"] = jnp.sum(grad_pred.astype(f32), axis=0, keepdims=True)
    grad_final_in = product(grad_pred, weight("output"))
    out["fshift"] = grad_final_in.astype(bf16)
    out["fscale"] = (grad_final_in * norm_final).astype(bf16)
    grad_residual = norm_back(grad_final_in * (1.0 + fscale), norm_final, inv_final)
    out["two"] = (grad_residual * gate).astype(bf16)
    grad_one = input_back(out["two"], weight("two")) * silu_slope(inner_one)
    out["one"] = grad_one.astype(bf16)
    grad_mlp_in = input_back(out["one"], weight("one"))
    out["shift"] = grad_mlp_in.astype(bf16)
    out["scale"] = (grad_mlp_in * affine).astype(bf16)
    out["gate"] = (grad_residual * inner_two).astype(bf16)
    grad_gated = input_back(out["shift"], weight("shift"))
    for name in ("scale", "gate", "fshift", "fscale"):
        grad_gated = grad_gated + input_back(out[name], weight(name))
    grad_cond = grad_gated * silu_slope(cond)
    out["cond"] = grad_cond.astype(bf16)
    out["condition"] = input_back(out["cond"], weight("cond")).astype(bf16)
    grad_affine = grad_mlp_in * (1.0 + scale)
    grad_entry = grad_residual + norm_back(grad_affine * gain, norm_head, inv_head)
    grad_entry = grad_entry.astype(bf16)
    sums["input"] = weight_grad(noisy, grad_entry)
    sums["gain"] = jnp.sum(grad_affine * norm_head, axis=0, keepdims=True)
    sums["entry"] = jnp.sum(grad_entry.astype(f32), axis=0, keepdims=True)
    sums["affine"] = jnp.sum(grad_affine, axis=0, keepdims=True)
    lanes = lax.broadcasted_iota(jnp.int32, (slot.shape[0], embedded.shape[0]), 1)
    onehot = (slot == lanes).astype(bf16)
    low_part = (grad_cond - out["cond"].astype(f32)).astype(bf16)
    sums["embedded"] = weight_grad(onehot, out["cond"]) + weight_grad(onehot, low_part)
    return out, sums


SQUARES = ("shift", "scale", "gate", "time2", "one", "two", "fshift", "fscale")
HEAD_OUT = (
    "gated", "mlp_in", "inner_act", "fshift", "fscale", "two", "one", "shift", "scale", "gate",
    "cond", "condition",
)
HEAD_SUMS = (
    ("input", CHANNELS), ("output", CHANNELS), ("embedded", 8), ("gain", 1), ("entry", 1),
    ("affine", 1), ("out_bias", 1),
)


def head_kernel(pack, w_cond, w_input, w_output, head_bias, gain, out_bias, embedded, values, k):
    rows = values[0].shape[0]
    step = 256
    world = pack.shape[0]
    used = [i for i, name in enumerate(SQUARES) if name != "time2"]
    height = sum(n for _, n in HEAD_SUMS)
    height += -height % 8
    smalls = [w_cond, w_input, w_output, head_bias, gain, out_bias, embedded]

    def body(*refs):
        ins = refs[: len(smalls)]
        pack_ref = refs[len(smalls)]
        tiles = refs[len(smalls) + 1 :][:4]
        outs = refs[len(smalls) + 5 :][: len(HEAD_OUT)]
        sums_ref, buffer, sems = refs[len(smalls) + 5 + len(HEAD_OUT) :]
        first = pl.program_id(0) == 0

        def fetch(n):
            return pltpu.make_async_copy(
                pack_ref.at[:, pl.ds(used[n] * k, k)], buffer.at[n], sems.at[n]
            )

        @pl.when(first)
        def _():
            for n in range(len(used)):
                fetch(n).start()

        ready = set()

        def weight(name):
            if name in ("cond", "input", "output"):
                return ins[("cond", "input", "output").index(name)][...]
            n = used.index(SQUARES.index(name))
            if n not in ready:
                ready.add(n)

                @pl.when(first)
                def _():
                    fetch(n).wait()

            return buffer[n].reshape(WIDTH, WIDTH)

        out, sums = head_step(
            weight,
            lambda i: ins[3][i : i + 1],
            ins[4][...],
            ins[5][...],
            ins[6][...],
            [t[...] for t in tiles],
        )
        for name, ref in zip(HEAD_OUT, outs):
            ref[...] = out[name]

        @pl.when(first)
        def _():
            sums_ref[...] = jnp.zeros((height, WIDTH), jnp.float32)

        at = 0
        for name, n in HEAD_SUMS:
            width = sums[name].shape[1]
            sums_ref[at : at + n, :width] += sums[name]
            at += n

    def tall(width):
        return pl.BlockSpec((step, width), lambda i: (i, 0))

    widths = [D if name == "condition" else WIDTH for name in HEAD_OUT]
    *outs, sums = pl.pallas_call(
        body,
        grid=(rows // step,),
        out_shape=[low_shape(rows, w) for w in widths]
        + [jax.ShapeDtypeStruct((height, WIDTH), jnp.float32)],
        in_specs=[
            pl.BlockSpec(v.shape, lambda i: (0, 0), pipeline_mode=pl.Buffered(1)) for v in smalls
        ]
        + [pl.BlockSpec(memory_space=pl.ANY)]
        + [tall(v.shape[1]) for v in values],
        out_specs=[tall(w) for w in widths]
        + [pl.BlockSpec((height, WIDTH), lambda i: (0, 0))],
        scratch_shapes=[
            pltpu.VMEM((len(used), world, k, WIDTH), jnp.bfloat16),
            pltpu.SemaphoreType.DMA((len(used),)),
        ],
        compiler_params=pltpu.CompilerParams(vmem_limit_bytes=60 * MIB),
        cost_estimate=LIGHT,
    )(*smalls, pack, *values)
    return dict(zip(HEAD_OUT, outs)), sums


def pack_block_grads(pairs, core, dp_size):
    count = dp_size // 2
    half = D // 2
    packs = []
    for c in (1 - core, core):
        parts = []
        for left_side, right_side in pairs:
            for at in range(0, right_side.shape[1], D):
                part = lax.dynamic_slice_in_dim(right_side, at + c * half, half, 1)
                part = weight_grad(left_side, part).astype(jnp.bfloat16)
                parts.append(part.reshape(count, 2, -1, half))
        packs.append(jnp.concatenate(parts, axis=2))
    return packs


def put_halves(first, sent, kept, at_row, whole):
    half = D // 2
    count = sent.shape[0]
    n = whole.shape[0] // (2 * count)
    left, right = whole[:, :half], whole[:, half:]
    for out, part in (
        (sent, jnp.where(first, right, left)),
        (kept, jnp.where(first, left, right)),
    ):
        part = part.reshape(count, 2, n, half).astype(jnp.bfloat16)
        out[:, :, at_row : at_row + n] = part


def feed_forward(second_in, middle, ups, up_bias, w_down, down_bias, place, copy_size, kernels):
    bf16, f32 = jnp.bfloat16, jnp.float32
    rows = middle.shape[0]
    steps = len(ups)

    def step_of(hidden):
        half = 0.5 * (1.0 + lax.erf(hidden * 2.0 ** (-0.5)))
        bell = jnp.exp(-0.5 * hidden * hidden) * (2.0 * math.pi) ** (-0.5)
        return (hidden * half).astype(bf16), (half + hidden * bell).astype(bf16)

    if not kernels:
        hidden = product(second_in, jnp.concatenate(ups, axis=1)) + up_bias
        active, slope = step_of(hidden)
        output = middle + product(active, w_down) + down_bias
        return output.astype(bf16), slope, None, active

    per = w_down.shape[0] // steps
    k = per // (2 * copy_size)
    width = per // copy_size

    def body(at, *refs):
        up_refs, refs = refs[:steps], refs[steps:]
        in_ref, middle_ref, bias_ref, down_ref, down_bias_ref = refs[:5]
        out_ref, slope_ref, chosen_ref, total, hidden = refs[5:]
        step = pl.program_id(0)
        for n in range(steps):

            @pl.when(step == n)
            def _():
                hidden[...] = product(in_ref[...], up_refs[n][...])

        active, slope = step_of(hidden[...] + bias_ref[...])
        slope_ref[...] = slope
        part = product(active, down_ref[...])
        source = lax.broadcasted_iota(jnp.int32, (per, width), 0)
        target = lax.broadcasted_iota(jnp.int32, (per, width), 1)
        wanted = (target // k * copy_size + at[0]) * k + target % k
        one_hot = (source == wanted).astype(bf16)
        chosen_ref[0] = product(active, one_hot).astype(bf16)

        @pl.when(step == 0)
        def _():
            total[...] = middle_ref[...] + down_bias_ref[...] + part

        @pl.when(step > 0)
        def _():
            total[...] += part

        @pl.when(step == steps - 1)
        def _():
            out_ref[...] = total[...].astype(bf16)

    def full(v):
        return pl.BlockSpec(v.shape, lambda j: (0,) * len(v.shape), pipeline_mode=pl.Buffered(1))

    out, slope, chosen = pl.pallas_call(
        body,
        grid=(steps,),
        out_shape=[low_shape(rows, D), low_shape(rows, per * steps), low_shape(steps, rows, width)],
        in_specs=[pl.BlockSpec(memory_space=pltpu.SMEM)]
        + [full(v) for v in (*ups, second_in, middle)]
        + [
            pl.BlockSpec((1, per), lambda j: (0, j)),
            pl.BlockSpec((per, D), lambda j: (j, 0)),
            full(down_bias),
        ],
        out_specs=[
            pl.BlockSpec((rows, D), lambda j: (0, 0)),
            pl.BlockSpec((rows, per), lambda j: (0, j)),
            pl.BlockSpec((1, rows, width), lambda j: (j, 0, 0)),
        ],
        scratch_shapes=[pltpu.VMEM((rows, D), f32), pltpu.VMEM((rows, per), f32)],
        compiler_params=pltpu.CompilerParams(vmem_limit_bytes=48 * MIB),
        cost_estimate=LIGHT,
    )(place[None], *ups, second_in, middle, up_bias, w_down, down_bias)
    return out, slope, chosen, None


def block_back_one(pieces, slope, ups, w_down, w_proj, lefts, norm, inverse, gain, core, dp_size, kernels):
    bf16, f32 = jnp.bfloat16, jnp.float32
    micros, own, _ = pieces[0].shape
    rows = micros * own * len(pieces)
    steps = len(ups)
    k = lefts[0].shape[1] // dp_size
    k_down = w_down.shape[0] // (dp_size * len(pieces))
    if not kernels:
        grad = jnp.stack(pieces, axis=1).reshape(rows, D)
        hidden = (input_back(grad, w_down) * slope.astype(f32)).astype(bf16)
        second = input_back(hidden, jnp.concatenate(ups, axis=1))
        middle = grad.astype(f32) + norm_back(second * gain, norm, inverse)
        low = middle.astype(bf16)
        sums = [jnp.sum(second * norm, axis=0), jnp.sum(second, axis=0)]
        sums = jnp.stack(sums + [column_sum(low), column_sum(grad)])
        packs = pack_block_grads([(lefts[0], hidden), (lefts[1], grad)], core, dp_size)
        mixed = input_back(low, w_proj).astype(bf16)
        return *packs, middle, low, mixed, sums, column_sum(hidden).reshape(steps, 1, D)

    def body(at, *refs):
        piece_refs, refs = refs[: len(pieces)], refs[len(pieces) :]
        up_refs, refs = refs[:steps], refs[steps:]
        slope_ref, down_ref, proj_ref, left_up, left_down, norm_ref, inv_ref, gain_ref = refs[:8]
        sent, kept, middle_ref, low_ref, mixed_ref, sums_ref, hidden_sums, grad, total = refs[8:]
        step = pl.program_id(0)
        first = at[0] == 0

        @pl.when(step == 0)
        def _():
            for m in range(micros):
                for n, ref in enumerate(piece_refs):
                    start = (m * len(pieces) + n) * own
                    grad[start : start + own] = ref[m]
            for n in range(steps):
                here = pl.ds(n * dp_size // (2 * steps), dp_size // (2 * steps))
                part = dot0(left_down[n], grad[...])
                put_halves(first, sent.at[here], kept.at[here], steps * k, part)
            total[...] = jnp.zeros_like(total)

        hidden = dot1(grad[...], down_ref[...]) * slope_ref[...].astype(f32)
        hidden = hidden.astype(bf16)
        ones = jnp.ones((8, rows), bf16)
        hidden_sums[0] = jnp.dot(ones, hidden, preferred_element_type=f32)
        up_grad = dot0(left_up[...], hidden)
        for n in range(steps):

            @pl.when(step == n)
            def _():
                total[...] += dot1(hidden, up_refs[n][...])
                put_halves(first, sent, kept, n * k, up_grad)

        @pl.when(step == steps - 1)
        def _():
            second, norm_now = total[...], norm_ref[...]
            given = grad[...].astype(f32)
            middle = given + norm_back(second * gain_ref[...], norm_now, inv_ref[...])
            low = middle.astype(bf16)
            middle_ref[...] = middle
            low_ref[...] = low
            mixed_ref[...] = dot1(low, proj_ref[...]).astype(bf16)
            for n, values in enumerate((second * norm_now, second, low.astype(f32), given)):
                sums_ref[n : n + 1] = jnp.sum(values, axis=0, keepdims=True)

    def full(v):
        return pl.BlockSpec(v.shape, lambda j: (0,) * len(v.shape), pipeline_mode=pl.Buffered(1))

    pack = low_shape(dp_size // 2, 2, steps * k + k_down, D // 2)
    tall = jax.ShapeDtypeStruct((rows, D), f32)
    outs = [pack, pack, tall, low_shape(rows, D), low_shape(rows, D)]
    outs += [jax.ShapeDtypeStruct((8, D), f32)]
    ins = [*pieces, *ups, slope, w_down, w_proj, *lefts, norm, inverse, gain]
    in_specs = [full(v) for v in ins]
    in_specs[len(pieces) + steps] = pl.BlockSpec((rows, D), lambda j: (0, j))
    in_specs[len(pieces) + steps + 1] = pl.BlockSpec((D, D), lambda j: (j, 0))
    return pl.pallas_call(
        body,
        grid=(steps,),
        out_shape=outs + [jax.ShapeDtypeStruct((steps, 8, D), f32)],
        in_specs=[pl.BlockSpec(memory_space=pltpu.SMEM)] + in_specs,
        out_specs=[pl.BlockSpec(v.shape, lambda j, n=len(v.shape): (0,) * n) for v in outs]
        + [pl.BlockSpec((1, 8, D), lambda j: (j, 0, 0))],
        scratch_shapes=[pltpu.VMEM((rows, D), bf16), pltpu.VMEM((rows, D), f32)],
        compiler_params=pltpu.CompilerParams(vmem_limit_bytes=60 * MIB),
        cost_estimate=LIGHT,
    )(jnp.asarray(core, jnp.int32)[None], *ins)


def block_back_two(grads, weights, lefts, low, middle, norm, inverse, gain, sums, hidden_sums, own, micros, core, dp_size, kernels):
    f32 = jnp.float32
    rows = low.shape[0]
    length = rows // micros
    steps = hidden_sums.shape[0]

    def smalls(first, norm_now, q, v):
        return [
            jnp.sum(first * norm_now, axis=0, keepdims=True),
            None,
            jnp.sum(first, axis=0, keepdims=True),
            jnp.sum(q.astype(f32), axis=0, keepdims=True),
            jnp.sum(v.astype(f32), axis=0, keepdims=True),
        ]

    if not kernels:
        first = sum(input_back(g, w) for g, w in zip(grads, weights))
        input_grad = middle + norm_back(first * gain, norm, inverse)
        input_grad = input_grad.reshape(micros, length, D)[:, :own]
        rows_of = smalls(first, norm, grads[0], grads[2])
        rows_of[1] = sums[:1]
        small = jnp.concatenate([*rows_of, sums[2:3], sums[1:2], sums[3:4], hidden_sums[:, 0]])
        pairs = [(lefts[0], g) for g in grads] + [(lefts[1], low)]
        return *pack_block_grads(pairs, core, dp_size), input_grad, small

    k = lefts[0].shape[1] // dp_size

    def body(at, *refs):
        grad_refs, weight_refs, refs = refs[:3], refs[3:6], refs[6:]
        left_in, left_mixed, low_ref, middle_ref, norm_ref, inv_ref, gain_ref = refs[:7]
        sums_ref, hidden_ref, sent, kept, out_ref, small_ref = refs[7:]
        flag = at[0] == 0
        for n, ref in enumerate(grad_refs):
            put_halves(flag, sent, kept, n * k, dot0(left_in[...], ref[...]))
        put_halves(flag, sent, kept, 3 * k, dot0(left_mixed[...], low_ref[...]))
        first = dot1(grad_refs[0][...], weight_refs[0][...])
        for g, w in zip(grad_refs[1:], weight_refs[1:]):
            first = first + dot1(g[...], w[...])
        for n, value in enumerate(
            smalls(first, norm_ref[...], grad_refs[0][...], grad_refs[2][...])
        ):
            if value is not None:
                small_ref[n : n + 1] = value
        small_ref[1:2] = sums_ref[0:1]
        small_ref[5:6] = sums_ref[2:3]
        small_ref[6:7] = sums_ref[1:2]
        small_ref[7:8] = sums_ref[3:4]
        for n in range(steps):
            small_ref[8 + n : 9 + n] = hidden_ref[n, 0:1]
        for m in range(micros):
            here = pl.ds(m * length, own)
            back = norm_back(
                first[m * length : m * length + own] * gain_ref[...], norm_ref[here], inv_ref[here]
            )
            out_ref[m] = middle_ref[here] + back

    pack = low_shape(dp_size // 2, 2, 4 * k, D // 2)
    outs = [pack, pack, jax.ShapeDtypeStruct((micros, own, D), f32)]
    outs += [jax.ShapeDtypeStruct((8 + steps, D), f32)]
    ins = [*grads, *weights, *lefts, low, middle, norm, inverse, gain, sums, hidden_sums]
    return small_call(body, outs, [core], ins)


def shards(
    block_input,
    image_ids,
    latents,
    noise,
    timesteps,
    norm_gains,
    block_biases,
    w_qkv,
    w_proj,
    w_up,
    up_bias,
    w_down,
    head_gain,
    head_biases,
    w_cond,
    w_time1,
    w_time2,
    w_input,
    w_ada,
    w_mlp1,
    w_mlp2,
    w_final,
    w_output,
    output_bias,
):
    bf16, f32 = jnp.bfloat16, jnp.float32
    dp_size, copy_size = lax.axis_size("dp"), lax.axis_size("copy")
    world = dp_size * copy_size
    place = lax.axis_index("copy")
    micros, _, own, _ = block_input.shape
    length = image_ids.shape[2]
    total = micros * length
    k_d, k_ff, k_w, k_t = D // world, w_down.shape[0], WIDTH // world, w_time1.shape[0]
    ff = k_ff * world
    kernels = k_d % 8 == 0 and k_w % 16 == 0 and k_t % 8 == 0
    score_scale = HEAD_DIM ** (-0.5)

    def cut(matrix, width):
        return [matrix[:, i : i + width] for i in range(0, matrix.shape[1], width)]

    def pad_flat(parts, width):
        flat = jnp.concatenate([padded_lanes(p) for p in parts])
        count = -(-flat.shape[0] // (16 * width)) * 16 * width
        return jnp.pad(flat, (0, count - flat.shape[0])).reshape(-1, width)

    groups = [
        (cut(w_qkv, D) + [w_proj, pad_flat([norm_gains, block_biases, up_bias[None]], D)], 2),
        (cut(w_up, D) + [w_down], 4),
        (
            cut(w_ada, WIDTH)
            + [w_time2, w_mlp1, w_mlp2]
            + cut(w_final, WIDTH)
            + [w_cond, w_time1]
            + [pad_flat([w_input, w_output.T, head_gain[None], head_biases], WIDTH)],
            0,
        ),
    ]

    def everyone(pack):
        return [shift_copy(pack, copy_size, copy_size - j) for j in range(1, copy_size)]

    def unpack(pack, parts):
        out, at = [], 0
        for part in parts:
            out.append(pack[:, at : at + part.shape[0]].reshape(-1, pack.shape[2]))
            at += part.shape[0]
        return out

    own_rows = block_input[:, 0]
    packs = [jnp.concatenate(parts, 0) for parts, _ in groups]
    if kernels and dp_size == 8 and copy_size == 4:
        head_own = packs[2]
        arrived = [everyone(packs[0])]
        *arrived[0], packs[1] = tie(*arrived[0], packs[1])
        arrived.append(everyone(packs[1]))
        *arrived[1], own_rows, head_own = tie(*arrived[1], own_rows, head_own)
        rows_arrived = everyone(own_rows)
        full = [
            gather(pack, sum(p.shape[0] for p in parts[:n]), got)
            for pack, (parts, n), got in zip(packs[:2], groups[:2], arrived[:2])
        ]
        head = lax.all_gather(head_own, ("dp", "copy"), axis=0)
        full.append(head)
    else:
        rows_arrived = everyone(own_rows)
        full = [lax.all_gather(pack, ("dp", "copy"), axis=0) for pack in packs]
    head_pack = full[2]
    full = [unpack(pack, parts) for pack, (parts, _) in zip(full, groups)]

    rows = jnp.stack([own_rows, *rows_arrived], axis=1).reshape(total, D).astype(f32)

    def turned(values):
        twice = jnp.concatenate([values, values], axis=1)
        return lax.dynamic_slice_in_dim(twice, place * own, length, 1)

    ids = turned(image_ids[:, 0])
    latent_rows = turned(latents[:, 0]).reshape(total, CHANNELS)
    noise_rows = turned(noise[:, 0, 0]).reshape(total, CHANNELS)

    w_q, w_k, w_v, w_proj_full, small = full[0]
    w_down_full = full[1][4]
    small = small.reshape(world, -1)
    gains, biases, up_bias_full = spread(small, [(2, k_d), (6, k_d), (1, k_ff)])

    norm_one, inv_one = normalize(rows)
    first_in = (norm_one * gains[0] + biases[0]).astype(bf16)
    queries = (product(first_in, w_q) + biases[1]).astype(bf16)
    key_rows = product(first_in, w_k).astype(bf16)
    value_rows = (product(first_in, w_v) + biases[2]).astype(bf16)
    mixed = attention(queries, key_rows, value_rows, ids)
    middle = rows + product(mixed, w_proj_full) + biases[3]
    norm_two, inv_two = normalize(middle)
    second_in = (norm_two * gains[1] + biases[4]).astype(bf16)
    condition, slope, active_z, active = feed_forward(
        second_in,
        middle,
        full[1][:4],
        up_bias_full,
        w_down_full,
        biases[5:6],
        place,
        copy_size,
        kernels,
    )

    def chosen(values):
        width = values.shape[1]
        k = width // world
        source = jnp.arange(width, dtype=jnp.int32)[:, None]
        target = jnp.arange(dp_size * k, dtype=jnp.int32)[None, :]
        wanted = (target // k * copy_size + place) * k + target % k
        return product(values, (source == wanted).astype(bf16)).astype(bf16)

    condition, first_z, mixed_z, second_z, active_z, slope, norm_one, inv_one, norm_two, inv_two = tie(
        condition,
        chosen(first_in),
        chosen(mixed),
        chosen(second_in),
        chosen(active) if active_z is None else active_z,
        slope,
        norm_one,
        inv_one,
        norm_two,
        inv_two,
    )
    core = lax.axis_index("dp") & 1

    def split_pack(pack, parts):
        out, at = [], 0
        for rows_of in parts:
            out.append(pack[at : at + rows_of])
            at += rows_of
        return out

    def after(first, *values):
        first = list(first)
        return list(tie(*first, *values)[len(first) :])

    def send_after(reduction, first):
        reduction.sent = after(first, *reduction.sent)
        return reduction.receive()

    def form_after(reduction, first):
        reduction.got = after(first, *reduction.got)
        reduction.advance()
        return [*reduction.sent, *reduction.kept]

    def to_copies(reduction, first):
        reduction.got = after(first, *reduction.got)
        chunks = cut_copies(reduction.kept, reduction.got, place, copy_size, kernels)
        arriving = [shift_copy(chunks[j], copy_size, j) for j in range(1, copy_size)]
        return [chunks[0], *arriving]

    def whole(other, mine):
        got = swap_bit(other, dp_size, 0)
        left = jnp.where(core == 0, mine, got)
        right = jnp.where(core == 0, got, mine)
        return jnp.concatenate([left, right], axis=1).astype(f32)

    def finish(reduction):
        while reduction.left:
            reduction.advance().receive()
        parts = [
            jnp.concatenate([v[0] for v in values], axis=1)
            for values in (reduction.kept, reduction.got)
        ]
        return whole(*own_and_other(parts, (0, core), kernels))

    squares = dict(zip(SQUARES, full[2][:8]))
    w_cond_full, w_time1_full, small = full[2][8:]
    w_time2_full = squares["time2"]
    small = small.reshape(world, -1)
    w_input_full, w_output_t, head_gain_f, head_bias = spread(
        small, [(CHANNELS, k_w), (CHANNELS, k_w), (1, k_w), (12, k_w)]
    )
    w_input_full, w_output_t = w_input_full.astype(bf16), w_output_t.astype(bf16)

    row_slot = ids + IMAGES * jnp.arange(micros, dtype=jnp.int32)[:, None]
    row_slot = jnp.where(ids >= 0, row_slot, -1).reshape(total, 1)
    step_vals = timesteps[:, 0, 0].reshape(micros * IMAGES).astype(f32)
    sinusoid_in = sinusoid(step_vals).astype(bf16)
    time_one = product(sinusoid_in, w_time1_full) + head_bias[1]
    time_act = jax.nn.silu(time_one).astype(bf16)
    embedded = product(time_act, w_time2_full) + head_bias[2]
    factors = plan(step_vals)
    slots = jnp.arange(micros * IMAGES, dtype=jnp.int32)[None, :]
    mixing = [
        jnp.sum(jnp.where(row_slot == slots, factors[None, :, i], 0.0), axis=1, keepdims=True)
        for i in range(2)
    ]
    noisy = (latent_rows * mixing[0] + noise_rows * mixing[1]).astype(bf16)
    values = (condition, noisy, noise_rows, row_slot)
    out_bias = output_bias.astype(f32)[None]
    if kernels:
        out, sums = head_kernel(
            head_pack,
            w_cond_full,
            w_input_full,
            w_output_t,
            head_bias,
            head_gain_f,
            out_bias,
            embedded,
            values,
            k_w,
        )
    else:
        others = {"cond": w_cond_full, "input": w_input_full, "output": w_output_t, **squares}
        out, sums = head_step(
            others.get,
            lambda i: head_bias[i : i + 1],
            head_gain_f,
            out_bias,
            embedded,
            values,
        )
        sums = [jnp.pad(sums[n], ((0, 0), (0, WIDTH - sums[n].shape[1]))) for n, _ in HEAD_SUMS]
        sums = jnp.concatenate(sums)
        sums = jnp.pad(sums, ((0, -sums.shape[0] % 8), (0, 0)))
    chunks = out["condition"].reshape(micros, copy_size, own, D)
    chunks = [chunks[:, j] for j in range(copy_size)]
    at_embedded = 2 * CHANNELS
    grad_embedded = sums[at_embedded : at_embedded + micros * IMAGES].astype(bf16)
    grad_time_one = (input_back(grad_embedded, w_time2_full) * silu_slope(time_one)).astype(bf16)
    arriving = [shift_copy(chunks[j], copy_size, j) for j in range(1, copy_size)]
    (gated,) = after(chunks, out["gated"])
    send, keep, sums_one = pack_head_grads(
        [
            (gated, out["fshift"]),
            (gated, out["fscale"]),
            (out["inner_act"], out["two"]),
            (out["mlp_in"], out["one"]),
        ],
        core,
        dp_size,
        copy_size,
        kernels,
    )
    pack_one = Reduction([send], [keep], 2 * k_w, dp_size, kernels)
    arriving = after([keep], *arriving)
    grad_z_own = sum_low([chunks[0], *arriving], kernels)
    arriving = [shift_copy(grad_z_own, copy_size, copy_size - j) for j in range(1, copy_size)]
    send_after(pack_one, [grad_z_own])
    (gated,) = after([grad_z_own], gated)
    of_head = 2 * CHANNELS + 8
    send, keep, small_grads = pack_head_grads(
        [
            (gated, out["shift"]),
            (gated, out["scale"]),
            (gated, out["gate"]),
            (time_act, grad_embedded),
            (condition, out["cond"]),
            (sinusoid_in, grad_time_one),
        ],
        core,
        dp_size,
        copy_size,
        kernels,
        (sums_one, sums),
        (
            (2, 0, 2 * CHANNELS),
            (2, of_head, 1),
            (0, 4, 2),
            (0, 3, 1),
            (2, of_head + 1, 2),
            (1, 3, 1),
            (1, 2, 1),
            (0, 0, 3),
            (1, 0, 2),
            (2, of_head + 3, 1),
            (2, of_head + 4, 2),
        ),
    )
    pack_two = Reduction([send], [keep], 3 * k_w, dp_size, kernels)
    formed = form_after(pack_one, [keep])
    arriving = after(formed, *arriving)
    send_after(pack_one, arriving)
    send_after(pack_two, arriving)

    def swap_copies(values, shift, first):
        return values + after(first, swap_copy(values, copy_size, shift))[0]

    send, keep, grad_middle, grad_branch, grad_mixed, block_sums, hidden_sums = block_back_one(
        [grad_z_own, *arriving],
        slope,
        full[1][:4],
        w_down_full,
        w_proj_full,
        (second_z, active_z),
        norm_two,
        inv_two,
        gains[1:2],
        core,
        dp_size,
        kernels,
    )
    sent, kept = [send], [keep]
    small_grads = swap_copies(small_grads, 1, [grad_mixed])
    formed = form_after(pack_two, [small_grads])
    send_after(pack_two, formed)
    formed = form_after(pack_one, formed)
    send_after(pack_one, formed)
    (grad_mixed,) = after(formed, grad_mixed)
    back = None
    for m in range(micros):
        back = attention_back(queries, key_rows, value_rows, grad_mixed, ids, m, back)
    small_grads = swap_copies(small_grads, 2, back)
    formed = form_after(pack_two, [small_grads])
    send_after(pack_two, formed)
    one_parts = to_copies(pack_one, formed)
    back = after([one_parts[0]], *back)
    send, keep, input_grad, block_small = block_back_two(
        back,
        (w_q, w_k, w_v),
        (first_z, mixed_z),
        grad_branch,
        grad_middle,
        norm_one,
        inv_one,
        gains[:1],
        block_sums,
        hidden_sums,
        own,
        micros,
        core,
        dp_size,
        kernels,
    )
    one_parts = after([keep], *one_parts)
    own_one_parts = own_and_other(one_parts, (place, core), kernels)
    sent, kept = sent + [send], kept + [keep]
    pack_three = Reduction(sent, kept, 6 * k_d, dp_size, kernels)
    send_after(pack_three, own_one_parts)
    head_rows = small_grads.shape[0]
    block_small = jnp.pad(block_small, ((0, -block_small.shape[0] % 8), (0, WIDTH - D)))
    small_grads = jnp.concatenate([small_grads, block_small], axis=0)
    everywhere = lax.all_gather(small_grads, "dp", axis=0)
    small_grads = everywhere[0]
    for n in range(1, dp_size):
        small_grads = small_grads + everywhere[n]
    block_small = small_grads[head_rows:, :D]
    formed = form_after(pack_three, own_one_parts)
    send_after(pack_three, formed)
    two_parts = to_copies(pack_two, formed)
    while pack_three.left:
        formed = form_after(pack_three, [two_parts[0]])
        send_after(pack_three, formed)
    two_parts = after(formed, *two_parts)
    own_two_parts = own_and_other(two_parts, (place, core), kernels)
    own_all = finish(pack_three)
    own_up = jnp.concatenate(split_pack(own_all, [k_d] * 4), axis=1)
    own_down = own_all[4 * k_d : 4 * k_d + k_ff]
    own_four = own_all[4 * k_d + k_ff :]
    own_q, own_k, own_v, own_proj = split_pack(own_four, [k_d] * 4)
    own_fshift, own_fscale, own_two, own_one = split_pack(
        whole(*own_one_parts), [k_w] * 4
    )
    own_shift, own_scale, own_gate, own_time2, own_cond, own_time1 = split_pack(
        whole(*own_two_parts), [k_w] * 4 + [k_d, k_t]
    )
    me = lax.axis_index("dp") * copy_size + place
    own_rest = lax.dynamic_slice_in_dim(block_small[:8], me * k_d, k_d, 1)
    own_gains, own_biases = own_rest[:2], own_rest[2:]
    own_up_bias = lax.dynamic_slice_in_dim(block_small[8 : 8 + ff // D].reshape(ff), me * k_ff, k_ff)
    own_small = lax.dynamic_slice_in_dim(small_grads, me * k_w, k_w, 1)
    own_w_input = own_small[:CHANNELS]
    own_w_output = own_small[CHANNELS : 2 * CHANNELS].T
    own_head_gain = own_small[2 * CHANNELS]
    own_head_biases = own_small[2 * CHANNELS + 1 : 2 * CHANNELS + 13]
    grad_out_bias = small_grads[2 * CHANNELS + 13, :CHANNELS]

    input_grad = input_grad.reshape(micros, 1, own, D)
    block_output = condition.reshape(micros, length, D)[:, :own].reshape(micros, 1, own, D)
    return (
        block_output,
        input_grad,
        own_gains,
        own_biases,
        jnp.concatenate([own_q, own_k, own_v], axis=1),
        own_proj,
        own_up,
        own_up_bias,
        own_down,
        own_head_gain,
        own_head_biases,
        own_cond,
        own_time1,
        own_time2,
        own_w_input,
        jnp.concatenate([own_shift, own_scale, own_gate], axis=1),
        own_one,
        own_two,
        jnp.concatenate([own_fshift, own_fscale], axis=1),
        own_w_output,
        grad_out_bias,
    )


def solution(mesh):
    in_specs = (
        P(None, "dp", "copy", None),
        P(None, "dp", None),
        P(None, "dp", None, None),
        P(None, "copy", "dp", None, None),
        P(None, "copy", "dp", None),
        P(None, ("dp", "copy")),
        P(None, ("dp", "copy")),
        P(("dp", "copy"), None),
        P(("dp", "copy"), None),
        P(("dp", "copy"), None),
        P(("dp", "copy")),
        P(("dp", "copy"), None),
        P(("dp", "copy")),
        P(None, ("dp", "copy")),
        P(("dp", "copy"), None),
        P(("dp", "copy"), None),
        P(("dp", "copy"), None),
        P(None, ("dp", "copy")),
        P(("dp", "copy"), None),
        P(("dp", "copy"), None),
        P(("dp", "copy"), None),
        P(("dp", "copy"), None),
        P(("dp", "copy"), None),
        P(),
    )
    out_specs = (
        P(None, "dp", "copy", None),
        P(None, "dp", "copy", None),
        P(None, ("dp", "copy")),
        P(None, ("dp", "copy")),
        P(("dp", "copy"), None),
        P(("dp", "copy"), None),
        P(("dp", "copy"), None),
        P(("dp", "copy")),
        P(("dp", "copy"), None),
        P(("dp", "copy")),
        P(None, ("dp", "copy")),
        P(("dp", "copy"), None),
        P(("dp", "copy"), None),
        P(("dp", "copy"), None),
        P(None, ("dp", "copy")),
        P(("dp", "copy"), None),
        P(("dp", "copy"), None),
        P(("dp", "copy"), None),
        P(("dp", "copy"), None),
        P(("dp", "copy"), None),
        P(),
    )
    return jax.shard_map(shards, mesh=mesh, in_specs=in_specs, out_specs=out_specs, check_vma=False)
```

```python
import functools
import math

import jax
import jax.numpy as jnp
from jax import lax
from jax.experimental import pallas as pl
from jax.experimental.pallas import tpu as pltpu
from jax.sharding import PartitionSpec as P

D = 768
HEADS = 12
HEAD_DIM = 64
WIDTH = 1024
FREQ = 256
CHANNELS = 16
IMAGES = 4


epsilon = 1e-06
highest = lax.Precision.HIGHEST


def product(left_side, right_side):
    return jnp.dot(left_side, right_side, preferred_element_type=jnp.float32)


def weight_grad(left_side, right_side):
    return lax.dot_general(
        left_side, right_side, (((0,), (0,)), ((), ())), preferred_element_type=jnp.float32
    )


def input_back(gradient, weight):
    return lax.dot_general(
        gradient, weight, (((1,), (1,)), ((), ())), preferred_element_type=jnp.float32
    )


def column_sum(values):
    return jnp.sum(values.astype(jnp.float32), axis=0)


def normalize(values):
    center = values - jnp.mean(values, axis=-1, keepdims=True)
    inverse = lax.rsqrt(jnp.mean(center * center, axis=-1, keepdims=True) + epsilon)
    return (center * inverse, inverse)


def norm_back(gradient, normed, inverse):
    return inverse * (
        gradient
        - jnp.mean(gradient, axis=-1, keepdims=True)
        - normed * jnp.mean(gradient * normed, axis=-1, keepdims=True)
    )


def silu_slope(values):
    sigma = jax.nn.sigmoid(values)
    return sigma * (1.0 + values * (1.0 - sigma))


def gelu_slope(values):
    return 0.5 * (1.0 + lax.erf(values * 2.0 ** (-0.5))) + values * jnp.exp(
        -0.5 * values * values
    ) * (2.0 * math.pi) ** (-0.5)


def sinusoid(step_vals):
    half_width = FREQ // 2
    rates = jnp.exp(-math.log(10000.0) * jnp.arange(half_width, dtype=jnp.float32) / half_width)
    angles = step_vals[:, None] * rates[None, :]
    return jnp.concatenate([jnp.cos(angles), jnp.sin(angles)], axis=1)


def plan(step_vals):
    anchor = math.cos(0.008 / 1.008 * math.pi / 2.0) ** 2
    angle_now = ((step_vals + 1.0) / 1000.0 + 0.008) / 1.008 * (math.pi / 2.0)
    signal = jnp.cos(angle_now) ** 2 / anchor
    return jnp.stack([jnp.sqrt(signal), jnp.sqrt(1.0 - signal)], axis=1)


def tdot(left_side, right_side):
    return lax.dot_general(
        left_side, right_side, (((0,), (0,)), ((), ())), preferred_element_type=jnp.float32
    )


def swap_bit(values, size, bit):
    return lax.ppermute(values, "dp", [(i, i ^ (1 << bit)) for i in range(size)])


def shift_copy(values, size, shift):
    return lax.ppermute(values, "copy", [(i, (i + shift) % size) for i in range(size)])


def swap_copy(values, size, shift):
    return lax.ppermute(values, "copy", [(i, i ^ shift) for i in range(size)])


def pick(values, index, axis):
    return lax.dynamic_index_in_dim(values, index, axis, keepdims=False)


def tie(*values):
    return lax.optimization_barrier(values)


MIB = 1 << 20


def cost(microseconds):
    return pl.CostEstimate(
        flops=int(microseconds * 10**9), bytes_accessed=10**5, transcendentals=0
    )


def dot0(left_side, right_side):
    return lax.dot_general(
        left_side, right_side, (((0,), (0,)), ((), ())), preferred_element_type=jnp.float32
    )


def dot1(left_side, right_side):
    return lax.dot_general(
        left_side, right_side, (((1,), (1,)), ((), ())), preferred_element_type=jnp.float32
    )


def small_call(body, outs, scalars, ins):
    size = sum(math.prod(o.shape) * o.dtype.itemsize for o in outs)
    size += sum(math.prod(v.shape) * v.dtype.itemsize for v in ins)
    return pl.pallas_call(
        body,
        out_shape=outs,
        in_specs=[pl.BlockSpec(memory_space=pltpu.SMEM)]
        + [pl.BlockSpec(memory_space=pltpu.VMEM)] * len(ins),
        out_specs=[pl.BlockSpec(memory_space=pltpu.VMEM)] * len(outs),
        compiler_params=pltpu.CompilerParams(vmem_limit_bytes=60 * MIB),
        cost_estimate=cost(size / 2.2e6),
    )(jnp.stack([jnp.asarray(v, jnp.int32) for v in scalars]), *ins)


def low_shape(*dims):
    return jax.ShapeDtypeStruct(dims, jnp.bfloat16)


def add_up(one, two):
    return one.astype(jnp.float32) + two.astype(jnp.float32)


def cut_first(keeps, gots, rows, bits, kernels):
    count, mids, _, width = keeps[0].shape
    half = count // 2
    sizes = [k.shape[2] for k in keeps]
    total = sum(sizes)

    if not kernels:
        sums = jnp.concatenate([add_up(k, g) for k, g in zip(keeps, gots)], axis=2)
        sums = sums.astype(jnp.bfloat16)
        first = sums[:, :, :rows].reshape(2, half, mids, rows, width)
        second = sums[:, :, rows:].reshape(half, 2, mids, total - rows, width)
        return [
            pick(first, 1 - bits[0], 0),
            pick(first, bits[0], 0),
            pick(second, 1 - bits[1], 1),
            pick(second, bits[1], 1),
        ]

    def body(at, *refs):
        keep_refs, got_refs = refs[: len(keeps)], refs[len(keeps) : 2 * len(keeps)]
        outs = refs[2 * len(keeps) :]
        for out, bit, low in zip(outs, (1 - at[0], at[0], 1 - at[1], at[1]), (0, 0, 1, 1)):
            begin, end = (rows, total) if low else (0, rows)
            at_row = 0
            for keep, got, n in zip(keep_refs, got_refs, sizes):
                top, bottom = max(begin, at_row), min(end, at_row + n)
                if top < bottom:
                    cut = pl.ds(top - at_row, bottom - top)
                    for i in range(half):
                        p = 2 * i + bit if low else bit * half + i
                        value = add_up(keep[p, :, cut], got[p, :, cut]).astype(jnp.bfloat16)
                        out[i, :, top - begin : bottom - begin] = value
                at_row += n

    outs = [low_shape(half, mids, n, width) for n in (rows, rows, total - rows, total - rows)]
    return small_call(body, outs, bits, [*keeps, *gots])


def cut_next(keeps, gots, bits, kernels):
    count, mids, _, width = keeps[0].shape
    half = count // 2
    sizes = [k.shape[2] for k in keeps]
    if not kernels:
        sums = [add_up(k, g).astype(jnp.bfloat16) for k, g in zip(keeps, gots)]
        first = sums[0].reshape(2, half, mids, sizes[0], width)
        second = sums[1].reshape(half, 2, mids, sizes[1], width)
        return [
            pick(first, 1 - bits[0], 0),
            pick(first, bits[0], 0),
            pick(second, 1 - bits[1], 1),
            pick(second, bits[1], 1),
        ]

    def body(at, keep_one, got_one, keep_two, got_two, *outs):
        for out, bit, top in zip(outs, (1 - at[0], at[0], 1 - at[1], at[1]), (0, 0, 1, 1)):
            keep, got = (keep_two, got_two) if top else (keep_one, got_one)
            for i in range(half):
                p = 2 * i + bit if top else bit * half + i
                out[i] = add_up(keep[p], got[p]).astype(jnp.bfloat16)

    outs = [low_shape(half, mids, n, width) for n in (sizes[0], sizes[0], sizes[1], sizes[1])]
    return small_call(body, outs, bits, [keeps[0], gots[0], keeps[1], gots[1]])


def cut_copies(keeps, gots, place, copy_size, kernels):
    _, mids, _, width = keeps[0].shape
    sizes = [k.shape[2] for k in keeps]
    total = sum(sizes)
    if not kernels:
        sums = jnp.concatenate([add_up(k, g)[0] for k, g in zip(keeps, gots)], axis=1)
        sums = sums.astype(jnp.bfloat16).reshape(2, copy_size, total, width)
        return [pick(sums, lax.rem(place + j, copy_size), 1) for j in range(copy_size)]

    def body(at, keep_one, got_one, keep_two, got_two, *outs):
        for j in range(copy_size):
            z = lax.rem(at[0] + j, copy_size)
            for c in range(2):
                m = c * copy_size + z
                top = add_up(keep_one[0, m], got_one[0, m]).astype(jnp.bfloat16)
                low = add_up(keep_two[0, m], got_two[0, m]).astype(jnp.bfloat16)
                outs[j][c, : sizes[0]] = top
                outs[j][c, sizes[0] :] = low

    outs = [low_shape(2, total, width)] * copy_size
    return small_call(body, outs, [place], [keeps[0], gots[0], keeps[1], gots[1]])


def sum_low(parts, kernels):
    if not kernels:
        return sum(p.astype(jnp.float32) for p in parts).astype(jnp.bfloat16)

    def body(at, *refs):
        total = refs[0][...].astype(jnp.float32)
        for ref in refs[1:-1]:
            total = total + ref[...].astype(jnp.float32)
        refs[-1][...] = total.astype(jnp.bfloat16)

    return small_call(body, [low_shape(*parts[0].shape)], [0], parts)[0]


def cut_copy_halves(keeps, gots, place, copy_size, kernels):
    _, mids, _, width = keeps[0].shape
    sizes = [k.shape[2] for k in keeps]
    total, half = sum(sizes), copy_size // 2
    if not kernels:
        sums = jnp.concatenate([add_up(k, g)[0] for k, g in zip(keeps, gots)], axis=1)
        sums = sums.astype(jnp.bfloat16).reshape(2, 2, half, total, width)
        top = place // half
        return [pick(sums, 1 - top, 1), pick(sums, top, 1)]

    def body(at, keep_one, got_one, keep_two, got_two, *outs):
        top = at[0] // half
        for out, bit in zip(outs, (1 - top, top)):
            for c in range(2):
                for j in range(half):
                    m = c * copy_size + bit * half + j
                    first = add_up(keep_one[0, m], got_one[0, m]).astype(jnp.bfloat16)
                    second = add_up(keep_two[0, m], got_two[0, m]).astype(jnp.bfloat16)
                    out[c, j, : sizes[0]] = first
                    out[c, j, sizes[0] :] = second

    outs = [low_shape(2, half, total, width)] * 2
    return small_call(body, outs, [place], [keeps[0], gots[0], keeps[1], gots[1]])


def cut_copy_last(keep, got, place, kernels):
    if not kernels:
        sums = add_up(keep, got).astype(jnp.bfloat16)
        return [pick(sums, 1 - place % 2, 1), pick(sums, place % 2, 1)]

    def body(at, keep_ref, got_ref, *outs):
        low = lax.rem(at[0], 2)
        for out, bit in zip(outs, (1 - low, low)):
            for c in range(2):
                out[c] = add_up(keep_ref[c, bit], got_ref[c, bit]).astype(jnp.bfloat16)

    return small_call(body, [low_shape(2, *keep.shape[2:])] * 2, [place], [keep, got])


def own_and_other(parts, scalars, kernels):
    place, core = scalars
    count = len(parts)
    _, total, width = parts[0].shape
    if not kernels:
        stacked = jnp.stack(parts).astype(jnp.float32)
        sums = 0.0
        for i in range(count):
            sums = sums + pick(stacked, lax.rem(place + count - i, count), 0)
        sums = sums.astype(jnp.bfloat16)
        return [pick(sums, 1 - core, 0), pick(sums, core, 0)]

    def body(at, *refs):
        for out, c in zip(refs[count:], (1 - at[1], at[1])):
            values = [r[c].astype(jnp.float32) for r in refs[:count]]
            sums = None
            for i in range(count):
                turn = lax.rem(at[0] + count - i, count)
                value = values[0]
                for j in range(1, count):
                    value = jnp.where(turn == j, values[j], value)
                sums = value if sums is None else sums + value
            out[...] = sums.astype(jnp.bfloat16)

    return small_call(body, [low_shape(total, width)] * 2, scalars, parts)


class Reduction:
    def __init__(self, sent, kept, rows, size, kernels):
        self.size, self.rows, self.kernels = size, rows, kernels
        self.left = size.bit_length() - 2
        self.me = lax.axis_index("dp")
        self.sent, self.kept, self.bits = list(sent), list(kept), [0] * len(sent)
        self.first = True

    def receive(self):
        self.got = [swap_bit(v, self.size, bit) for v, bit in zip(self.sent, self.bits)]
        return self

    def advance(self):
        if self.first:
            self.bits = [self.left, 1]
            bits = [(self.me >> b) & 1 for b in self.bits]
            cuts = cut_first(self.kept, self.got, self.rows, bits, self.kernels)
        else:
            self.bits = [self.bits[0] - 1, self.bits[1] + 1]
            bits = [(self.me >> b) & 1 for b in self.bits]
            cuts = cut_next(self.kept, self.got, bits, self.kernels)
        self.first = False
        self.left -= 1
        self.sent, self.kept = [cuts[0], cuts[2]], [cuts[1], cuts[3]]
        return self


def attend(ids_col, ids_row, q, k, lanes, head, scale):
    wanted = (lanes >= HEAD_DIM) if head else (lanes < HEAD_DIM)
    scores = dot1(jnp.where(wanted, q, 0), k) * scale
    scores = jnp.where(ids_col == ids_row, scores, -1e30)
    exps = jnp.exp(scores - jnp.max(scores, axis=-1, keepdims=True))
    return wanted, exps / jnp.sum(exps, axis=-1, keepdims=True)


def attention_specs(micros, length, first=0):
    wide = pl.BlockSpec((length, 2 * HEAD_DIM), lambda m, h: (m + first, h))
    col = pl.BlockSpec((length, 1), lambda m, h: (m + first, 0))
    row = pl.BlockSpec((1, 1, length), lambda m, h: (m + first, 0, 0))
    return wide, col, row


def attention(queries, key_rows, value_rows, ids):
    micros, length = ids.shape
    scale = HEAD_DIM ** (-0.5)
    wide, col, row = attention_specs(micros, length)

    def body(col_ref, row_ref, q_ref, k_ref, v_ref, out_ref):
        lanes = lax.broadcasted_iota(jnp.int32, (1, 2 * HEAD_DIM), 1)
        outs = []
        for head in range(2):
            _, probs = attend(
                col_ref[...], row_ref[0], q_ref[...], k_ref[...], lanes, head, scale
            )
            outs.append(
                jnp.dot(
                    probs.astype(jnp.bfloat16), v_ref[...], preferred_element_type=jnp.float32
                )
            )
        out_ref[...] = jnp.where(lanes < HEAD_DIM, outs[0], outs[1]).astype(jnp.bfloat16)

    return pl.pallas_call(
        body,
        grid=(micros, HEADS // 2),
        out_shape=low_shape(micros * length, D),
        in_specs=[col, row, wide, wide, wide],
        out_specs=wide,
        compiler_params=pltpu.CompilerParams(vmem_limit_bytes=24 * MIB),
        cost_estimate=cost(15.0),
    )(ids.reshape(-1, 1), ids[:, None], queries, key_rows, value_rows)


def attention_back(queries, key_rows, value_rows, grad_mixed, ids, which, before):
    micros, length = ids.shape
    scale = HEAD_DIM ** (-0.5)
    wide, col, row = attention_specs(micros, length, which)

    def body(col_ref, row_ref, q_ref, k_ref, v_ref, g_ref, *outs):
        lanes = lax.broadcasted_iota(jnp.int32, (1, 2 * HEAD_DIM), 1)
        q, k, v, g = q_ref[...], k_ref[...], v_ref[...], g_ref[...]
        parts = []
        for head in range(2):
            wanted, probs = attend(col_ref[...], row_ref[0], q, k, lanes, head, scale)
            grad_probs = dot1(jnp.where(wanted, g, 0), v)
            delta = jnp.sum(grad_probs * probs, axis=-1, keepdims=True)
            grad_scores = (probs * (grad_probs - delta)).astype(jnp.bfloat16)
            parts.append(
                (
                    jnp.dot(grad_scores, k, preferred_element_type=jnp.float32) * scale,
                    dot0(grad_scores, q) * scale,
                    dot0(probs.astype(jnp.bfloat16), g),
                )
            )
        for out, one, two in zip(outs[-3:], *parts):
            out[...] = jnp.where(lanes < HEAD_DIM, one, two).astype(jnp.bfloat16)

    return pl.pallas_call(
        body,
        grid=(1, HEADS // 2),
        out_shape=[low_shape(micros * length, D)] * 3,
        in_specs=[col, row, wide, wide, wide, wide]
        + [pl.BlockSpec(memory_space=pl.ANY)] * len(before or ()),
        out_specs=[wide] * 3,
        input_output_aliases={6 + i: i for i in range(len(before or ()))},
        compiler_params=pltpu.CompilerParams(vmem_limit_bytes=60 * MIB),
        cost_estimate=cost(12.0),
    )(ids.reshape(-1, 1), ids[:, None], queries, key_rows, value_rows, grad_mixed, *(before or ()))


def pack_head_grads(pairs, core, dp_size, copy_size, kernels, others=(), plan=None):
    world = dp_size * copy_size
    count, mids = dp_size // 2, 2 * copy_size
    width = pairs[0][1].shape[1]
    half = width // 2
    sizes = [p[0].shape[1] // world for p in pairs]
    total = sum(sizes)
    if not kernels:
        packs = []
        for c in (1 - core, core):
            parts = []
            for left_side, right_side in pairs:
                part = lax.dynamic_slice_in_dim(right_side, c * half, half, 1)
                part = weight_grad(left_side, part).astype(jnp.bfloat16)
                parts.append(part.reshape(count, mids, -1, half))
            packs.append(jnp.concatenate(parts, axis=2))
        given = [jnp.stack([column_sum(p[1]) for p in pairs]), *others]
        if plan is None:
            return packs + given
        return packs + [jnp.concatenate([given[i][at : at + n] for i, at, n in plan])]

    lefts, which = [], []
    for left_side, _ in pairs:
        seen = [i for i, other in enumerate(lefts) if other is left_side]
        which.append(seen[0] if seen else len(lefts))
        lefts += [] if seen else [left_side]
    rights = [p[1] for p in pairs]
    narrow = [v.shape[1] // count % 128 == 0 for v in lefts]
    held = [i for i, w in enumerate(which) if not narrow[w]]

    where, height = list(range(len(pairs))), len(pairs)
    if plan is not None:
        at_row = 0
        for source, row, n in plan:
            if not source:
                where[row : row + n] = range(at_row, at_row + n)
            at_row += n
        height = at_row

    def body(at, *refs):
        left_refs = refs[: len(lefts)]
        right_refs = refs[len(lefts) : len(lefts) + len(rights)]
        other_refs, refs = refs[len(lefts) + len(rights) :][: len(others)], refs[len(others) :]
        sent, kept, sums = refs[len(lefts) + len(rights) :][:3]
        scratch = refs[len(lefts) + len(rights) + 3 :]
        first = at[0] == 0
        step = pl.program_id(0)

        @pl.when(step == 0)
        def _():
            for i, right in enumerate(right_refs):
                ones = jnp.ones((8, right.shape[0]), jnp.bfloat16)
                row = jnp.dot(ones, right[...], preferred_element_type=jnp.float32)
                sums[where[i] : where[i] + 1] = row[:1]
            at = 0
            for source, row, n in plan or ():
                if source:
                    sums[at : at + n] = other_refs[source - 1][row : row + n]
                at += n
            for i, buffer in zip(held, scratch):
                buffer[...] = dot0(left_refs[which[i]][...], right_refs[i][...])

        at_row = 0
        for i, n in enumerate(sizes):
            if i in held:
                rows = mids * n
                whole = scratch[held.index(i)][pl.ds(pl.multiple_of(step * rows, 8), rows)]
            else:
                whole = dot0(left_refs[which[i]][...], right_refs[i][...])
            left, right = whole[:, :half], whole[:, half:]
            for out, part in (
                (sent, jnp.where(first, right, left)),
                (kept, jnp.where(first, left, right)),
            ):
                out[0, :, at_row : at_row + n] = part.reshape(mids, n, half).astype(jnp.bfloat16)
            at_row += n

    in_specs = [pl.BlockSpec(memory_space=pltpu.SMEM)]
    for v, cut_up in zip(lefts, narrow):
        if cut_up:
            in_specs.append(pl.BlockSpec((v.shape[0], v.shape[1] // count), lambda p: (0, p)))
        else:
            in_specs.append(pl.BlockSpec(v.shape, lambda p: (0, 0)))
    in_specs += [pl.BlockSpec(v.shape, lambda p: (0, 0)) for v in [*rights, *others]]
    out_spec = pl.BlockSpec((1, mids, total, half), lambda p: (p, 0, 0, 0))
    return pl.pallas_call(
        body,
        grid=(count,),
        out_shape=[low_shape(count, mids, total, half)] * 2
        + [jax.ShapeDtypeStruct((height, width), jnp.float32)],
        in_specs=in_specs,
        out_specs=[out_spec] * 2 + [pl.BlockSpec((height, width), lambda p: (0, 0))],
        scratch_shapes=[
            pltpu.VMEM((lefts[which[i]].shape[1], width), jnp.float32) for i in held
        ],
        compiler_params=pltpu.CompilerParams(vmem_limit_bytes=60 * MIB),
        cost_estimate=cost(13.0),
    )(jnp.asarray(core, jnp.int32)[None], *lefts, *rights, *others)


def assemble(pieces, scalars, copy_size, rows):
    width = pieces[0][0].shape[-1]
    total = rows

    def body(at, *refs):
        ins, out, sems = refs[: len(pieces)], refs[len(pieces)], refs[len(pieces) + 1]
        copies = []
        for ref, (value, first, flip, vary) in zip(ins, pieces):
            for d in range(2):
                for j in range(copy_size):
                    dp = at[0] ^ (flip | (vary if d else 0))
                    owner = dp * copy_size + lax.rem(at[1] + j, copy_size)
                    copy = pltpu.make_async_copy(
                        ref.at[d, j],
                        out.at[owner, pl.ds(first, value.shape[2])],
                        sems.at[len(copies)],
                    )
                    copy.start()
                    copies.append(copy)
        for copy in copies:
            copy.wait()

    return pl.pallas_call(
        body,
        out_shape=low_shape(8 * copy_size, total, width),
        in_specs=[pl.BlockSpec(memory_space=pltpu.SMEM)]
        + [pl.BlockSpec(memory_space=pl.ANY)] * len(pieces),
        out_specs=pl.BlockSpec(memory_space=pl.ANY),
        scratch_shapes=[pltpu.SemaphoreType.DMA((len(pieces) * 2 * copy_size,))],
        compiler_params=pltpu.CompilerParams(vmem_limit_bytes=4 * MIB),
        cost_estimate=cost(8.0),
    )(jnp.stack([jnp.asarray(v, jnp.int32) for v in scalars]), *[p[0] for p in pieces])


def gather(pack, rows, arrived):
    total = pack.shape[0]
    along = [pack, *arrived]
    pieces = []
    for first, last, bits in ((0, rows, (2, 1)), (rows, total, (1, 2))):
        held = jnp.stack([v[first:last] for v in along])
        held = jnp.stack([held, swap_bit(held, 8, bits[0])])
        got = swap_bit(held, 8, bits[1])
        vary = 1 << bits[0]
        other = 1 << bits[1]
        pieces += [(held, first, 0, vary), (got, first, other, vary)]
        pieces += [
            (swap_bit(held, 8, 0), first, 1, vary),
            (swap_bit(got, 8, 0), first, other | 1, vary),
        ]
    return assemble(pieces, (lax.axis_index("dp"), lax.axis_index("copy")), 4, total)


LANES = 128


def padded_lanes(values):
    return jnp.pad(values, ((0, 0), (0, LANES - values.shape[1]))).reshape(-1)


def lay(ins, shape, plan, vectors):
    height, width = shape
    start = max(p[5] + p[3] for p in plan)

    def body(*refs):
        out = refs[-1]
        for which, row, column, rows, columns, there in plan:
            out[there : there + rows] = refs[which][row : row + rows, column : column + columns]
        values = []
        for which, turned in vectors:
            value = refs[which][...].astype(jnp.float32)
            value = value.T if turned else value
            values += [value[i : i + 1] for i in range(value.shape[0])]
        zero = jnp.zeros((1, LANES), jnp.float32)
        values = [
            jnp.concatenate([v, zero[:, : LANES - v.shape[1]]], axis=1) for v in values
        ]
        values += [zero] * ((height - start) * width // LANES - len(values))
        per = width // LANES
        lines = [
            jnp.concatenate(values[i : i + per], axis=1) for i in range(0, len(values), per)
        ]
        if lines:
            out[start:] = jnp.concatenate(lines, axis=0).astype(jnp.bfloat16)

    return pl.pallas_call(
        body,
        out_shape=low_shape(height, width),
        in_specs=[pl.BlockSpec(memory_space=pltpu.VMEM)] * len(ins),
        out_specs=pl.BlockSpec(memory_space=pltpu.VMEM),
        compiler_params=pltpu.CompilerParams(vmem_limit_bytes=16 * MIB),
        cost_estimate=cost(2.0),
    )(*ins)


def spread(packed, sizes):
    world = packed.shape[0]
    total = sum(count for count, _ in sizes)

    def body(packed_ref, *outs):
        at = 0
        for (count, k), out in zip(sizes, outs):
            width = world * k
            column = lax.broadcasted_iota(jnp.int32, (LANES, width), 1)
            row = lax.broadcasted_iota(jnp.int32, (LANES, width), 0)
            tile = (row == column % k).astype(jnp.bfloat16)
            owner = lax.broadcasted_iota(jnp.int32, (world, width), 0)
            own = owner == lax.broadcasted_iota(jnp.int32, (world, width), 1) // k
            for i in range(count):
                block = packed_ref[:, (at + i) * LANES : (at + i + 1) * LANES]
                values = jnp.dot(block, tile, preferred_element_type=jnp.float32)
                out[i : i + 1] = jnp.sum(jnp.where(own, values, 0.0), axis=0, keepdims=True)
            at += count

    return pl.pallas_call(
        body,
        out_shape=[
            jax.ShapeDtypeStruct((count, world * k), jnp.float32) for count, k in sizes
        ],
        in_specs=[pl.BlockSpec(memory_space=pltpu.VMEM)],
        out_specs=[pl.BlockSpec(memory_space=pltpu.VMEM)] * len(sizes),
        compiler_params=pltpu.CompilerParams(vmem_limit_bytes=16 * MIB),
        cost_estimate=cost(0.7),
    )(packed[:, : total * LANES])


def head_step(weight, head_bias, gain, out_bias, embedded, values):
    bf16, f32 = jnp.bfloat16, jnp.float32
    condition, noisy, noise, slot = values
    out, sums = {}, {}
    valid = (slot >= 0).astype(f32)
    cond = product(condition, weight("cond")) + head_bias(0)
    chosen = jnp.zeros_like(cond)
    for i in range(embedded.shape[0]):
        chosen = jnp.where(slot == i, embedded[i : i + 1], chosen)
    cond = cond + chosen
    gated = jax.nn.silu(cond).astype(bf16)
    out["gated"] = gated
    entry = product(noisy, weight("input")) + head_bias(3)
    norm_head, inv_head = normalize(entry)
    affine = norm_head * gain + head_bias(4)
    shift = product(gated, weight("shift")) + head_bias(7)
    scale = product(gated, weight("scale")) + head_bias(8)
    mlp_in = (affine * (1.0 + scale) + shift).astype(bf16)
    out["mlp_in"] = mlp_in
    inner_one = product(mlp_in, weight("one")) + head_bias(5)
    inner_act = jax.nn.silu(inner_one).astype(bf16)
    out["inner_act"] = inner_act
    inner_two = product(inner_act, weight("two")) + head_bias(6)
    gate = product(gated, weight("gate")) + head_bias(9)
    residual = entry + gate * inner_two
    fshift = product(gated, weight("fshift")) + head_bias(10)
    fscale = product(gated, weight("fscale")) + head_bias(11)
    norm_final, inv_final = normalize(residual)
    final_in = (norm_final * (1.0 + fscale) + fshift).astype(bf16)
    predicted = input_back(final_in, weight("output")) + out_bias
    grad_pred = ((predicted - noise) * valid).astype(bf16)
    sums["output"] = weight_grad(grad_pred, final_in)
    sums["out_bias"] = jnp.sum(grad_pred.astype(f32), axis=0, keepdims=True)
    grad_final_in = product(grad_pred, weight("output"))
    out["fshift"] = grad_final_in.astype(bf16)
    out["fscale"] = (grad_final_in * norm_final).astype(bf16)
    grad_residual = norm_back(grad_final_in * (1.0 + fscale), norm_final, inv_final)
    out["two"] = (grad_residual * gate).astype(bf16)
    grad_one = input_back(out["two"], weight("two")) * silu_slope(inner_one)
    out["one"] = grad_one.astype(bf16)
    grad_mlp_in = input_back(out["one"], weight("one"))
    out["shift"] = grad_mlp_in.astype(bf16)
    out["scale"] = (grad_mlp_in * affine).astype(bf16)
    out["gate"] = (grad_residual * inner_two).astype(bf16)
    grad_gated = input_back(out["shift"], weight("shift"))
    for name in ("scale", "gate", "fshift", "fscale"):
        grad_gated = grad_gated + input_back(out[name], weight(name))
    grad_cond = grad_gated * silu_slope(cond)
    out["cond"] = grad_cond.astype(bf16)
    out["condition"] = input_back(out["cond"], weight("cond")).astype(bf16)
    grad_affine = grad_mlp_in * (1.0 + scale)
    grad_entry = grad_residual + norm_back(grad_affine * gain, norm_head, inv_head)
    grad_entry = grad_entry.astype(bf16)
    sums["input"] = weight_grad(noisy, grad_entry)
    sums["gain"] = jnp.sum(grad_affine * norm_head, axis=0, keepdims=True)
    sums["entry"] = jnp.sum(grad_entry.astype(f32), axis=0, keepdims=True)
    sums["affine"] = jnp.sum(grad_affine, axis=0, keepdims=True)
    lanes = lax.broadcasted_iota(jnp.int32, (slot.shape[0], embedded.shape[0]), 1)
    onehot = (slot == lanes).astype(bf16)
    low_part = (grad_cond - out["cond"].astype(f32)).astype(bf16)
    sums["embedded"] = weight_grad(onehot, out["cond"]) + weight_grad(onehot, low_part)
    return out, sums


SQUARES = ("shift", "scale", "gate", "time2", "one", "two", "fshift", "fscale")
HEAD_OUT = (
    "gated", "mlp_in", "inner_act", "fshift", "fscale", "two", "one", "shift", "scale", "gate",
    "cond", "condition",
)
HEAD_SUMS = (
    ("input", CHANNELS), ("output", CHANNELS), ("embedded", 8), ("gain", 1), ("entry", 1),
    ("affine", 1), ("out_bias", 1),
)


def head_kernel(pack, w_cond, w_input, w_output, head_bias, gain, out_bias, embedded, values, k):
    rows = values[0].shape[0]
    step = 256
    world = pack.shape[0]
    used = [i for i, name in enumerate(SQUARES) if name != "time2"]
    height = sum(n for _, n in HEAD_SUMS)
    height += -height % 8
    smalls = [w_cond, w_input, w_output, head_bias, gain, out_bias, embedded]

    def body(*refs):
        ins = refs[: len(smalls)]
        pack_ref = refs[len(smalls)]
        tiles = refs[len(smalls) + 1 :][:4]
        outs = refs[len(smalls) + 5 :][: len(HEAD_OUT)]
        sums_ref, buffer, sems = refs[len(smalls) + 5 + len(HEAD_OUT) :]
        first = pl.program_id(0) == 0

        def fetch(n):
            return pltpu.make_async_copy(
                pack_ref.at[:, pl.ds(used[n] * k, k)], buffer.at[n], sems.at[n]
            )

        @pl.when(first)
        def _():
            for n in range(len(used)):
                fetch(n).start()

        ready = set()

        def weight(name):
            if name in ("cond", "input", "output"):
                return ins[("cond", "input", "output").index(name)][...]
            n = used.index(SQUARES.index(name))
            if n not in ready:
                ready.add(n)

                @pl.when(first)
                def _():
                    fetch(n).wait()

            return buffer[n].reshape(WIDTH, WIDTH)

        out, sums = head_step(
            weight,
            lambda i: ins[3][i : i + 1],
            ins[4][...],
            ins[5][...],
            ins[6][...],
            [t[...] for t in tiles],
        )
        for name, ref in zip(HEAD_OUT, outs):
            ref[...] = out[name]

        @pl.when(first)
        def _():
            sums_ref[...] = jnp.zeros((height, WIDTH), jnp.float32)

        at = 0
        for name, n in HEAD_SUMS:
            width = sums[name].shape[1]
            sums_ref[at : at + n, :width] += sums[name]
            at += n

    def tall(width):
        return pl.BlockSpec((step, width), lambda i: (i, 0))

    widths = [D if name == "condition" else WIDTH for name in HEAD_OUT]
    *outs, sums = pl.pallas_call(
        body,
        grid=(rows // step,),
        out_shape=[low_shape(rows, w) for w in widths]
        + [jax.ShapeDtypeStruct((height, WIDTH), jnp.float32)],
        in_specs=[
            pl.BlockSpec(v.shape, lambda i: (0, 0), pipeline_mode=pl.Buffered(1)) for v in smalls
        ]
        + [pl.BlockSpec(memory_space=pl.ANY)]
        + [tall(v.shape[1]) for v in values],
        out_specs=[tall(w) for w in widths]
        + [pl.BlockSpec((height, WIDTH), lambda i: (0, 0))],
        scratch_shapes=[
            pltpu.VMEM((len(used), world, k, WIDTH), jnp.bfloat16),
            pltpu.SemaphoreType.DMA((len(used),)),
        ],
        compiler_params=pltpu.CompilerParams(vmem_limit_bytes=60 * MIB),
        cost_estimate=cost(45.0),
    )(*smalls, pack, *values)
    return dict(zip(HEAD_OUT, outs)), sums


def pack_block_grads(pairs, core, dp_size):
    count = dp_size // 2
    half = D // 2
    packs = []
    for c in (1 - core, core):
        parts = []
        for left_side, right_side in pairs:
            for at in range(0, right_side.shape[1], D):
                part = lax.dynamic_slice_in_dim(right_side, at + c * half, half, 1)
                part = weight_grad(left_side, part).astype(jnp.bfloat16)
                parts.append(part.reshape(count, 2, -1, half))
        packs.append(jnp.concatenate(parts, axis=2))
    return packs


def put_halves(first, sent, kept, at_row, whole):
    half = D // 2
    count = sent.shape[0]
    n = whole.shape[0] // (2 * count)
    left, right = whole[:, :half], whole[:, half:]
    for out, part in (
        (sent, jnp.where(first, right, left)),
        (kept, jnp.where(first, left, right)),
    ):
        part = part.reshape(count, 2, n, half).astype(jnp.bfloat16)
        out[:, :, at_row : at_row + n] = part


def feed_forward(second_in, middle, ups, up_bias, w_down, down_bias, place, copy_size, kernels):
    bf16, f32 = jnp.bfloat16, jnp.float32
    rows = middle.shape[0]
    steps = len(ups)

    def step_of(hidden):
        half = 0.5 * (1.0 + lax.erf(hidden * 2.0 ** (-0.5)))
        bell = jnp.exp(-0.5 * hidden * hidden) * (2.0 * math.pi) ** (-0.5)
        return (hidden * half).astype(bf16), (half + hidden * bell).astype(bf16)

    if not kernels:
        hidden = product(second_in, jnp.concatenate(ups, axis=1)) + up_bias
        active, slope = step_of(hidden)
        output = middle + product(active, w_down) + down_bias
        return output.astype(bf16), slope, None, active

    per = w_down.shape[0] // steps
    k = per // (2 * copy_size)
    width = per // copy_size

    def body(at, *refs):
        up_refs, refs = refs[:steps], refs[steps:]
        in_ref, middle_ref, bias_ref, down_ref, down_bias_ref = refs[:5]
        out_ref, slope_ref, chosen_ref, total, hidden = refs[5:]
        step = pl.program_id(0)
        for n in range(steps):

            @pl.when(step == n)
            def _():
                hidden[...] = product(in_ref[...], up_refs[n][...])

        active, slope = step_of(hidden[...] + bias_ref[...])
        slope_ref[...] = slope
        part = product(active, down_ref[...])
        source = lax.broadcasted_iota(jnp.int32, (per, width), 0)
        target = lax.broadcasted_iota(jnp.int32, (per, width), 1)
        wanted = (target // k * copy_size + at[0]) * k + target % k
        one_hot = (source == wanted).astype(bf16)
        chosen_ref[0] = product(active, one_hot).astype(bf16)

        @pl.when(step == 0)
        def _():
            total[...] = middle_ref[...] + down_bias_ref[...] + part

        @pl.when(step > 0)
        def _():
            total[...] += part

        @pl.when(step == steps - 1)
        def _():
            out_ref[...] = total[...].astype(bf16)

    def full(v):
        return pl.BlockSpec(v.shape, lambda j: (0,) * len(v.shape), pipeline_mode=pl.Buffered(1))

    out, slope, chosen = pl.pallas_call(
        body,
        grid=(steps,),
        out_shape=[low_shape(rows, D), low_shape(rows, per * steps), low_shape(steps, rows, width)],
        in_specs=[pl.BlockSpec(memory_space=pltpu.SMEM)]
        + [full(v) for v in (*ups, second_in, middle)]
        + [
            pl.BlockSpec((1, per), lambda j: (0, j)),
            pl.BlockSpec((per, D), lambda j: (j, 0)),
            full(down_bias),
        ],
        out_specs=[
            pl.BlockSpec((rows, D), lambda j: (0, 0)),
            pl.BlockSpec((rows, per), lambda j: (0, j)),
            pl.BlockSpec((1, rows, width), lambda j: (j, 0, 0)),
        ],
        scratch_shapes=[pltpu.VMEM((rows, D), f32), pltpu.VMEM((rows, per), f32)],
        compiler_params=pltpu.CompilerParams(vmem_limit_bytes=48 * MIB),
        cost_estimate=cost(18.0),
    )(place[None], *ups, second_in, middle, up_bias, w_down, down_bias)
    return out, slope, chosen, None


def block_back_one(pieces, slope, ups, w_down, w_proj, lefts, norm, inverse, gain, core, dp_size, kernels):
    bf16, f32 = jnp.bfloat16, jnp.float32
    micros, own, _ = pieces[0].shape
    rows = micros * own * len(pieces)
    steps = len(ups)
    k = lefts[0].shape[1] // dp_size
    k_down = w_down.shape[0] // (dp_size * len(pieces))
    if not kernels:
        grad = jnp.stack(pieces, axis=1).reshape(rows, D)
        hidden = (input_back(grad, w_down) * slope.astype(f32)).astype(bf16)
        second = input_back(hidden, jnp.concatenate(ups, axis=1))
        middle = grad.astype(f32) + norm_back(second * gain, norm, inverse)
        low = middle.astype(bf16)
        sums = [jnp.sum(second * norm, axis=0), jnp.sum(second, axis=0)]
        sums = jnp.stack(sums + [column_sum(low), column_sum(grad)])
        packs = pack_block_grads([(lefts[0], hidden), (lefts[1], grad)], core, dp_size)
        mixed = input_back(low, w_proj).astype(bf16)
        return *packs, middle, low, mixed, sums, column_sum(hidden).reshape(steps, 1, D)

    def body(at, *refs):
        piece_refs, refs = refs[: len(pieces)], refs[len(pieces) :]
        up_refs, refs = refs[:steps], refs[steps:]
        slope_ref, down_ref, proj_ref, left_up, left_down, norm_ref, inv_ref, gain_ref = refs[:8]
        sent, kept, middle_ref, low_ref, mixed_ref, sums_ref, hidden_sums, grad, total = refs[8:]
        step = pl.program_id(0)
        first = at[0] == 0

        @pl.when(step == 0)
        def _():
            for m in range(micros):
                for n, ref in enumerate(piece_refs):
                    start = (m * len(pieces) + n) * own
                    grad[start : start + own] = ref[m]
            for n in range(steps):
                here = pl.ds(n * dp_size // (2 * steps), dp_size // (2 * steps))
                part = dot0(left_down[n], grad[...])
                put_halves(first, sent.at[here], kept.at[here], steps * k, part)
            total[...] = jnp.zeros_like(total)

        hidden = dot1(grad[...], down_ref[...]) * slope_ref[...].astype(f32)
        hidden = hidden.astype(bf16)
        ones = jnp.ones((8, rows), bf16)
        hidden_sums[0] = jnp.dot(ones, hidden, preferred_element_type=f32)
        up_grad = dot0(left_up[...], hidden)
        for n in range(steps):

            @pl.when(step == n)
            def _():
                total[...] += dot1(hidden, up_refs[n][...])
                put_halves(first, sent, kept, n * k, up_grad)

        @pl.when(step == steps - 1)
        def _():
            second, norm_now = total[...], norm_ref[...]
            given = grad[...].astype(f32)
            middle = given + norm_back(second * gain_ref[...], norm_now, inv_ref[...])
            low = middle.astype(bf16)
            middle_ref[...] = middle
            low_ref[...] = low
            mixed_ref[...] = dot1(low, proj_ref[...]).astype(bf16)
            for n, values in enumerate((second * norm_now, second, low.astype(f32), given)):
                sums_ref[n : n + 1] = jnp.sum(values, axis=0, keepdims=True)

    def full(v):
        return pl.BlockSpec(v.shape, lambda j: (0,) * len(v.shape), pipeline_mode=pl.Buffered(1))

    pack = low_shape(dp_size // 2, 2, steps * k + k_down, D // 2)
    tall = jax.ShapeDtypeStruct((rows, D), f32)
    outs = [pack, pack, tall, low_shape(rows, D), low_shape(rows, D)]
    outs += [jax.ShapeDtypeStruct((8, D), f32)]
    ins = [*pieces, *ups, slope, w_down, w_proj, *lefts, norm, inverse, gain]
    in_specs = [full(v) for v in ins]
    in_specs[len(pieces) + steps] = pl.BlockSpec((rows, D), lambda j: (0, j))
    in_specs[len(pieces) + steps + 1] = pl.BlockSpec((D, D), lambda j: (j, 0))
    return pl.pallas_call(
        body,
        grid=(steps,),
        out_shape=outs + [jax.ShapeDtypeStruct((steps, 8, D), f32)],
        in_specs=[pl.BlockSpec(memory_space=pltpu.SMEM)] + in_specs,
        out_specs=[pl.BlockSpec(v.shape, lambda j, n=len(v.shape): (0,) * n) for v in outs]
        + [pl.BlockSpec((1, 8, D), lambda j: (j, 0, 0))],
        scratch_shapes=[pltpu.VMEM((rows, D), bf16), pltpu.VMEM((rows, D), f32)],
        compiler_params=pltpu.CompilerParams(vmem_limit_bytes=60 * MIB),
        cost_estimate=cost(24.0),
    )(jnp.asarray(core, jnp.int32)[None], *ins)


def block_back_two(grads, weights, lefts, low, middle, norm, inverse, gain, sums, hidden_sums, own, micros, core, dp_size, kernels):
    f32 = jnp.float32
    rows = low.shape[0]
    length = rows // micros
    steps = hidden_sums.shape[0]

    def smalls(first, norm_now, q, v):
        return [
            jnp.sum(first * norm_now, axis=0, keepdims=True),
            None,
            jnp.sum(first, axis=0, keepdims=True),
            jnp.sum(q.astype(f32), axis=0, keepdims=True),
            jnp.sum(v.astype(f32), axis=0, keepdims=True),
        ]

    if not kernels:
        first = sum(input_back(g, w) for g, w in zip(grads, weights))
        input_grad = middle + norm_back(first * gain, norm, inverse)
        input_grad = input_grad.reshape(micros, length, D)[:, :own]
        rows_of = smalls(first, norm, grads[0], grads[2])
        rows_of[1] = sums[:1]
        small = jnp.concatenate([*rows_of, sums[2:3], sums[1:2], sums[3:4], hidden_sums[:, 0]])
        pairs = [(lefts[0], g) for g in grads] + [(lefts[1], low)]
        return *pack_block_grads(pairs, core, dp_size), input_grad, small

    k = lefts[0].shape[1] // dp_size

    def body(at, *refs):
        grad_refs, weight_refs, refs = refs[:3], refs[3:6], refs[6:]
        left_in, left_mixed, low_ref, middle_ref, norm_ref, inv_ref, gain_ref = refs[:7]
        sums_ref, hidden_ref, sent, kept, out_ref, small_ref = refs[7:]
        flag = at[0] == 0
        for n, ref in enumerate(grad_refs):
            put_halves(flag, sent, kept, n * k, dot0(left_in[...], ref[...]))
        put_halves(flag, sent, kept, 3 * k, dot0(left_mixed[...], low_ref[...]))
        first = dot1(grad_refs[0][...], weight_refs[0][...])
        for g, w in zip(grad_refs[1:], weight_refs[1:]):
            first = first + dot1(g[...], w[...])
        for n, value in enumerate(
            smalls(first, norm_ref[...], grad_refs[0][...], grad_refs[2][...])
        ):
            if value is not None:
                small_ref[n : n + 1] = value
        small_ref[1:2] = sums_ref[0:1]
        small_ref[5:6] = sums_ref[2:3]
        small_ref[6:7] = sums_ref[1:2]
        small_ref[7:8] = sums_ref[3:4]
        for n in range(steps):
            small_ref[8 + n : 9 + n] = hidden_ref[n, 0:1]
        for m in range(micros):
            here = pl.ds(m * length, own)
            back = norm_back(
                first[m * length : m * length + own] * gain_ref[...], norm_ref[here], inv_ref[here]
            )
            out_ref[m] = middle_ref[here] + back

    pack = low_shape(dp_size // 2, 2, 4 * k, D // 2)
    outs = [pack, pack, jax.ShapeDtypeStruct((micros, own, D), f32)]
    outs += [jax.ShapeDtypeStruct((8 + steps, D), f32)]
    ins = [*grads, *weights, *lefts, low, middle, norm, inverse, gain, sums, hidden_sums]
    return small_call(body, outs, [core], ins)


def shards(
    block_input,
    image_ids,
    latents,
    noise,
    timesteps,
    norm_gains,
    block_biases,
    w_qkv,
    w_proj,
    w_up,
    up_bias,
    w_down,
    head_gain,
    head_biases,
    w_cond,
    w_time1,
    w_time2,
    w_input,
    w_ada,
    w_mlp1,
    w_mlp2,
    w_final,
    w_output,
    output_bias,
):
    bf16, f32 = jnp.bfloat16, jnp.float32
    dp_size, copy_size = lax.axis_size("dp"), lax.axis_size("copy")
    world = dp_size * copy_size
    place = lax.axis_index("copy")
    micros, _, own, _ = block_input.shape
    length = image_ids.shape[2]
    total = micros * length
    k_d, k_ff, k_w, k_t = D // world, w_down.shape[0], WIDTH // world, w_time1.shape[0]
    ff = k_ff * world
    kernels = k_d % 8 == 0 and k_w % 16 == 0 and k_t % 8 == 0
    score_scale = HEAD_DIM ** (-0.5)

    def cut(matrix, width):
        return [matrix[:, i : i + width] for i in range(0, matrix.shape[1], width)]

    def pad_flat(parts, width):
        flat = jnp.concatenate([padded_lanes(p) for p in parts])
        count = -(-flat.shape[0] // (16 * width)) * 16 * width
        return jnp.pad(flat, (0, count - flat.shape[0])).reshape(-1, width)

    groups = [
        (cut(w_qkv, D) + [w_proj, pad_flat([norm_gains, block_biases, up_bias[None]], D)], 2),
        (cut(w_up, D) + [w_down], 4),
        (
            cut(w_ada, WIDTH)
            + [w_time2, w_mlp1, w_mlp2]
            + cut(w_final, WIDTH)
            + [w_cond, w_time1]
            + [pad_flat([w_input, w_output.T, head_gain[None], head_biases], WIDTH)],
            0,
        ),
    ]

    def everyone(pack):
        return [shift_copy(pack, copy_size, copy_size - j) for j in range(1, copy_size)]

    def unpack(pack, parts):
        out, at = [], 0
        for part in parts:
            out.append(pack[:, at : at + part.shape[0]].reshape(-1, pack.shape[2]))
            at += part.shape[0]
        return out

    own_rows = block_input[:, 0]
    if kernels:
        square = range(3)
        packs = [
            lay(
                [w_qkv, w_proj, norm_gains, block_biases, up_bias[None]],
                (4 * k_d + 16, D),
                [(0, 0, i * D, k_d, D, i * k_d) for i in square] + [(1, 0, 0, k_d, D, 3 * k_d)],
                [(2, False), (3, False), (4, False)],
            ),
            lay(
                [w_up, w_down],
                (ff // D * k_d + k_ff, D),
                [(0, 0, i * D, k_d, D, i * k_d) for i in range(ff // D)]
                + [(1, 0, 0, k_ff, D, ff // D * k_d)],
                [],
            ),
            lay(
                [w_ada, w_time2, w_mlp1, w_mlp2, w_final, w_cond, w_time1]
                + [w_input, w_output, head_gain[None], head_biases],
                (8 * k_w + k_d + k_t + 16, WIDTH),
                [(0, 0, i * WIDTH, k_w, WIDTH, i * k_w) for i in square]
                + [(i, 0, 0, k_w, WIDTH, (2 + i) * k_w) for i in (1, 2, 3)]
                + [(4, 0, i * WIDTH, k_w, WIDTH, (6 + i) * k_w) for i in range(2)]
                + [(5, 0, 0, k_d, WIDTH, 8 * k_w), (6, 0, 0, k_t, WIDTH, 8 * k_w + k_d)],
                [(7, False), (8, True), (9, False), (10, False)],
            ),
        ]
    else:
        packs = [jnp.concatenate(parts, 0) for parts, _ in groups]
    if kernels and dp_size == 8 and copy_size == 4:
        head_own = packs[2]
        arrived = [everyone(packs[0])]
        *arrived[0], packs[1] = tie(*arrived[0], packs[1])
        arrived.append(everyone(packs[1]))
        *arrived[1], own_rows, head_own = tie(*arrived[1], own_rows, head_own)
        rows_arrived = everyone(own_rows)
        full = [
            gather(pack, sum(p.shape[0] for p in parts[:n]), got)
            for pack, (parts, n), got in zip(packs[:2], groups[:2], arrived[:2])
        ]
        head = lax.all_gather(head_own, ("dp", "copy"), axis=0)
        full.append(head)
    else:
        rows_arrived = everyone(own_rows)
        full = [lax.all_gather(pack, ("dp", "copy"), axis=0) for pack in packs]
    head_pack = full[2]
    full = [unpack(pack, parts) for pack, (parts, _) in zip(full, groups)]

    rows = jnp.stack([own_rows, *rows_arrived], axis=1).reshape(total, D).astype(f32)

    def turned(values):
        twice = jnp.concatenate([values, values], axis=1)
        return lax.dynamic_slice_in_dim(twice, place * own, length, 1)

    ids = turned(image_ids[:, 0])
    latent_rows = turned(latents[:, 0]).reshape(total, CHANNELS)
    noise_rows = turned(noise[:, 0, 0]).reshape(total, CHANNELS)

    w_q, w_k, w_v, w_proj_full, small = full[0]
    w_down_full = full[1][4]
    small = small.reshape(world, -1)
    gains, biases, up_bias_full = spread(small, [(2, k_d), (6, k_d), (1, k_ff)])

    norm_one, inv_one = normalize(rows)
    first_in = (norm_one * gains[0] + biases[0]).astype(bf16)
    queries = (product(first_in, w_q) + biases[1]).astype(bf16)
    key_rows = product(first_in, w_k).astype(bf16)
    value_rows = (product(first_in, w_v) + biases[2]).astype(bf16)
    mixed = attention(queries, key_rows, value_rows, ids)
    middle = rows + product(mixed, w_proj_full) + biases[3]
    norm_two, inv_two = normalize(middle)
    second_in = (norm_two * gains[1] + biases[4]).astype(bf16)
    condition, slope, active_z, active = feed_forward(
        second_in,
        middle,
        full[1][:4],
        up_bias_full,
        w_down_full,
        biases[5:6],
        place,
        copy_size,
        kernels,
    )

    def chosen(values):
        width = values.shape[1]
        k = width // world
        source = jnp.arange(width, dtype=jnp.int32)[:, None]
        target = jnp.arange(dp_size * k, dtype=jnp.int32)[None, :]
        wanted = (target // k * copy_size + place) * k + target % k
        return product(values, (source == wanted).astype(bf16)).astype(bf16)

    condition, first_z, mixed_z, second_z, active_z, slope, norm_one, inv_one, norm_two, inv_two = tie(
        condition,
        chosen(first_in),
        chosen(mixed),
        chosen(second_in),
        chosen(active) if active_z is None else active_z,
        slope,
        norm_one,
        inv_one,
        norm_two,
        inv_two,
    )
    core = lax.axis_index("dp") & 1

    def split_pack(pack, parts):
        out, at = [], 0
        for rows_of in parts:
            out.append(pack[at : at + rows_of])
            at += rows_of
        return out

    def after(first, *values):
        first = list(first)
        return list(tie(*first, *values)[len(first) :])

    def send_after(reduction, first):
        reduction.sent = after(first, *reduction.sent)
        return reduction.receive()

    def form_after(reduction, first):
        reduction.got = after(first, *reduction.got)
        reduction.advance()
        return [*reduction.sent, *reduction.kept]

    def to_copies(reduction, first):
        reduction.got = after(first, *reduction.got)
        chunks = cut_copies(reduction.kept, reduction.got, place, copy_size, kernels)
        arriving = [shift_copy(chunks[j], copy_size, j) for j in range(1, copy_size)]
        return [chunks[0], *arriving]

    def whole(other, mine):
        got = swap_bit(other, dp_size, 0)
        left = jnp.where(core == 0, mine, got)
        right = jnp.where(core == 0, got, mine)
        return jnp.concatenate([left, right], axis=1).astype(f32)

    def finish(reduction):
        while reduction.left:
            reduction.advance().receive()
        parts = [
            jnp.concatenate([v[0] for v in values], axis=1)
            for values in (reduction.kept, reduction.got)
        ]
        return whole(*own_and_other(parts, (0, core), kernels))

    squares = dict(zip(SQUARES, full[2][:8]))
    w_cond_full, w_time1_full, small = full[2][8:]
    w_time2_full = squares["time2"]
    small = small.reshape(world, -1)
    w_input_full, w_output_t, head_gain_f, head_bias = spread(
        small, [(CHANNELS, k_w), (CHANNELS, k_w), (1, k_w), (12, k_w)]
    )
    w_input_full, w_output_t = w_input_full.astype(bf16), w_output_t.astype(bf16)

    row_slot = ids + IMAGES * jnp.arange(micros, dtype=jnp.int32)[:, None]
    row_slot = jnp.where(ids >= 0, row_slot, -1).reshape(total, 1)
    step_vals = timesteps[:, 0, 0].reshape(micros * IMAGES).astype(f32)
    sinusoid_in = sinusoid(step_vals).astype(bf16)
    time_one = product(sinusoid_in, w_time1_full) + head_bias[1]
    time_act = jax.nn.silu(time_one).astype(bf16)
    embedded = product(time_act, w_time2_full) + head_bias[2]
    factors = plan(step_vals)
    slots = jnp.arange(micros * IMAGES, dtype=jnp.int32)[None, :]
    mixing = [
        jnp.sum(jnp.where(row_slot == slots, factors[None, :, i], 0.0), axis=1, keepdims=True)
        for i in range(2)
    ]
    noisy = (latent_rows * mixing[0] + noise_rows * mixing[1]).astype(bf16)
    values = (condition, noisy, noise_rows, row_slot)
    out_bias = output_bias.astype(f32)[None]
    if kernels:
        out, sums = head_kernel(
            head_pack,
            w_cond_full,
            w_input_full,
            w_output_t,
            head_bias,
            head_gain_f,
            out_bias,
            embedded,
            values,
            k_w,
        )
    else:
        others = {"cond": w_cond_full, "input": w_input_full, "output": w_output_t, **squares}
        out, sums = head_step(
            others.get,
            lambda i: head_bias[i : i + 1],
            head_gain_f,
            out_bias,
            embedded,
            values,
        )
        sums = [jnp.pad(sums[n], ((0, 0), (0, WIDTH - sums[n].shape[1]))) for n, _ in HEAD_SUMS]
        sums = jnp.concatenate(sums)
        sums = jnp.pad(sums, ((0, -sums.shape[0] % 8), (0, 0)))
    chunks = out["condition"].reshape(micros, copy_size, own, D)
    chunks = [chunks[:, j] for j in range(copy_size)]
    at_embedded = 2 * CHANNELS
    grad_embedded = sums[at_embedded : at_embedded + micros * IMAGES].astype(bf16)
    grad_time_one = (input_back(grad_embedded, w_time2_full) * silu_slope(time_one)).astype(bf16)
    arriving = [shift_copy(chunks[j], copy_size, j) for j in range(1, copy_size)]
    (gated,) = after(chunks, out["gated"])
    send, keep, sums_one = pack_head_grads(
        [
            (gated, out["fshift"]),
            (gated, out["fscale"]),
            (out["inner_act"], out["two"]),
            (out["mlp_in"], out["one"]),
        ],
        core,
        dp_size,
        copy_size,
        kernels,
    )
    pack_one = Reduction([send], [keep], 2 * k_w, dp_size, kernels)
    arriving = after([keep], *arriving)
    grad_z_own = sum_low([chunks[0], *arriving], kernels)
    arriving = [shift_copy(grad_z_own, copy_size, copy_size - j) for j in range(1, copy_size)]
    send_after(pack_one, [grad_z_own])
    (gated,) = after([grad_z_own], gated)
    of_head = 2 * CHANNELS + 8
    send, keep, small_grads = pack_head_grads(
        [
            (gated, out["shift"]),
            (gated, out["scale"]),
            (gated, out["gate"]),
            (time_act, grad_embedded),
            (condition, out["cond"]),
            (sinusoid_in, grad_time_one),
        ],
        core,
        dp_size,
        copy_size,
        kernels,
        (sums_one, sums),
        (
            (2, 0, 2 * CHANNELS),
            (2, of_head, 1),
            (0, 4, 2),
            (0, 3, 1),
            (2, of_head + 1, 2),
            (1, 3, 1),
            (1, 2, 1),
            (0, 0, 3),
            (1, 0, 2),
            (2, of_head + 3, 1),
            (2, of_head + 4, 2),
        ),
    )
    pack_two = Reduction([send], [keep], 3 * k_w, dp_size, kernels)
    formed = form_after(pack_one, [keep])
    arriving = after(formed, *arriving)
    send_after(pack_one, arriving)
    send_after(pack_two, arriving)

    def swap_copies(values, shift, first):
        return values + after(first, swap_copy(values, copy_size, shift))[0]

    send, keep, grad_middle, grad_branch, grad_mixed, block_sums, hidden_sums = block_back_one(
        [grad_z_own, *arriving],
        slope,
        full[1][:4],
        w_down_full,
        w_proj_full,
        (second_z, active_z),
        norm_two,
        inv_two,
        gains[1:2],
        core,
        dp_size,
        kernels,
    )
    sent, kept = [send], [keep]
    formed = form_after(pack_one, [grad_mixed])
    send_after(pack_one, formed)
    small_grads = swap_copies(small_grads, 1, formed)
    formed = form_after(pack_two, [small_grads])
    send_after(pack_two, formed)
    (grad_mixed,) = after(formed, grad_mixed)
    back = attention_back(queries, key_rows, value_rows, grad_mixed, ids, 0, None)
    pack_one.got = after(back, *pack_one.got)
    send, one_half = cut_copy_halves(pack_one.kept, pack_one.got, place, copy_size, kernels)
    one_got = swap_copy(send, copy_size, copy_size // 2)
    small_grads = swap_copies(small_grads, 2, [one_half])
    (grad_mixed,) = after([small_grads], grad_mixed)
    for m in range(1, micros):
        back = attention_back(queries, key_rows, value_rows, grad_mixed, ids, m, back)
    formed = form_after(pack_two, back)
    send_after(pack_two, formed)
    (one_got,) = after(formed, one_got)
    send, one_last = cut_copy_last(one_half, one_got, place, kernels)
    one_got = swap_copy(send, copy_size, 1)
    back = after([one_last], *back)
    send, keep, input_grad, block_small = block_back_two(
        back,
        (w_q, w_k, w_v),
        (first_z, mixed_z),
        grad_branch,
        grad_middle,
        norm_one,
        inv_one,
        gains[:1],
        block_sums,
        hidden_sums,
        own,
        micros,
        core,
        dp_size,
        kernels,
    )
    sent, kept = sent + [send], kept + [keep]
    pack_three = Reduction(sent, kept, 6 * k_d, dp_size, kernels)
    two_parts = to_copies(pack_two, [keep])
    (one_got,) = after([two_parts[0]], one_got)
    own_one_parts = own_and_other([one_last, one_got], (0, core), kernels)
    send_after(pack_three, own_one_parts)
    head_rows = small_grads.shape[0]
    block_small = jnp.pad(block_small, ((0, -block_small.shape[0] % 8), (0, WIDTH - D)))
    small_grads = jnp.concatenate([small_grads, block_small], axis=0)
    everywhere = lax.all_gather(small_grads, "dp", axis=0)
    small_grads = everywhere[0]
    for n in range(1, dp_size):
        small_grads = small_grads + everywhere[n]
    block_small = small_grads[head_rows:, :D]
    formed = form_after(pack_three, own_one_parts)
    send_after(pack_three, formed)
    while pack_three.left:
        formed = form_after(pack_three, [two_parts[0]])
        send_after(pack_three, formed)
    two_parts = after(formed, *two_parts)
    own_two_parts = own_and_other(two_parts, (place, core), kernels)
    own_all = finish(pack_three)
    own_up = jnp.concatenate(split_pack(own_all, [k_d] * 4), axis=1)
    own_down = own_all[4 * k_d : 4 * k_d + k_ff]
    own_four = own_all[4 * k_d + k_ff :]
    own_q, own_k, own_v, own_proj = split_pack(own_four, [k_d] * 4)
    own_fshift, own_fscale, own_two, own_one = split_pack(
        whole(*own_one_parts), [k_w] * 4
    )
    own_shift, own_scale, own_gate, own_time2, own_cond, own_time1 = split_pack(
        whole(*own_two_parts), [k_w] * 4 + [k_d, k_t]
    )
    me = lax.axis_index("dp") * copy_size + place
    own_rest = lax.dynamic_slice_in_dim(block_small[:8], me * k_d, k_d, 1)
    own_gains, own_biases = own_rest[:2], own_rest[2:]
    own_up_bias = lax.dynamic_slice_in_dim(block_small[8 : 8 + ff // D].reshape(ff), me * k_ff, k_ff)
    own_small = lax.dynamic_slice_in_dim(small_grads, me * k_w, k_w, 1)
    own_w_input = own_small[:CHANNELS]
    own_w_output = own_small[CHANNELS : 2 * CHANNELS].T
    own_head_gain = own_small[2 * CHANNELS]
    own_head_biases = own_small[2 * CHANNELS + 1 : 2 * CHANNELS + 13]
    grad_out_bias = small_grads[2 * CHANNELS + 13, :CHANNELS]

    input_grad = input_grad.reshape(micros, 1, own, D)
    block_output = condition.reshape(micros, length, D)[:, :own].reshape(micros, 1, own, D)
    return (
        block_output,
        input_grad,
        own_gains,
        own_biases,
        jnp.concatenate([own_q, own_k, own_v], axis=1),
        own_proj,
        own_up,
        own_up_bias,
        own_down,
        own_head_gain,
        own_head_biases,
        own_cond,
        own_time1,
        own_time2,
        own_w_input,
        jnp.concatenate([own_shift, own_scale, own_gate], axis=1),
        own_one,
        own_two,
        jnp.concatenate([own_fshift, own_fscale], axis=1),
        own_w_output,
        grad_out_bias,
    )


def solution(mesh):
    in_specs = (
        P(None, "dp", "copy", None),
        P(None, "dp", None),
        P(None, "dp", None, None),
        P(None, "copy", "dp", None, None),
        P(None, "copy", "dp", None),
        P(None, ("dp", "copy")),
        P(None, ("dp", "copy")),
        P(("dp", "copy"), None),
        P(("dp", "copy"), None),
        P(("dp", "copy"), None),
        P(("dp", "copy")),
        P(("dp", "copy"), None),
        P(("dp", "copy")),
        P(None, ("dp", "copy")),
        P(("dp", "copy"), None),
        P(("dp", "copy"), None),
        P(("dp", "copy"), None),
        P(None, ("dp", "copy")),
        P(("dp", "copy"), None),
        P(("dp", "copy"), None),
        P(("dp", "copy"), None),
        P(("dp", "copy"), None),
        P(("dp", "copy"), None),
        P(),
    )
    out_specs = (
        P(None, "dp", "copy", None),
        P(None, "dp", "copy", None),
        P(None, ("dp", "copy")),
        P(None, ("dp", "copy")),
        P(("dp", "copy"), None),
        P(("dp", "copy"), None),
        P(("dp", "copy"), None),
        P(("dp", "copy")),
        P(("dp", "copy"), None),
        P(("dp", "copy")),
        P(None, ("dp", "copy")),
        P(("dp", "copy"), None),
        P(("dp", "copy"), None),
        P(("dp", "copy"), None),
        P(None, ("dp", "copy")),
        P(("dp", "copy"), None),
        P(("dp", "copy"), None),
        P(("dp", "copy"), None),
        P(("dp", "copy"), None),
        P(("dp", "copy"), None),
        P(),
    )
    return jax.shard_map(shards, mesh=mesh, in_specs=in_specs, out_specs=out_specs, check_vma=False)
```

```python
import functools
import math

import jax
import jax.numpy as jnp
from jax import lax
from jax.experimental import pallas as pl
from jax.experimental.pallas import tpu as pltpu
from jax.sharding import PartitionSpec as P

D = 768
HEADS = 12
HEAD_DIM = 64
WIDTH = 1024
FREQ = 256
CHANNELS = 16
IMAGES = 4


epsilon = 1e-06
highest = lax.Precision.HIGHEST


def product(left_side, right_side):
    return jnp.dot(left_side, right_side, preferred_element_type=jnp.float32)


def weight_grad(left_side, right_side):
    return lax.dot_general(
        left_side, right_side, (((0,), (0,)), ((), ())), preferred_element_type=jnp.float32
    )


def input_back(gradient, weight):
    return lax.dot_general(
        gradient, weight, (((1,), (1,)), ((), ())), preferred_element_type=jnp.float32
    )


def column_sum(values):
    return jnp.sum(values.astype(jnp.float32), axis=0)


def normalize(values):
    center = values - jnp.mean(values, axis=-1, keepdims=True)
    inverse = lax.rsqrt(jnp.mean(center * center, axis=-1, keepdims=True) + epsilon)
    return (center * inverse, inverse)


def norm_back(gradient, normed, inverse):
    return inverse * (
        gradient
        - jnp.mean(gradient, axis=-1, keepdims=True)
        - normed * jnp.mean(gradient * normed, axis=-1, keepdims=True)
    )


def silu_slope(values):
    sigma = jax.nn.sigmoid(values)
    return sigma * (1.0 + values * (1.0 - sigma))


def gelu_slope(values):
    return 0.5 * (1.0 + lax.erf(values * 2.0 ** (-0.5))) + values * jnp.exp(
        -0.5 * values * values
    ) * (2.0 * math.pi) ** (-0.5)


def sinusoid(step_vals):
    half_width = FREQ // 2
    rates = jnp.exp(-math.log(10000.0) * jnp.arange(half_width, dtype=jnp.float32) / half_width)
    angles = step_vals[:, None] * rates[None, :]
    return jnp.concatenate([jnp.cos(angles), jnp.sin(angles)], axis=1)


def plan(step_vals):
    anchor = math.cos(0.008 / 1.008 * math.pi / 2.0) ** 2
    angle_now = ((step_vals + 1.0) / 1000.0 + 0.008) / 1.008 * (math.pi / 2.0)
    signal = jnp.cos(angle_now) ** 2 / anchor
    return jnp.stack([jnp.sqrt(signal), jnp.sqrt(1.0 - signal)], axis=1)


def tdot(left_side, right_side):
    return lax.dot_general(
        left_side, right_side, (((0,), (0,)), ((), ())), preferred_element_type=jnp.float32
    )


def swap_bit(values, size, bit):
    return lax.ppermute(values, "dp", [(i, i ^ (1 << bit)) for i in range(size)])


def shift_copy(values, size, shift):
    return lax.ppermute(values, "copy", [(i, (i + shift) % size) for i in range(size)])


def swap_copy(values, size, shift):
    return lax.ppermute(values, "copy", [(i, i ^ shift) for i in range(size)])


def pick(values, index, axis):
    return lax.dynamic_index_in_dim(values, index, axis, keepdims=False)


def tie(*values):
    return lax.optimization_barrier(values)


MIB = 1 << 20


def cost(microseconds):
    return pl.CostEstimate(
        flops=int(microseconds * 10**9), bytes_accessed=10**5, transcendentals=0
    )


def dot0(left_side, right_side):
    return lax.dot_general(
        left_side, right_side, (((0,), (0,)), ((), ())), preferred_element_type=jnp.float32
    )


def dot1(left_side, right_side):
    return lax.dot_general(
        left_side, right_side, (((1,), (1,)), ((), ())), preferred_element_type=jnp.float32
    )


def small_call(body, outs, scalars, ins):
    size = sum(math.prod(o.shape) * o.dtype.itemsize for o in outs)
    size += sum(math.prod(v.shape) * v.dtype.itemsize for v in ins)
    return pl.pallas_call(
        body,
        out_shape=outs,
        in_specs=[pl.BlockSpec(memory_space=pltpu.SMEM)]
        + [pl.BlockSpec(memory_space=pltpu.VMEM)] * len(ins),
        out_specs=[pl.BlockSpec(memory_space=pltpu.VMEM)] * len(outs),
        compiler_params=pltpu.CompilerParams(vmem_limit_bytes=60 * MIB),
        cost_estimate=cost(size / 2.2e6),
    )(jnp.stack([jnp.asarray(v, jnp.int32) for v in scalars]), *ins)


def low_shape(*dims):
    return jax.ShapeDtypeStruct(dims, jnp.bfloat16)


def add_up(one, two):
    return one.astype(jnp.float32) + two.astype(jnp.float32)


def cut_first(keeps, gots, rows, bits, kernels):
    count, mids, _, width = keeps[0].shape
    half = count // 2
    sizes = [k.shape[2] for k in keeps]
    total = sum(sizes)

    if not kernels:
        sums = jnp.concatenate([add_up(k, g) for k, g in zip(keeps, gots)], axis=2)
        sums = sums.astype(jnp.bfloat16)
        first = sums[:, :, :rows].reshape(2, half, mids, rows, width)
        second = sums[:, :, rows:].reshape(half, 2, mids, total - rows, width)
        return [
            pick(first, 1 - bits[0], 0),
            pick(first, bits[0], 0),
            pick(second, 1 - bits[1], 1),
            pick(second, bits[1], 1),
        ]

    def body(at, *refs):
        keep_refs, got_refs = refs[: len(keeps)], refs[len(keeps) : 2 * len(keeps)]
        outs = refs[2 * len(keeps) :]
        for out, bit, low in zip(outs, (1 - at[0], at[0], 1 - at[1], at[1]), (0, 0, 1, 1)):
            begin, end = (rows, total) if low else (0, rows)
            at_row = 0
            for keep, got, n in zip(keep_refs, got_refs, sizes):
                top, bottom = max(begin, at_row), min(end, at_row + n)
                if top < bottom:
                    cut = pl.ds(top - at_row, bottom - top)
                    for i in range(half):
                        p = 2 * i + bit if low else bit * half + i
                        value = add_up(keep[p, :, cut], got[p, :, cut]).astype(jnp.bfloat16)
                        out[i, :, top - begin : bottom - begin] = value
                at_row += n

    outs = [low_shape(half, mids, n, width) for n in (rows, rows, total - rows, total - rows)]
    return small_call(body, outs, bits, [*keeps, *gots])


def cut_next(keeps, gots, bits, kernels):
    count, mids, _, width = keeps[0].shape
    half = count // 2
    sizes = [k.shape[2] for k in keeps]
    if not kernels:
        sums = [add_up(k, g).astype(jnp.bfloat16) for k, g in zip(keeps, gots)]
        first = sums[0].reshape(2, half, mids, sizes[0], width)
        second = sums[1].reshape(half, 2, mids, sizes[1], width)
        return [
            pick(first, 1 - bits[0], 0),
            pick(first, bits[0], 0),
            pick(second, 1 - bits[1], 1),
            pick(second, bits[1], 1),
        ]

    def body(at, keep_one, got_one, keep_two, got_two, *outs):
        for out, bit, top in zip(outs, (1 - at[0], at[0], 1 - at[1], at[1]), (0, 0, 1, 1)):
            keep, got = (keep_two, got_two) if top else (keep_one, got_one)
            for i in range(half):
                p = 2 * i + bit if top else bit * half + i
                out[i] = add_up(keep[p], got[p]).astype(jnp.bfloat16)

    outs = [low_shape(half, mids, n, width) for n in (sizes[0], sizes[0], sizes[1], sizes[1])]
    return small_call(body, outs, bits, [keeps[0], gots[0], keeps[1], gots[1]])


def cut_copies(keeps, gots, place, copy_size, kernels):
    _, mids, _, width = keeps[0].shape
    sizes = [k.shape[2] for k in keeps]
    total = sum(sizes)
    if not kernels:
        sums = jnp.concatenate([add_up(k, g)[0] for k, g in zip(keeps, gots)], axis=1)
        sums = sums.astype(jnp.bfloat16).reshape(2, copy_size, total, width)
        return [pick(sums, lax.rem(place + j, copy_size), 1) for j in range(copy_size)]

    def body(at, keep_one, got_one, keep_two, got_two, *outs):
        for j in range(copy_size):
            z = lax.rem(at[0] + j, copy_size)
            for c in range(2):
                m = c * copy_size + z
                top = add_up(keep_one[0, m], got_one[0, m]).astype(jnp.bfloat16)
                low = add_up(keep_two[0, m], got_two[0, m]).astype(jnp.bfloat16)
                outs[j][c, : sizes[0]] = top
                outs[j][c, sizes[0] :] = low

    outs = [low_shape(2, total, width)] * copy_size
    return small_call(body, outs, [place], [keeps[0], gots[0], keeps[1], gots[1]])


def sum_low(parts, kernels):
    if not kernels:
        return sum(p.astype(jnp.float32) for p in parts).astype(jnp.bfloat16)

    def body(at, *refs):
        total = refs[0][...].astype(jnp.float32)
        for ref in refs[1:-1]:
            total = total + ref[...].astype(jnp.float32)
        refs[-1][...] = total.astype(jnp.bfloat16)

    return small_call(body, [low_shape(*parts[0].shape)], [0], parts)[0]


def cut_copy_halves(keeps, gots, place, copy_size, kernels):
    _, mids, _, width = keeps[0].shape
    sizes = [k.shape[2] for k in keeps]
    total, half = sum(sizes), copy_size // 2
    if not kernels:
        sums = jnp.concatenate([add_up(k, g)[0] for k, g in zip(keeps, gots)], axis=1)
        sums = sums.astype(jnp.bfloat16).reshape(2, 2, half, total, width)
        top = place // half
        return [pick(sums, 1 - top, 1), pick(sums, top, 1)]

    def body(at, keep_one, got_one, keep_two, got_two, *outs):
        top = at[0] // half
        for out, bit in zip(outs, (1 - top, top)):
            for c in range(2):
                for j in range(half):
                    m = c * copy_size + bit * half + j
                    first = add_up(keep_one[0, m], got_one[0, m]).astype(jnp.bfloat16)
                    second = add_up(keep_two[0, m], got_two[0, m]).astype(jnp.bfloat16)
                    out[c, j, : sizes[0]] = first
                    out[c, j, sizes[0] :] = second

    outs = [low_shape(2, half, total, width)] * 2
    return small_call(body, outs, [place], [keeps[0], gots[0], keeps[1], gots[1]])


def cut_copy_last(keep, got, place, kernels):
    if not kernels:
        sums = add_up(keep, got).astype(jnp.bfloat16)
        return [pick(sums, 1 - place % 2, 1), pick(sums, place % 2, 1)]

    def body(at, keep_ref, got_ref, *outs):
        low = lax.rem(at[0], 2)
        for out, bit in zip(outs, (1 - low, low)):
            for c in range(2):
                out[c] = add_up(keep_ref[c, bit], got_ref[c, bit]).astype(jnp.bfloat16)

    return small_call(body, [low_shape(2, *keep.shape[2:])] * 2, [place], [keep, got])


def own_and_other(parts, scalars, kernels):
    place, core = scalars
    count = len(parts)
    _, total, width = parts[0].shape
    if not kernels:
        stacked = jnp.stack(parts).astype(jnp.float32)
        sums = 0.0
        for i in range(count):
            sums = sums + pick(stacked, lax.rem(place + count - i, count), 0)
        sums = sums.astype(jnp.bfloat16)
        return [pick(sums, 1 - core, 0), pick(sums, core, 0)]

    def body(at, *refs):
        for out, c in zip(refs[count:], (1 - at[1], at[1])):
            values = [r[c].astype(jnp.float32) for r in refs[:count]]
            sums = None
            for i in range(count):
                turn = lax.rem(at[0] + count - i, count)
                value = values[0]
                for j in range(1, count):
                    value = jnp.where(turn == j, values[j], value)
                sums = value if sums is None else sums + value
            out[...] = sums.astype(jnp.bfloat16)

    return small_call(body, [low_shape(total, width)] * 2, scalars, parts)


class Reduction:
    def __init__(self, sent, kept, rows, size, kernels):
        self.size, self.rows, self.kernels = size, rows, kernels
        self.left = size.bit_length() - 2
        self.me = lax.axis_index("dp")
        self.sent, self.kept, self.bits = list(sent), list(kept), [0] * len(sent)
        self.first = True

    def receive(self):
        self.got = [swap_bit(v, self.size, bit) for v, bit in zip(self.sent, self.bits)]
        return self

    def advance(self):
        if self.first:
            self.bits = [self.left, 1]
            bits = [(self.me >> b) & 1 for b in self.bits]
            cuts = cut_first(self.kept, self.got, self.rows, bits, self.kernels)
        else:
            self.bits = [self.bits[0] - 1, self.bits[1] + 1]
            bits = [(self.me >> b) & 1 for b in self.bits]
            cuts = cut_next(self.kept, self.got, bits, self.kernels)
        self.first = False
        self.left -= 1
        self.sent, self.kept = [cuts[0], cuts[2]], [cuts[1], cuts[3]]
        return self


def attend(ids_col, ids_row, q, k, lanes, head, scale):
    wanted = (lanes >= HEAD_DIM) if head else (lanes < HEAD_DIM)
    scores = dot1(jnp.where(wanted, q, 0), k) * scale
    scores = jnp.where(ids_col == ids_row, scores, -1e30)
    exps = jnp.exp(scores - jnp.max(scores, axis=-1, keepdims=True))
    return wanted, exps / jnp.sum(exps, axis=-1, keepdims=True)


def attention_specs(micros, length, first=0):
    wide = pl.BlockSpec((length, 2 * HEAD_DIM), lambda m, h: (m + first, h))
    col = pl.BlockSpec((length, 1), lambda m, h: (m + first, 0))
    row = pl.BlockSpec((1, 1, length), lambda m, h: (m + first, 0, 0))
    return wide, col, row


def attention(queries, key_rows, value_rows, ids):
    micros, length = ids.shape
    scale = HEAD_DIM ** (-0.5)
    wide, col, row = attention_specs(micros, length)

    def body(col_ref, row_ref, q_ref, k_ref, v_ref, out_ref):
        lanes = lax.broadcasted_iota(jnp.int32, (1, 2 * HEAD_DIM), 1)
        outs = []
        for head in range(2):
            _, probs = attend(
                col_ref[...], row_ref[0], q_ref[...], k_ref[...], lanes, head, scale
            )
            outs.append(
                jnp.dot(
                    probs.astype(jnp.bfloat16), v_ref[...], preferred_element_type=jnp.float32
                )
            )
        out_ref[...] = jnp.where(lanes < HEAD_DIM, outs[0], outs[1]).astype(jnp.bfloat16)

    return pl.pallas_call(
        body,
        grid=(micros, HEADS // 2),
        out_shape=low_shape(micros * length, D),
        in_specs=[col, row, wide, wide, wide],
        out_specs=wide,
        compiler_params=pltpu.CompilerParams(vmem_limit_bytes=24 * MIB),
        cost_estimate=cost(15.0),
    )(ids.reshape(-1, 1), ids[:, None], queries, key_rows, value_rows)


def attention_back(queries, key_rows, value_rows, grad_mixed, ids, which, before):
    micros, length = ids.shape
    scale = HEAD_DIM ** (-0.5)
    wide, col, row = attention_specs(micros, length, which)

    def body(col_ref, row_ref, q_ref, k_ref, v_ref, g_ref, *outs):
        lanes = lax.broadcasted_iota(jnp.int32, (1, 2 * HEAD_DIM), 1)
        q, k, v, g = q_ref[...], k_ref[...], v_ref[...], g_ref[...]
        parts = []
        for head in range(2):
            wanted, probs = attend(col_ref[...], row_ref[0], q, k, lanes, head, scale)
            grad_probs = dot1(jnp.where(wanted, g, 0), v)
            delta = jnp.sum(grad_probs * probs, axis=-1, keepdims=True)
            grad_scores = (probs * (grad_probs - delta)).astype(jnp.bfloat16)
            parts.append(
                (
                    jnp.dot(grad_scores, k, preferred_element_type=jnp.float32) * scale,
                    dot0(grad_scores, q) * scale,
                    dot0(probs.astype(jnp.bfloat16), g),
                )
            )
        for out, one, two in zip(outs[-3:], *parts):
            out[...] = jnp.where(lanes < HEAD_DIM, one, two).astype(jnp.bfloat16)

    return pl.pallas_call(
        body,
        grid=(1, HEADS // 2),
        out_shape=[low_shape(micros * length, D)] * 3,
        in_specs=[col, row, wide, wide, wide, wide]
        + [pl.BlockSpec(memory_space=pl.ANY)] * len(before or ()),
        out_specs=[wide] * 3,
        input_output_aliases={6 + i: i for i in range(len(before or ()))},
        compiler_params=pltpu.CompilerParams(vmem_limit_bytes=60 * MIB),
        cost_estimate=cost(12.0),
    )(ids.reshape(-1, 1), ids[:, None], queries, key_rows, value_rows, grad_mixed, *(before or ()))


def pack_head_grads(pairs, core, dp_size, copy_size, kernels, others=(), plan=None):
    world = dp_size * copy_size
    count, mids = dp_size // 2, 2 * copy_size
    width = pairs[0][1].shape[1]
    half = width // 2
    sizes = [p[0].shape[1] // world for p in pairs]
    total = sum(sizes)
    if not kernels:
        packs = []
        for c in (1 - core, core):
            parts = []
            for left_side, right_side in pairs:
                part = lax.dynamic_slice_in_dim(right_side, c * half, half, 1)
                part = weight_grad(left_side, part).astype(jnp.bfloat16)
                parts.append(part.reshape(count, mids, -1, half))
            packs.append(jnp.concatenate(parts, axis=2))
        given = [jnp.stack([column_sum(p[1]) for p in pairs]), *others]
        if plan is None:
            return packs + given
        return packs + [jnp.concatenate([given[i][at : at + n] for i, at, n in plan])]

    lefts, which = [], []
    for left_side, _ in pairs:
        seen = [i for i, other in enumerate(lefts) if other is left_side]
        which.append(seen[0] if seen else len(lefts))
        lefts += [] if seen else [left_side]
    rights = [p[1] for p in pairs]
    narrow = [v.shape[1] // count % 128 == 0 for v in lefts]
    held = [i for i, w in enumerate(which) if not narrow[w]]

    where, height = list(range(len(pairs))), len(pairs)
    if plan is not None:
        at_row = 0
        for source, row, n in plan:
            if not source:
                where[row : row + n] = range(at_row, at_row + n)
            at_row += n
        height = at_row

    def body(at, *refs):
        left_refs = refs[: len(lefts)]
        right_refs = refs[len(lefts) : len(lefts) + len(rights)]
        other_refs, refs = refs[len(lefts) + len(rights) :][: len(others)], refs[len(others) :]
        sent, kept, sums = refs[len(lefts) + len(rights) :][:3]
        scratch = refs[len(lefts) + len(rights) + 3 :]
        first = at[0] == 0
        step = pl.program_id(0)

        @pl.when(step == 0)
        def _():
            for i, right in enumerate(right_refs):
                ones = jnp.ones((8, right.shape[0]), jnp.bfloat16)
                row = jnp.dot(ones, right[...], preferred_element_type=jnp.float32)
                sums[where[i] : where[i] + 1] = row[:1]
            at = 0
            for source, row, n in plan or ():
                if source:
                    sums[at : at + n] = other_refs[source - 1][row : row + n]
                at += n
            for i, buffer in zip(held, scratch):
                buffer[...] = dot0(left_refs[which[i]][...], right_refs[i][...])

        at_row = 0
        for i, n in enumerate(sizes):
            if i in held:
                rows = mids * n
                whole = scratch[held.index(i)][pl.ds(pl.multiple_of(step * rows, 8), rows)]
            else:
                whole = dot0(left_refs[which[i]][...], right_refs[i][...])
            left, right = whole[:, :half], whole[:, half:]
            for out, part in (
                (sent, jnp.where(first, right, left)),
                (kept, jnp.where(first, left, right)),
            ):
                out[0, :, at_row : at_row + n] = part.reshape(mids, n, half).astype(jnp.bfloat16)
            at_row += n

    in_specs = [pl.BlockSpec(memory_space=pltpu.SMEM)]
    for v, cut_up in zip(lefts, narrow):
        if cut_up:
            in_specs.append(pl.BlockSpec((v.shape[0], v.shape[1] // count), lambda p: (0, p)))
        else:
            in_specs.append(pl.BlockSpec(v.shape, lambda p: (0, 0)))
    in_specs += [pl.BlockSpec(v.shape, lambda p: (0, 0)) for v in [*rights, *others]]
    out_spec = pl.BlockSpec((1, mids, total, half), lambda p: (p, 0, 0, 0))
    return pl.pallas_call(
        body,
        grid=(count,),
        out_shape=[low_shape(count, mids, total, half)] * 2
        + [jax.ShapeDtypeStruct((height, width), jnp.float32)],
        in_specs=in_specs,
        out_specs=[out_spec] * 2 + [pl.BlockSpec((height, width), lambda p: (0, 0))],
        scratch_shapes=[
            pltpu.VMEM((lefts[which[i]].shape[1], width), jnp.float32) for i in held
        ],
        compiler_params=pltpu.CompilerParams(vmem_limit_bytes=60 * MIB),
        cost_estimate=cost(13.0),
    )(jnp.asarray(core, jnp.int32)[None], *lefts, *rights, *others)


def assemble(pieces, scalars, copy_size, rows):
    width = pieces[0][0].shape[-1]
    total = rows

    def body(at, *refs):
        ins, out, sems = refs[: len(pieces)], refs[len(pieces)], refs[len(pieces) + 1]
        copies = []
        for ref, (value, first, flip, vary) in zip(ins, pieces):
            for d in range(2):
                for j in range(copy_size):
                    dp = at[0] ^ (flip | (vary if d else 0))
                    owner = dp * copy_size + lax.rem(at[1] + j, copy_size)
                    copy = pltpu.make_async_copy(
                        ref.at[d, j],
                        out.at[owner, pl.ds(first, value.shape[2])],
                        sems.at[len(copies)],
                    )
                    copy.start()
                    copies.append(copy)
        for copy in copies:
            copy.wait()

    return pl.pallas_call(
        body,
        out_shape=low_shape(8 * copy_size, total, width),
        in_specs=[pl.BlockSpec(memory_space=pltpu.SMEM)]
        + [pl.BlockSpec(memory_space=pl.ANY)] * len(pieces),
        out_specs=pl.BlockSpec(memory_space=pl.ANY),
        scratch_shapes=[pltpu.SemaphoreType.DMA((len(pieces) * 2 * copy_size,))],
        compiler_params=pltpu.CompilerParams(vmem_limit_bytes=4 * MIB),
        cost_estimate=cost(8.0),
    )(jnp.stack([jnp.asarray(v, jnp.int32) for v in scalars]), *[p[0] for p in pieces])


def gather(pack, rows, arrived):
    total = pack.shape[0]
    along = [pack, *arrived]
    pieces = []
    for first, last, bits in ((0, rows, (2, 1)), (rows, total, (1, 2))):
        held = jnp.stack([v[first:last] for v in along])
        held = jnp.stack([held, swap_bit(held, 8, bits[0])])
        got = swap_bit(held, 8, bits[1])
        vary = 1 << bits[0]
        other = 1 << bits[1]
        pieces += [(held, first, 0, vary), (got, first, other, vary)]
        pieces += [
            (swap_bit(held, 8, 0), first, 1, vary),
            (swap_bit(got, 8, 0), first, other | 1, vary),
        ]
    return assemble(pieces, (lax.axis_index("dp"), lax.axis_index("copy")), 4, total)


LANES = 128


def padded_lanes(values):
    return jnp.pad(values, ((0, 0), (0, LANES - values.shape[1]))).reshape(-1)


def lay(ins, shape, plan, vectors):
    height, width = shape
    start = max(p[5] + p[3] for p in plan)

    def body(*refs):
        out = refs[-1]
        for which, row, column, rows, columns, there in plan:
            out[there : there + rows] = refs[which][row : row + rows, column : column + columns]
        values = []
        for which, turned in vectors:
            value = refs[which][...].astype(jnp.float32)
            value = value.T if turned else value
            values += [value[i : i + 1] for i in range(value.shape[0])]
        zero = jnp.zeros((1, LANES), jnp.float32)
        values = [
            jnp.concatenate([v, zero[:, : LANES - v.shape[1]]], axis=1) for v in values
        ]
        values += [zero] * ((height - start) * width // LANES - len(values))
        per = width // LANES
        lines = [
            jnp.concatenate(values[i : i + per], axis=1) for i in range(0, len(values), per)
        ]
        if lines:
            out[start:] = jnp.concatenate(lines, axis=0).astype(jnp.bfloat16)

    return pl.pallas_call(
        body,
        out_shape=low_shape(height, width),
        in_specs=[pl.BlockSpec(memory_space=pltpu.VMEM)] * len(ins),
        out_specs=pl.BlockSpec(memory_space=pltpu.VMEM),
        compiler_params=pltpu.CompilerParams(vmem_limit_bytes=16 * MIB),
        cost_estimate=cost(2.0),
    )(*ins)


def spread(packed, sizes):
    world = packed.shape[0]
    total = sum(count for count, _ in sizes)

    def body(packed_ref, *outs):
        at = 0
        for (count, k), out in zip(sizes, outs):
            width = world * k
            column = lax.broadcasted_iota(jnp.int32, (LANES, width), 1)
            row = lax.broadcasted_iota(jnp.int32, (LANES, width), 0)
            tile = (row == column % k).astype(jnp.bfloat16)
            owner = lax.broadcasted_iota(jnp.int32, (world, width), 0)
            own = owner == lax.broadcasted_iota(jnp.int32, (world, width), 1) // k
            for i in range(count):
                block = packed_ref[:, (at + i) * LANES : (at + i + 1) * LANES]
                values = jnp.dot(block, tile, preferred_element_type=jnp.float32)
                out[i : i + 1] = jnp.sum(jnp.where(own, values, 0.0), axis=0, keepdims=True)
            at += count

    return pl.pallas_call(
        body,
        out_shape=[
            jax.ShapeDtypeStruct((count, world * k), jnp.float32) for count, k in sizes
        ],
        in_specs=[pl.BlockSpec(memory_space=pltpu.VMEM)],
        out_specs=[pl.BlockSpec(memory_space=pltpu.VMEM)] * len(sizes),
        compiler_params=pltpu.CompilerParams(vmem_limit_bytes=16 * MIB),
        cost_estimate=cost(0.7),
    )(packed[:, : total * LANES])


def head_step(weight, head_bias, gain, out_bias, embedded, values):
    bf16, f32 = jnp.bfloat16, jnp.float32
    condition, noisy, noise, slot = values
    out, sums = {}, {}
    valid = (slot >= 0).astype(f32)
    cond = product(condition, weight("cond")) + head_bias(0)
    chosen = jnp.zeros_like(cond)
    for i in range(embedded.shape[0]):
        chosen = jnp.where(slot == i, embedded[i : i + 1], chosen)
    cond = cond + chosen
    gated = jax.nn.silu(cond).astype(bf16)
    out["gated"] = gated
    entry = product(noisy, weight("input")) + head_bias(3)
    norm_head, inv_head = normalize(entry)
    affine = norm_head * gain + head_bias(4)
    shift = product(gated, weight("shift")) + head_bias(7)
    scale = product(gated, weight("scale")) + head_bias(8)
    mlp_in = (affine * (1.0 + scale) + shift).astype(bf16)
    out["mlp_in"] = mlp_in
    inner_one = product(mlp_in, weight("one")) + head_bias(5)
    inner_act = jax.nn.silu(inner_one).astype(bf16)
    out["inner_act"] = inner_act
    inner_two = product(inner_act, weight("two")) + head_bias(6)
    gate = product(gated, weight("gate")) + head_bias(9)
    residual = entry + gate * inner_two
    fshift = product(gated, weight("fshift")) + head_bias(10)
    fscale = product(gated, weight("fscale")) + head_bias(11)
    norm_final, inv_final = normalize(residual)
    final_in = (norm_final * (1.0 + fscale) + fshift).astype(bf16)
    predicted = input_back(final_in, weight("output")) + out_bias
    grad_pred = ((predicted - noise) * valid).astype(bf16)
    sums["output"] = weight_grad(grad_pred, final_in)
    sums["out_bias"] = jnp.sum(grad_pred.astype(f32), axis=0, keepdims=True)
    grad_final_in = product(grad_pred, weight("output"))
    out["fshift"] = grad_final_in.astype(bf16)
    out["fscale"] = (grad_final_in * norm_final).astype(bf16)
    grad_residual = norm_back(grad_final_in * (1.0 + fscale), norm_final, inv_final)
    out["two"] = (grad_residual * gate).astype(bf16)
    grad_one = input_back(out["two"], weight("two")) * silu_slope(inner_one)
    out["one"] = grad_one.astype(bf16)
    grad_mlp_in = input_back(out["one"], weight("one"))
    out["shift"] = grad_mlp_in.astype(bf16)
    out["scale"] = (grad_mlp_in * affine).astype(bf16)
    out["gate"] = (grad_residual * inner_two).astype(bf16)
    grad_gated = input_back(out["shift"], weight("shift"))
    for name in ("scale", "gate", "fshift", "fscale"):
        grad_gated = grad_gated + input_back(out[name], weight(name))
    grad_cond = grad_gated * silu_slope(cond)
    out["cond"] = grad_cond.astype(bf16)
    out["condition"] = input_back(out["cond"], weight("cond")).astype(bf16)
    grad_affine = grad_mlp_in * (1.0 + scale)
    grad_entry = grad_residual + norm_back(grad_affine * gain, norm_head, inv_head)
    grad_entry = grad_entry.astype(bf16)
    sums["input"] = weight_grad(noisy, grad_entry)
    sums["gain"] = jnp.sum(grad_affine * norm_head, axis=0, keepdims=True)
    sums["entry"] = jnp.sum(grad_entry.astype(f32), axis=0, keepdims=True)
    sums["affine"] = jnp.sum(grad_affine, axis=0, keepdims=True)
    lanes = lax.broadcasted_iota(jnp.int32, (slot.shape[0], embedded.shape[0]), 1)
    onehot = (slot == lanes).astype(bf16)
    low_part = (grad_cond - out["cond"].astype(f32)).astype(bf16)
    sums["embedded"] = weight_grad(onehot, out["cond"]) + weight_grad(onehot, low_part)
    return out, sums


SQUARES = ("shift", "scale", "gate", "time2", "one", "two", "fshift", "fscale")
HEAD_OUT = (
    "gated", "mlp_in", "inner_act", "fshift", "fscale", "two", "one", "shift", "scale", "gate",
    "cond",
)
HEAD_SUMS = (
    ("input", CHANNELS), ("output", CHANNELS), ("embedded", 8), ("gain", 1), ("entry", 1),
    ("affine", 1), ("out_bias", 1),
)


def head_kernel(pack, w_cond, w_input, w_output, head_bias, gain, out_bias, embedded, values, k, cut):
    rows = values[0].shape[0]
    micros, own = cut
    step = rows // micros
    world = pack.shape[0]
    used = [i for i, name in enumerate(SQUARES) if name != "time2"]
    height = sum(n for _, n in HEAD_SUMS)
    height += -height % 8
    smalls = [w_cond, w_input, w_output, head_bias, gain, out_bias, embedded]

    def body(*refs):
        ins = refs[: len(smalls)]
        pack_ref = refs[len(smalls)]
        tiles = refs[len(smalls) + 1 :][:4]
        outs = refs[len(smalls) + 5 :][: len(HEAD_OUT)]
        rest = refs[len(smalls) + 5 + len(HEAD_OUT) :]
        chunks, (sums_ref, buffer, sems) = rest[:-3], rest[-3:]
        first = pl.program_id(0) == 0

        def fetch(n):
            return pltpu.make_async_copy(
                pack_ref.at[:, pl.ds(used[n] * k, k)], buffer.at[n], sems.at[n]
            )

        @pl.when(first)
        def _():
            for n in range(len(used)):
                fetch(n).start()

        ready = set()

        def weight(name):
            if name in ("cond", "input", "output"):
                return ins[("cond", "input", "output").index(name)][...]
            n = used.index(SQUARES.index(name))
            if n not in ready:
                ready.add(n)

                @pl.when(first)
                def _():
                    fetch(n).wait()

            return buffer[n].reshape(WIDTH, WIDTH)

        out, sums = head_step(
            weight,
            lambda i: ins[3][i : i + 1],
            ins[4][...],
            ins[5][...],
            ins[6][...],
            [t[...] for t in tiles],
        )
        for name, ref in zip(HEAD_OUT, outs):
            ref[...] = out[name]
        for n, ref in enumerate(chunks):
            ref[0] = out["condition"][n * own : (n + 1) * own]

        @pl.when(first)
        def _():
            sums_ref[...] = jnp.zeros((height, WIDTH), jnp.float32)

        at = 0
        for name, n in HEAD_SUMS:
            width = sums[name].shape[1]
            sums_ref[at : at + n, :width] += sums[name]
            at += n

    def tall(width):
        return pl.BlockSpec((step, width), lambda i: (i, 0))

    count = step // own
    *outs, sums = pl.pallas_call(
        body,
        grid=(rows // step,),
        out_shape=[low_shape(rows, WIDTH)] * len(HEAD_OUT)
        + [low_shape(micros, own, D)] * count
        + [jax.ShapeDtypeStruct((height, WIDTH), jnp.float32)],
        in_specs=[
            pl.BlockSpec(v.shape, lambda i: (0, 0), pipeline_mode=pl.Buffered(1)) for v in smalls
        ]
        + [pl.BlockSpec(memory_space=pl.ANY)]
        + [tall(v.shape[1]) for v in values],
        out_specs=[tall(WIDTH)] * len(HEAD_OUT)
        + [pl.BlockSpec((1, own, D), lambda i: (i, 0, 0))] * count
        + [pl.BlockSpec((height, WIDTH), lambda i: (0, 0))],
        scratch_shapes=[
            pltpu.VMEM((len(used), world, k, WIDTH), jnp.bfloat16),
            pltpu.SemaphoreType.DMA((len(used),)),
        ],
        compiler_params=pltpu.CompilerParams(vmem_limit_bytes=60 * MIB),
        cost_estimate=cost(45.0),
    )(*smalls, pack, *values)
    return dict(zip(HEAD_OUT, outs)), outs[len(HEAD_OUT) :], sums


def pack_block_grads(pairs, core, dp_size):
    count = dp_size // 2
    half = D // 2
    packs = []
    for c in (1 - core, core):
        parts = []
        for left_side, right_side in pairs:
            for at in range(0, right_side.shape[1], D):
                part = lax.dynamic_slice_in_dim(right_side, at + c * half, half, 1)
                part = product(left_side, part).astype(jnp.bfloat16)
                parts.append(part.reshape(count, 2, -1, half))
        packs.append(jnp.concatenate(parts, axis=2))
    return packs


def put_halves(first, sent, kept, at_row, whole):
    half = D // 2
    count = sent.shape[0]
    n = whole.shape[0] // (2 * count)
    left, right = whole[:, :half], whole[:, half:]
    for out, part in (
        (sent, jnp.where(first, right, left)),
        (kept, jnp.where(first, left, right)),
    ):
        part = part.reshape(count, 2, n, half).astype(jnp.bfloat16)
        out[:, :, at_row : at_row + n] = part


def feed_forward(second_in, middle, ups, up_bias, w_down, down_bias, place, copy_size, kernels):
    bf16, f32 = jnp.bfloat16, jnp.float32
    rows = middle.shape[0]
    steps = len(ups)

    def step_of(hidden):
        half = 0.5 * (1.0 + lax.erf(hidden * 2.0 ** (-0.5)))
        bell = jnp.exp(-0.5 * hidden * hidden) * (2.0 * math.pi) ** (-0.5)
        return (hidden * half).astype(bf16), (half + hidden * bell).astype(bf16)

    if not kernels:
        hidden = product(second_in, jnp.concatenate(ups, axis=1)) + up_bias
        active, slope = step_of(hidden)
        output = middle + product(active, w_down) + down_bias
        return output.astype(bf16), slope, None, active

    per = w_down.shape[0] // steps
    k = per // (2 * copy_size)
    width = per // copy_size

    def body(at, *refs):
        up_refs, refs = refs[:steps], refs[steps:]
        in_ref, middle_ref, bias_ref, down_ref, down_bias_ref = refs[:5]
        out_ref, slope_ref, chosen_ref, total, hidden = refs[5:]
        step = pl.program_id(0)
        for n in range(steps):

            @pl.when(step == n)
            def _():
                hidden[...] = product(in_ref[...], up_refs[n][...])

        active, slope = step_of(hidden[...] + bias_ref[...])
        slope_ref[...] = slope
        part = product(active, down_ref[...])
        source = lax.broadcasted_iota(jnp.int32, (width, per), 1)
        target = lax.broadcasted_iota(jnp.int32, (width, per), 0)
        wanted = (target // k * copy_size + at[0]) * k + target % k
        one_hot = (source == wanted).astype(bf16)
        chosen_ref[0] = dot1(one_hot, active).astype(bf16)

        @pl.when(step == 0)
        def _():
            total[...] = middle_ref[...] + down_bias_ref[...] + part

        @pl.when(step > 0)
        def _():
            total[...] += part

        @pl.when(step == steps - 1)
        def _():
            out_ref[...] = total[...].astype(bf16)

    def full(v):
        return pl.BlockSpec(v.shape, lambda j: (0,) * len(v.shape), pipeline_mode=pl.Buffered(1))

    out, slope, chosen = pl.pallas_call(
        body,
        grid=(steps,),
        out_shape=[low_shape(rows, D), low_shape(rows, per * steps), low_shape(steps, width, rows)],
        in_specs=[pl.BlockSpec(memory_space=pltpu.SMEM)]
        + [full(v) for v in (*ups, second_in, middle)]
        + [
            pl.BlockSpec((1, per), lambda j: (0, j)),
            pl.BlockSpec((per, D), lambda j: (j, 0)),
            full(down_bias),
        ],
        out_specs=[
            pl.BlockSpec((rows, D), lambda j: (0, 0)),
            pl.BlockSpec((rows, per), lambda j: (0, j)),
            pl.BlockSpec((1, width, rows), lambda j: (j, 0, 0)),
        ],
        scratch_shapes=[pltpu.VMEM((rows, D), f32), pltpu.VMEM((rows, per), f32)],
        compiler_params=pltpu.CompilerParams(vmem_limit_bytes=48 * MIB),
        cost_estimate=cost(18.0),
    )(place[None], *ups, second_in, middle, up_bias, w_down, down_bias)
    return out, slope, chosen, None


def block_back_one(pieces, slope, ups, w_down, w_proj, lefts, norm, inverse, gain, core, dp_size, kernels):
    bf16, f32 = jnp.bfloat16, jnp.float32
    micros, own, _ = pieces[0].shape
    rows = micros * own * len(pieces)
    steps = len(ups)
    k = lefts[0].shape[0] // dp_size
    k_down = w_down.shape[0] // (dp_size * len(pieces))
    if not kernels:
        grad = jnp.stack(pieces, axis=1).reshape(rows, D)
        hidden = (input_back(grad, w_down) * slope.astype(f32)).astype(bf16)
        second = input_back(hidden, jnp.concatenate(ups, axis=1))
        middle = grad.astype(f32) + norm_back(second * gain, norm, inverse)
        low = middle.astype(bf16)
        sums = [jnp.sum(second * norm, axis=0), jnp.sum(second, axis=0)]
        sums = jnp.stack(sums + [column_sum(low), column_sum(grad)])
        packs = pack_block_grads([(lefts[0], hidden), (lefts[1], grad)], core, dp_size)
        mixed = input_back(low, w_proj).astype(bf16)
        return *packs, middle, low, mixed, sums, column_sum(hidden).reshape(steps, 1, D)

    def body(at, *refs):
        piece_refs, refs = refs[: len(pieces)], refs[len(pieces) :]
        up_refs, refs = refs[:steps], refs[steps:]
        slope_ref, down_ref, proj_ref, left_up, left_down, norm_ref, inv_ref, gain_ref = refs[:8]
        sent, kept, middle_ref, low_ref, mixed_ref, sums_ref, hidden_sums, grad, total = refs[8:]
        step = pl.program_id(0)
        first = at[0] == 0

        @pl.when(step == 0)
        def _():
            for m in range(micros):
                for n, ref in enumerate(piece_refs):
                    start = (m * len(pieces) + n) * own
                    grad[start : start + own] = ref[m]
            for n in range(steps):
                here = pl.ds(n * dp_size // (2 * steps), dp_size // (2 * steps))
                part = product(left_down[n], grad[...])
                put_halves(first, sent.at[here], kept.at[here], steps * k, part)
            total[...] = jnp.zeros_like(total)

        hidden = dot1(grad[...], down_ref[...]) * slope_ref[...].astype(f32)
        hidden = hidden.astype(bf16)
        ones = jnp.ones((8, rows), bf16)
        hidden_sums[0] = jnp.dot(ones, hidden, preferred_element_type=f32)
        up_grad = product(left_up[...], hidden)
        for n in range(steps):

            @pl.when(step == n)
            def _():
                total[...] += dot1(hidden, up_refs[n][...])
                put_halves(first, sent, kept, n * k, up_grad)

        @pl.when(step == steps - 1)
        def _():
            second, norm_now = total[...], norm_ref[...]
            given = grad[...].astype(f32)
            middle = given + norm_back(second * gain_ref[...], norm_now, inv_ref[...])
            low = middle.astype(bf16)
            middle_ref[...] = middle
            low_ref[...] = low
            mixed_ref[...] = dot1(low, proj_ref[...]).astype(bf16)
            for n, values in enumerate((second * norm_now, second, low.astype(f32), given)):
                sums_ref[n : n + 1] = jnp.sum(values, axis=0, keepdims=True)

    def full(v):
        return pl.BlockSpec(v.shape, lambda j: (0,) * len(v.shape), pipeline_mode=pl.Buffered(1))

    pack = low_shape(dp_size // 2, 2, steps * k + k_down, D // 2)
    tall = jax.ShapeDtypeStruct((rows, D), f32)
    outs = [pack, pack, tall, low_shape(rows, D), low_shape(rows, D)]
    outs += [jax.ShapeDtypeStruct((8, D), f32)]
    ins = [*pieces, *ups, slope, w_down, w_proj, *lefts, norm, inverse, gain]
    in_specs = [full(v) for v in ins]
    in_specs[len(pieces) + steps] = pl.BlockSpec((rows, D), lambda j: (0, j))
    in_specs[len(pieces) + steps + 1] = pl.BlockSpec((D, D), lambda j: (j, 0))
    return pl.pallas_call(
        body,
        grid=(steps,),
        out_shape=outs + [jax.ShapeDtypeStruct((steps, 8, D), f32)],
        in_specs=[pl.BlockSpec(memory_space=pltpu.SMEM)] + in_specs,
        out_specs=[pl.BlockSpec(v.shape, lambda j, n=len(v.shape): (0,) * n) for v in outs]
        + [pl.BlockSpec((1, 8, D), lambda j: (j, 0, 0))],
        scratch_shapes=[pltpu.VMEM((rows, D), bf16), pltpu.VMEM((rows, D), f32)],
        compiler_params=pltpu.CompilerParams(vmem_limit_bytes=60 * MIB),
        cost_estimate=cost(24.0),
    )(jnp.asarray(core, jnp.int32)[None], *ins)


def block_back_two(grads, weights, lefts, low, middle, norm, inverse, gain, sums, hidden_sums, own, micros, core, dp_size, kernels):
    f32 = jnp.float32
    rows = low.shape[0]
    length = rows // micros
    steps = hidden_sums.shape[0]

    def smalls(first, norm_now, q, v):
        return [
            jnp.sum(first * norm_now, axis=0, keepdims=True),
            None,
            jnp.sum(first, axis=0, keepdims=True),
            jnp.sum(q.astype(f32), axis=0, keepdims=True),
            jnp.sum(v.astype(f32), axis=0, keepdims=True),
        ]

    if not kernels:
        first = sum(input_back(g, w) for g, w in zip(grads, weights))
        input_grad = middle + norm_back(first * gain, norm, inverse)
        input_grad = input_grad.reshape(micros, length, D)[:, :own]
        rows_of = smalls(first, norm, grads[0], grads[2])
        rows_of[1] = sums[:1]
        small = jnp.concatenate([*rows_of, sums[2:3], sums[1:2], sums[3:4], hidden_sums[:, 0]])
        pairs = [(lefts[0], g) for g in grads] + [(lefts[1], low)]
        return *pack_block_grads(pairs, core, dp_size), input_grad, small

    k = lefts[0].shape[0] // dp_size

    def body(at, *refs):
        grad_refs, weight_refs, refs = refs[:3], refs[3:6], refs[6:]
        left_in, left_mixed, low_ref, middle_ref, norm_ref, inv_ref, gain_ref = refs[:7]
        sums_ref, hidden_ref, sent, kept, out_ref, small_ref = refs[7:]
        flag = at[0] == 0
        for n, ref in enumerate(grad_refs):
            put_halves(flag, sent, kept, n * k, product(left_in[...], ref[...]))
        put_halves(flag, sent, kept, 3 * k, product(left_mixed[...], low_ref[...]))
        first = dot1(grad_refs[0][...], weight_refs[0][...])
        for g, w in zip(grad_refs[1:], weight_refs[1:]):
            first = first + dot1(g[...], w[...])
        for n, value in enumerate(
            smalls(first, norm_ref[...], grad_refs[0][...], grad_refs[2][...])
        ):
            if value is not None:
                small_ref[n : n + 1] = value
        small_ref[1:2] = sums_ref[0:1]
        small_ref[5:6] = sums_ref[2:3]
        small_ref[6:7] = sums_ref[1:2]
        small_ref[7:8] = sums_ref[3:4]
        for n in range(steps):
            small_ref[8 + n : 9 + n] = hidden_ref[n, 0:1]
        for m in range(micros):
            here = pl.ds(m * length, own)
            back = norm_back(
                first[m * length : m * length + own] * gain_ref[...], norm_ref[here], inv_ref[here]
            )
            out_ref[m] = middle_ref[here] + back

    pack = low_shape(dp_size // 2, 2, 4 * k, D // 2)
    outs = [pack, pack, jax.ShapeDtypeStruct((micros, own, D), f32)]
    outs += [jax.ShapeDtypeStruct((8 + steps, D), f32)]
    ins = [*grads, *weights, *lefts, low, middle, norm, inverse, gain, sums, hidden_sums]
    return small_call(body, outs, [core], ins)


def shards(
    block_input,
    image_ids,
    latents,
    noise,
    timesteps,
    norm_gains,
    block_biases,
    w_qkv,
    w_proj,
    w_up,
    up_bias,
    w_down,
    head_gain,
    head_biases,
    w_cond,
    w_time1,
    w_time2,
    w_input,
    w_ada,
    w_mlp1,
    w_mlp2,
    w_final,
    w_output,
    output_bias,
):
    bf16, f32 = jnp.bfloat16, jnp.float32
    dp_size, copy_size = lax.axis_size("dp"), lax.axis_size("copy")
    world = dp_size * copy_size
    place = lax.axis_index("copy")
    micros, _, own, _ = block_input.shape
    length = image_ids.shape[2]
    total = micros * length
    k_d, k_ff, k_w, k_t = D // world, w_down.shape[0], WIDTH // world, w_time1.shape[0]
    ff = k_ff * world
    kernels = k_d % 8 == 0 and k_w % 16 == 0 and k_t % 8 == 0
    score_scale = HEAD_DIM ** (-0.5)

    def cut(matrix, width):
        return [matrix[:, i : i + width] for i in range(0, matrix.shape[1], width)]

    def pad_flat(parts, width):
        flat = jnp.concatenate([padded_lanes(p) for p in parts])
        count = -(-flat.shape[0] // (16 * width)) * 16 * width
        return jnp.pad(flat, (0, count - flat.shape[0])).reshape(-1, width)

    groups = [
        (cut(w_qkv, D) + [w_proj, pad_flat([norm_gains, block_biases, up_bias[None]], D)], 2),
        (cut(w_up, D) + [w_down], 4),
        (
            cut(w_ada, WIDTH)
            + [w_time2, w_mlp1, w_mlp2]
            + cut(w_final, WIDTH)
            + [w_cond, w_time1]
            + [pad_flat([w_input, w_output.T, head_gain[None], head_biases], WIDTH)],
            0,
        ),
    ]

    def everyone(pack):
        return [shift_copy(pack, copy_size, copy_size - j) for j in range(1, copy_size)]

    def unpack(pack, parts):
        out, at = [], 0
        for part in parts:
            out.append(pack[:, at : at + part.shape[0]].reshape(-1, pack.shape[2]))
            at += part.shape[0]
        return out

    own_rows = block_input[:, 0]
    if kernels:
        square = range(3)
        packs = [
            lay(
                [w_qkv, w_proj, norm_gains, block_biases, up_bias[None]],
                (4 * k_d + 16, D),
                [(0, 0, i * D, k_d, D, i * k_d) for i in square] + [(1, 0, 0, k_d, D, 3 * k_d)],
                [(2, False), (3, False), (4, False)],
            ),
            lay(
                [w_up, w_down],
                (ff // D * k_d + k_ff, D),
                [(0, 0, i * D, k_d, D, i * k_d) for i in range(ff // D)]
                + [(1, 0, 0, k_ff, D, ff // D * k_d)],
                [],
            ),
            lay(
                [w_ada, w_time2, w_mlp1, w_mlp2, w_final, w_cond, w_time1]
                + [w_input, w_output, head_gain[None], head_biases],
                (8 * k_w + k_d + k_t + 16, WIDTH),
                [(0, 0, i * WIDTH, k_w, WIDTH, i * k_w) for i in square]
                + [(i, 0, 0, k_w, WIDTH, (2 + i) * k_w) for i in (1, 2, 3)]
                + [(4, 0, i * WIDTH, k_w, WIDTH, (6 + i) * k_w) for i in range(2)]
                + [(5, 0, 0, k_d, WIDTH, 8 * k_w), (6, 0, 0, k_t, WIDTH, 8 * k_w + k_d)],
                [(7, False), (8, True), (9, False), (10, False)],
            ),
        ]
    else:
        packs = [jnp.concatenate(parts, 0) for parts, _ in groups]
    if kernels and dp_size == 8 and copy_size == 4:
        head_own = packs[2]
        arrived = [everyone(packs[0])]
        *arrived[0], packs[1] = tie(*arrived[0], packs[1])
        arrived.append(everyone(packs[1]))
        *arrived[1], own_rows, head_own = tie(*arrived[1], own_rows, head_own)
        rows_arrived = everyone(own_rows)
        full = [
            gather(pack, sum(p.shape[0] for p in parts[:n]), got)
            for pack, (parts, n), got in zip(packs[:2], groups[:2], arrived[:2])
        ]
        head = lax.all_gather(head_own, ("dp", "copy"), axis=0)
        full.append(head)
    else:
        rows_arrived = everyone(own_rows)
        full = [lax.all_gather(pack, ("dp", "copy"), axis=0) for pack in packs]
    head_pack = full[2]
    full = [unpack(pack, parts) for pack, (parts, _) in zip(full, groups)]

    rows = jnp.stack([own_rows, *rows_arrived], axis=1).reshape(total, D).astype(f32)

    def turned(values):
        twice = jnp.concatenate([values, values], axis=1)
        return lax.dynamic_slice_in_dim(twice, place * own, length, 1)

    ids = turned(image_ids[:, 0])
    latent_rows = turned(latents[:, 0]).reshape(total, CHANNELS)
    noise_rows = turned(noise[:, 0, 0]).reshape(total, CHANNELS)

    w_q, w_k, w_v, w_proj_full, small = full[0]
    w_down_full = full[1][4]
    small = small.reshape(world, -1)
    gains, biases, up_bias_full = spread(small, [(2, k_d), (6, k_d), (1, k_ff)])

    norm_one, inv_one = normalize(rows)
    first_in = (norm_one * gains[0] + biases[0]).astype(bf16)
    queries = (product(first_in, w_q) + biases[1]).astype(bf16)
    key_rows = product(first_in, w_k).astype(bf16)
    value_rows = (product(first_in, w_v) + biases[2]).astype(bf16)
    mixed = attention(queries, key_rows, value_rows, ids)
    middle = rows + product(mixed, w_proj_full) + biases[3]
    norm_two, inv_two = normalize(middle)
    second_in = (norm_two * gains[1] + biases[4]).astype(bf16)
    condition, slope, active_z, active = feed_forward(
        second_in,
        middle,
        full[1][:4],
        up_bias_full,
        w_down_full,
        biases[5:6],
        place,
        copy_size,
        kernels,
    )

    def chosen(values):
        width = values.shape[1]
        k = width // world
        source = jnp.arange(width, dtype=jnp.int32)[None, :]
        target = jnp.arange(dp_size * k, dtype=jnp.int32)[:, None]
        wanted = (target // k * copy_size + place) * k + target % k
        return input_back((source == wanted).astype(bf16), values).astype(bf16)

    condition, first_z, mixed_z, second_z, active_z, slope, norm_one, inv_one, norm_two, inv_two = tie(
        condition,
        chosen(first_in),
        chosen(mixed),
        chosen(second_in),
        chosen(active) if active_z is None else active_z,
        slope,
        norm_one,
        inv_one,
        norm_two,
        inv_two,
    )
    core = lax.axis_index("dp") & 1

    def split_pack(pack, parts):
        out, at = [], 0
        for rows_of in parts:
            out.append(pack[at : at + rows_of])
            at += rows_of
        return out

    def after(first, *values):
        first = list(first)
        return list(tie(*first, *values)[len(first) :])

    def send_after(reduction, first):
        reduction.sent = after(first, *reduction.sent)
        return reduction.receive()

    def form_after(reduction, first):
        reduction.got = after(first, *reduction.got)
        reduction.advance()
        return [*reduction.sent, *reduction.kept]

    def to_copies(reduction, first):
        reduction.got = after(first, *reduction.got)
        chunks = cut_copies(reduction.kept, reduction.got, place, copy_size, kernels)
        arriving = [shift_copy(chunks[j], copy_size, j) for j in range(1, copy_size)]
        return [chunks[0], *arriving]

    def whole(other, mine):
        got = swap_bit(other, dp_size, 0)
        left = jnp.where(core == 0, mine, got)
        right = jnp.where(core == 0, got, mine)
        return jnp.concatenate([left, right], axis=1).astype(f32)

    def finish(reduction):
        while reduction.left:
            reduction.advance().receive()
        parts = [
            jnp.concatenate([v[0] for v in values], axis=1)
            for values in (reduction.kept, reduction.got)
        ]
        return whole(*own_and_other(parts, (0, core), kernels))

    squares = dict(zip(SQUARES, full[2][:8]))
    w_cond_full, w_time1_full, small = full[2][8:]
    w_time2_full = squares["time2"]
    small = small.reshape(world, -1)
    w_input_full, w_output_t, head_gain_f, head_bias = spread(
        small, [(CHANNELS, k_w), (CHANNELS, k_w), (1, k_w), (12, k_w)]
    )
    w_input_full, w_output_t = w_input_full.astype(bf16), w_output_t.astype(bf16)

    row_slot = ids + IMAGES * jnp.arange(micros, dtype=jnp.int32)[:, None]
    row_slot = jnp.where(ids >= 0, row_slot, -1).reshape(total, 1)
    step_vals = timesteps[:, 0, 0].reshape(micros * IMAGES).astype(f32)
    sinusoid_in = sinusoid(step_vals).astype(bf16)
    time_one = product(sinusoid_in, w_time1_full) + head_bias[1]
    time_act = jax.nn.silu(time_one).astype(bf16)
    embedded = product(time_act, w_time2_full) + head_bias[2]
    factors = plan(step_vals)
    slots = jnp.arange(micros * IMAGES, dtype=jnp.int32)[None, :]
    mixing = [
        jnp.sum(jnp.where(row_slot == slots, factors[None, :, i], 0.0), axis=1, keepdims=True)
        for i in range(2)
    ]
    noisy = (latent_rows * mixing[0] + noise_rows * mixing[1]).astype(bf16)
    values = (condition, noisy, noise_rows, row_slot)
    out_bias = output_bias.astype(f32)[None]
    if kernels:
        out, chunks, sums = head_kernel(
            head_pack,
            w_cond_full,
            w_input_full,
            w_output_t,
            head_bias,
            head_gain_f,
            out_bias,
            embedded,
            values,
            k_w,
            (micros, own),
        )
    else:
        others = {"cond": w_cond_full, "input": w_input_full, "output": w_output_t, **squares}
        out, sums = head_step(
            others.get,
            lambda i: head_bias[i : i + 1],
            head_gain_f,
            out_bias,
            embedded,
            values,
        )
        chunks = out["condition"].reshape(micros, copy_size, own, D)
        chunks = [chunks[:, j] for j in range(copy_size)]
        sums = [jnp.pad(sums[n], ((0, 0), (0, WIDTH - sums[n].shape[1]))) for n, _ in HEAD_SUMS]
        sums = jnp.concatenate(sums)
        sums = jnp.pad(sums, ((0, -sums.shape[0] % 8), (0, 0)))
    at_embedded = 2 * CHANNELS
    grad_embedded = sums[at_embedded : at_embedded + micros * IMAGES].astype(bf16)
    grad_time_one = (input_back(grad_embedded, w_time2_full) * silu_slope(time_one)).astype(bf16)
    arriving = [shift_copy(chunks[j], copy_size, j) for j in range(1, copy_size)]
    (gated,) = after(chunks, out["gated"])
    send, keep, sums_one = pack_head_grads(
        [
            (gated, out["fshift"]),
            (gated, out["fscale"]),
            (out["inner_act"], out["two"]),
            (out["mlp_in"], out["one"]),
        ],
        core,
        dp_size,
        copy_size,
        kernels,
    )
    pack_one = Reduction([send], [keep], 2 * k_w, dp_size, kernels)
    arriving = after([keep], *arriving)
    grad_z_own = sum_low([chunks[0], *arriving], kernels)
    arriving = [shift_copy(grad_z_own, copy_size, copy_size - j) for j in range(1, copy_size)]
    send_after(pack_one, [grad_z_own])
    (gated,) = after([grad_z_own], gated)
    of_head = 2 * CHANNELS + 8
    send, keep, small_grads = pack_head_grads(
        [
            (gated, out["shift"]),
            (gated, out["scale"]),
            (gated, out["gate"]),
            (time_act, grad_embedded),
            (condition, out["cond"]),
            (sinusoid_in, grad_time_one),
        ],
        core,
        dp_size,
        copy_size,
        kernels,
        (sums_one, sums),
        (
            (2, 0, 2 * CHANNELS),
            (2, of_head, 1),
            (0, 4, 2),
            (0, 3, 1),
            (2, of_head + 1, 2),
            (1, 3, 1),
            (1, 2, 1),
            (0, 0, 3),
            (1, 0, 2),
            (2, of_head + 3, 1),
            (2, of_head + 4, 2),
        ),
    )
    pack_two = Reduction([send], [keep], 3 * k_w, dp_size, kernels)
    formed = form_after(pack_one, [keep])
    arriving = after(formed, *arriving)
    send_after(pack_one, arriving)
    send_after(pack_two, arriving)

    def swap_copies(values, shift, first):
        return values + after(first, swap_copy(values, copy_size, shift))[0]

    send, keep, grad_middle, grad_branch, grad_mixed, block_sums, hidden_sums = block_back_one(
        [grad_z_own, *arriving],
        slope,
        full[1][:4],
        w_down_full,
        w_proj_full,
        (second_z, active_z),
        norm_two,
        inv_two,
        gains[1:2],
        core,
        dp_size,
        kernels,
    )
    sent, kept = [send], [keep]
    formed = form_after(pack_one, [grad_mixed])
    send_after(pack_one, formed)
    small_grads = swap_copies(small_grads, 1, formed)
    formed = form_after(pack_two, [small_grads])
    send_after(pack_two, formed)
    (grad_mixed,) = after(formed, grad_mixed)
    back = attention_back(queries, key_rows, value_rows, grad_mixed, ids, 0, None)
    pack_one.got = after(back, *pack_one.got)
    send, one_half = cut_copy_halves(pack_one.kept, pack_one.got, place, copy_size, kernels)
    one_got = swap_copy(send, copy_size, copy_size // 2)
    small_grads = swap_copies(small_grads, 2, [one_half])
    (grad_mixed,) = after([small_grads], grad_mixed)
    for m in range(1, micros):
        back = attention_back(queries, key_rows, value_rows, grad_mixed, ids, m, back)
    formed = form_after(pack_two, back)
    send_after(pack_two, formed)
    (one_got,) = after(formed, one_got)
    send, one_last = cut_copy_last(one_half, one_got, place, kernels)
    one_got = swap_copy(send, copy_size, 1)
    back = after([one_last], *back)
    send, keep, input_grad, block_small = block_back_two(
        back,
        (w_q, w_k, w_v),
        (first_z, mixed_z),
        grad_branch,
        grad_middle,
        norm_one,
        inv_one,
        gains[:1],
        block_sums,
        hidden_sums,
        own,
        micros,
        core,
        dp_size,
        kernels,
    )
    sent, kept = sent + [send], kept + [keep]
    pack_three = Reduction(sent, kept, 6 * k_d, dp_size, kernels)
    two_parts = to_copies(pack_two, [keep])
    (one_got,) = after([two_parts[0]], one_got)
    own_one_parts = own_and_other([one_last, one_got], (0, core), kernels)
    send_after(pack_three, own_one_parts)
    head_rows = small_grads.shape[0]
    block_small = jnp.pad(block_small, ((0, -block_small.shape[0] % 8), (0, WIDTH - D)))
    small_grads = jnp.concatenate([small_grads, block_small], axis=0)
    everywhere = lax.all_gather(small_grads, "dp", axis=0)
    small_grads = everywhere[0]
    for n in range(1, dp_size):
        small_grads = small_grads + everywhere[n]
    block_small = small_grads[head_rows:, :D]
    formed = form_after(pack_three, own_one_parts)
    send_after(pack_three, formed)
    while pack_three.left:
        formed = form_after(pack_three, [two_parts[0]])
        send_after(pack_three, formed)
    two_parts = after(formed, *two_parts)
    own_two_parts = own_and_other(two_parts, (place, core), kernels)
    own_all = finish(pack_three)
    own_up = jnp.concatenate(split_pack(own_all, [k_d] * 4), axis=1)
    own_down = own_all[4 * k_d : 4 * k_d + k_ff]
    own_four = own_all[4 * k_d + k_ff :]
    own_q, own_k, own_v, own_proj = split_pack(own_four, [k_d] * 4)
    own_fshift, own_fscale, own_two, own_one = split_pack(
        whole(*own_one_parts), [k_w] * 4
    )
    own_shift, own_scale, own_gate, own_time2, own_cond, own_time1 = split_pack(
        whole(*own_two_parts), [k_w] * 4 + [k_d, k_t]
    )
    me = lax.axis_index("dp") * copy_size + place
    own_rest = lax.dynamic_slice_in_dim(block_small[:8], me * k_d, k_d, 1)
    own_gains, own_biases = own_rest[:2], own_rest[2:]
    own_up_bias = lax.dynamic_slice_in_dim(block_small[8 : 8 + ff // D].reshape(ff), me * k_ff, k_ff)
    own_small = lax.dynamic_slice_in_dim(small_grads, me * k_w, k_w, 1)
    own_w_input = own_small[:CHANNELS]
    own_w_output = own_small[CHANNELS : 2 * CHANNELS].T
    own_head_gain = own_small[2 * CHANNELS]
    own_head_biases = own_small[2 * CHANNELS + 1 : 2 * CHANNELS + 13]
    grad_out_bias = small_grads[2 * CHANNELS + 13, :CHANNELS]

    input_grad = input_grad.reshape(micros, 1, own, D)
    block_output = condition.reshape(micros, length, D)[:, :own].reshape(micros, 1, own, D)
    return (
        block_output,
        input_grad,
        own_gains,
        own_biases,
        jnp.concatenate([own_q, own_k, own_v], axis=1),
        own_proj,
        own_up,
        own_up_bias,
        own_down,
        own_head_gain,
        own_head_biases,
        own_cond,
        own_time1,
        own_time2,
        own_w_input,
        jnp.concatenate([own_shift, own_scale, own_gate], axis=1),
        own_one,
        own_two,
        jnp.concatenate([own_fshift, own_fscale], axis=1),
        own_w_output,
        grad_out_bias,
    )


def solution(mesh):
    in_specs = (
        P(None, "dp", "copy", None),
        P(None, "dp", None),
        P(None, "dp", None, None),
        P(None, "copy", "dp", None, None),
        P(None, "copy", "dp", None),
        P(None, ("dp", "copy")),
        P(None, ("dp", "copy")),
        P(("dp", "copy"), None),
        P(("dp", "copy"), None),
        P(("dp", "copy"), None),
        P(("dp", "copy")),
        P(("dp", "copy"), None),
        P(("dp", "copy")),
        P(None, ("dp", "copy")),
        P(("dp", "copy"), None),
        P(("dp", "copy"), None),
        P(("dp", "copy"), None),
        P(None, ("dp", "copy")),
        P(("dp", "copy"), None),
        P(("dp", "copy"), None),
        P(("dp", "copy"), None),
        P(("dp", "copy"), None),
        P(("dp", "copy"), None),
        P(),
    )
    out_specs = (
        P(None, "dp", "copy", None),
        P(None, "dp", "copy", None),
        P(None, ("dp", "copy")),
        P(None, ("dp", "copy")),
        P(("dp", "copy"), None),
        P(("dp", "copy"), None),
        P(("dp", "copy"), None),
        P(("dp", "copy")),
        P(("dp", "copy"), None),
        P(("dp", "copy")),
        P(None, ("dp", "copy")),
        P(("dp", "copy"), None),
        P(("dp", "copy"), None),
        P(("dp", "copy"), None),
        P(None, ("dp", "copy")),
        P(("dp", "copy"), None),
        P(("dp", "copy"), None),
        P(("dp", "copy"), None),
        P(("dp", "copy"), None),
        P(("dp", "copy"), None),
        P(),
    )
    return jax.shard_map(shards, mesh=mesh, in_specs=in_specs, out_specs=out_specs, check_vma=False)
```

```python
import functools
import math

import jax
import jax.numpy as jnp
from jax import lax
from jax.experimental import pallas as pl
from jax.experimental.pallas import tpu as pltpu
from jax.sharding import PartitionSpec as P

D = 768
HEADS = 12
HEAD_DIM = 64
WIDTH = 1024
FREQ = 256
CHANNELS = 16
IMAGES = 4


epsilon = 1e-06
highest = lax.Precision.HIGHEST


def product(left_side, right_side):
    return jnp.dot(left_side, right_side, preferred_element_type=jnp.float32)


def weight_grad(left_side, right_side):
    return lax.dot_general(
        left_side, right_side, (((0,), (0,)), ((), ())), preferred_element_type=jnp.float32
    )


def input_back(gradient, weight):
    return lax.dot_general(
        gradient, weight, (((1,), (1,)), ((), ())), preferred_element_type=jnp.float32
    )


def column_sum(values):
    return jnp.sum(values.astype(jnp.float32), axis=0)


def normalize(values):
    center = values - jnp.mean(values, axis=-1, keepdims=True)
    inverse = lax.rsqrt(jnp.mean(center * center, axis=-1, keepdims=True) + epsilon)
    return (center * inverse, inverse)


def norm_back(gradient, normed, inverse):
    return inverse * (
        gradient
        - jnp.mean(gradient, axis=-1, keepdims=True)
        - normed * jnp.mean(gradient * normed, axis=-1, keepdims=True)
    )


def silu_slope(values):
    sigma = jax.nn.sigmoid(values)
    return sigma * (1.0 + values * (1.0 - sigma))


def gelu_slope(values):
    return 0.5 * (1.0 + lax.erf(values * 2.0 ** (-0.5))) + values * jnp.exp(
        -0.5 * values * values
    ) * (2.0 * math.pi) ** (-0.5)


def sinusoid(step_vals):
    half_width = FREQ // 2
    rates = jnp.exp(-math.log(10000.0) * jnp.arange(half_width, dtype=jnp.float32) / half_width)
    angles = step_vals[:, None] * rates[None, :]
    return jnp.concatenate([jnp.cos(angles), jnp.sin(angles)], axis=1)


def plan(step_vals):
    anchor = math.cos(0.008 / 1.008 * math.pi / 2.0) ** 2
    angle_now = ((step_vals + 1.0) / 1000.0 + 0.008) / 1.008 * (math.pi / 2.0)
    signal = jnp.cos(angle_now) ** 2 / anchor
    return jnp.stack([jnp.sqrt(signal), jnp.sqrt(1.0 - signal)], axis=1)


def tdot(left_side, right_side):
    return lax.dot_general(
        left_side, right_side, (((0,), (0,)), ((), ())), preferred_element_type=jnp.float32
    )


def swap_bit(values, size, bit):
    return lax.ppermute(values, "dp", [(i, i ^ (1 << bit)) for i in range(size)])


def shift_copy(values, size, shift):
    return lax.ppermute(values, "copy", [(i, (i + shift) % size) for i in range(size)])


def swap_copy(values, size, shift):
    return lax.ppermute(values, "copy", [(i, i ^ shift) for i in range(size)])


def pick(values, index, axis):
    return lax.dynamic_index_in_dim(values, index, axis, keepdims=False)


def tie(*values):
    return lax.optimization_barrier(values)


MIB = 1 << 20


def cost(microseconds):
    return pl.CostEstimate(
        flops=int(microseconds * 10**9), bytes_accessed=10**5, transcendentals=0
    )


def dot0(left_side, right_side):
    return lax.dot_general(
        left_side, right_side, (((0,), (0,)), ((), ())), preferred_element_type=jnp.float32
    )


def dot1(left_side, right_side):
    return lax.dot_general(
        left_side, right_side, (((1,), (1,)), ((), ())), preferred_element_type=jnp.float32
    )


def small_call(body, outs, scalars, ins):
    size = sum(math.prod(o.shape) * o.dtype.itemsize for o in outs)
    size += sum(math.prod(v.shape) * v.dtype.itemsize for v in ins)
    return pl.pallas_call(
        body,
        out_shape=outs,
        in_specs=[pl.BlockSpec(memory_space=pltpu.SMEM)]
        + [pl.BlockSpec(memory_space=pltpu.VMEM)] * len(ins),
        out_specs=[pl.BlockSpec(memory_space=pltpu.VMEM)] * len(outs),
        compiler_params=pltpu.CompilerParams(vmem_limit_bytes=2 * size + 16 * MIB),
        cost_estimate=cost(size / 2.2e6),
    )(jnp.stack([jnp.asarray(v, jnp.int32) for v in scalars]), *ins)


def low_shape(*dims):
    return jax.ShapeDtypeStruct(dims, jnp.bfloat16)


def add_up(one, two):
    return one.astype(jnp.float32) + two.astype(jnp.float32)


def cut_first(keeps, gots, rows, bits, kernels):
    count, mids, _, width = keeps[0].shape
    half = count // 2
    sizes = [k.shape[2] for k in keeps]
    total = sum(sizes)

    if not kernels:
        sums = jnp.concatenate([add_up(k, g) for k, g in zip(keeps, gots)], axis=2)
        sums = sums.astype(jnp.bfloat16)
        first = sums[:, :, :rows].reshape(2, half, mids, rows, width)
        second = sums[:, :, rows:].reshape(half, 2, mids, total - rows, width)
        return [
            pick(first, 1 - bits[0], 0),
            pick(first, bits[0], 0),
            pick(second, 1 - bits[1], 1),
            pick(second, bits[1], 1),
        ]

    def body(at, *refs):
        keep_refs, got_refs = refs[: len(keeps)], refs[len(keeps) : 2 * len(keeps)]
        outs = refs[2 * len(keeps) :]
        for out, bit, low in zip(outs, (1 - at[0], at[0], 1 - at[1], at[1]), (0, 0, 1, 1)):
            begin, end = (rows, total) if low else (0, rows)
            at_row = 0
            for keep, got, n in zip(keep_refs, got_refs, sizes):
                top, bottom = max(begin, at_row), min(end, at_row + n)
                if top < bottom:
                    cut = pl.ds(top - at_row, bottom - top)
                    for i in range(half):
                        p = 2 * i + bit if low else bit * half + i
                        value = add_up(keep[p, :, cut], got[p, :, cut]).astype(jnp.bfloat16)
                        out[i, :, top - begin : bottom - begin] = value
                at_row += n

    outs = [low_shape(half, mids, n, width) for n in (rows, rows, total - rows, total - rows)]
    return small_call(body, outs, bits, [*keeps, *gots])


def cut_next(keeps, gots, bits, kernels):
    count, mids, _, width = keeps[0].shape
    half = count // 2
    sizes = [k.shape[2] for k in keeps]
    if not kernels:
        sums = [add_up(k, g).astype(jnp.bfloat16) for k, g in zip(keeps, gots)]
        first = sums[0].reshape(2, half, mids, sizes[0], width)
        second = sums[1].reshape(half, 2, mids, sizes[1], width)
        return [
            pick(first, 1 - bits[0], 0),
            pick(first, bits[0], 0),
            pick(second, 1 - bits[1], 1),
            pick(second, bits[1], 1),
        ]

    def body(at, keep_one, got_one, keep_two, got_two, *outs):
        for out, bit, top in zip(outs, (1 - at[0], at[0], 1 - at[1], at[1]), (0, 0, 1, 1)):
            keep, got = (keep_two, got_two) if top else (keep_one, got_one)
            for i in range(half):
                p = 2 * i + bit if top else bit * half + i
                out[i] = add_up(keep[p], got[p]).astype(jnp.bfloat16)

    outs = [low_shape(half, mids, n, width) for n in (sizes[0], sizes[0], sizes[1], sizes[1])]
    return small_call(body, outs, bits, [keeps[0], gots[0], keeps[1], gots[1]])


def cut_copies(keeps, gots, place, copy_size, kernels):
    _, mids, _, width = keeps[0].shape
    sizes = [k.shape[2] for k in keeps]
    total = sum(sizes)
    if not kernels:
        sums = jnp.concatenate([add_up(k, g)[0] for k, g in zip(keeps, gots)], axis=1)
        sums = sums.astype(jnp.bfloat16).reshape(2, copy_size, total, width)
        return [pick(sums, lax.rem(place + j, copy_size), 1) for j in range(copy_size)]

    def body(at, keep_one, got_one, keep_two, got_two, *outs):
        for j in range(copy_size):
            z = lax.rem(at[0] + j, copy_size)
            for c in range(2):
                m = c * copy_size + z
                top = add_up(keep_one[0, m], got_one[0, m]).astype(jnp.bfloat16)
                low = add_up(keep_two[0, m], got_two[0, m]).astype(jnp.bfloat16)
                outs[j][c, : sizes[0]] = top
                outs[j][c, sizes[0] :] = low

    outs = [low_shape(2, total, width)] * copy_size
    return small_call(body, outs, [place], [keeps[0], gots[0], keeps[1], gots[1]])


def sum_low(parts, kernels):
    if not kernels:
        return sum(p.astype(jnp.float32) for p in parts).astype(jnp.bfloat16)

    def body(at, *refs):
        total = refs[0][...].astype(jnp.float32)
        for ref in refs[1:-1]:
            total = total + ref[...].astype(jnp.float32)
        refs[-1][...] = total.astype(jnp.bfloat16)

    return small_call(body, [low_shape(*parts[0].shape)], [0], parts)[0]


def cut_copy_halves(keeps, gots, place, copy_size, kernels):
    _, mids, _, width = keeps[0].shape
    sizes = [k.shape[2] for k in keeps]
    total, half = sum(sizes), copy_size // 2
    if not kernels:
        sums = jnp.concatenate([add_up(k, g)[0] for k, g in zip(keeps, gots)], axis=1)
        sums = sums.astype(jnp.bfloat16).reshape(2, 2, half, total, width)
        top = place // half
        return [pick(sums, 1 - top, 1), pick(sums, top, 1)]

    def body(at, keep_one, got_one, keep_two, got_two, *outs):
        top = at[0] // half
        for out, bit in zip(outs, (1 - top, top)):
            for c in range(2):
                for j in range(half):
                    m = c * copy_size + bit * half + j
                    first = add_up(keep_one[0, m], got_one[0, m]).astype(jnp.bfloat16)
                    second = add_up(keep_two[0, m], got_two[0, m]).astype(jnp.bfloat16)
                    out[c, j, : sizes[0]] = first
                    out[c, j, sizes[0] :] = second

    outs = [low_shape(2, half, total, width)] * 2
    return small_call(body, outs, [place], [keeps[0], gots[0], keeps[1], gots[1]])


def cut_copy_last(keep, got, place, kernels):
    if not kernels:
        sums = add_up(keep, got).astype(jnp.bfloat16)
        return [pick(sums, 1 - place % 2, 1), pick(sums, place % 2, 1)]

    def body(at, keep_ref, got_ref, *outs):
        low = lax.rem(at[0], 2)
        for out, bit in zip(outs, (1 - low, low)):
            for c in range(2):
                out[c] = add_up(keep_ref[c, bit], got_ref[c, bit]).astype(jnp.bfloat16)

    return small_call(body, [low_shape(2, *keep.shape[2:])] * 2, [place], [keep, got])


def own_and_other(parts, scalars, kernels):
    place, core = scalars
    count = len(parts)
    _, total, width = parts[0].shape
    if not kernels:
        stacked = jnp.stack(parts).astype(jnp.float32)
        sums = 0.0
        for i in range(count):
            sums = sums + pick(stacked, lax.rem(place + count - i, count), 0)
        sums = sums.astype(jnp.bfloat16)
        return [pick(sums, 1 - core, 0), pick(sums, core, 0)]

    def body(at, *refs):
        for out, c in zip(refs[count:], (1 - at[1], at[1])):
            values = [r[c].astype(jnp.float32) for r in refs[:count]]
            sums = None
            for i in range(count):
                turn = lax.rem(at[0] + count - i, count)
                value = values[0]
                for j in range(1, count):
                    value = jnp.where(turn == j, values[j], value)
                sums = value if sums is None else sums + value
            out[...] = sums.astype(jnp.bfloat16)

    return small_call(body, [low_shape(total, width)] * 2, scalars, parts)


class Reduction:
    def __init__(self, sent, kept, rows, size, kernels):
        self.size, self.rows, self.kernels = size, rows, kernels
        self.left = size.bit_length() - 2
        self.me = lax.axis_index("dp")
        self.sent, self.kept, self.bits = list(sent), list(kept), [0] * len(sent)
        self.first = True

    def receive(self):
        self.got = [swap_bit(v, self.size, bit) for v, bit in zip(self.sent, self.bits)]
        return self

    def advance(self):
        if self.first:
            self.bits = [self.left, 1]
            bits = [(self.me >> b) & 1 for b in self.bits]
            cuts = cut_first(self.kept, self.got, self.rows, bits, self.kernels)
        else:
            self.bits = [self.bits[0] - 1, self.bits[1] + 1]
            bits = [(self.me >> b) & 1 for b in self.bits]
            cuts = cut_next(self.kept, self.got, bits, self.kernels)
        self.first = False
        self.left -= 1
        self.sent, self.kept = [cuts[0], cuts[2]], [cuts[1], cuts[3]]
        return self


def attend(ids_col, ids_row, q, k, lanes, head, scale):
    wanted = (lanes >= HEAD_DIM) if head else (lanes < HEAD_DIM)
    scores = dot1(jnp.where(wanted, q, 0), k) * scale
    scores = jnp.where(ids_col == ids_row, scores, -1e30)
    exps = jnp.exp(scores - jnp.max(scores, axis=-1, keepdims=True))
    return wanted, exps / jnp.sum(exps, axis=-1, keepdims=True)


def attention_specs(micros, length, first=0):
    wide = pl.BlockSpec((length, 2 * HEAD_DIM), lambda m, h: (m + first, h))
    col = pl.BlockSpec((length, 1), lambda m, h: (m + first, 0))
    row = pl.BlockSpec((1, 1, length), lambda m, h: (m + first, 0, 0))
    return wide, col, row


def attention(queries, key_rows, value_rows, ids):
    micros, length = ids.shape
    scale = HEAD_DIM ** (-0.5)
    wide, col, row = attention_specs(micros, length)

    def body(col_ref, row_ref, q_ref, k_ref, v_ref, out_ref):
        lanes = lax.broadcasted_iota(jnp.int32, (1, 2 * HEAD_DIM), 1)
        outs = []
        for head in range(2):
            _, probs = attend(
                col_ref[...], row_ref[0], q_ref[...], k_ref[...], lanes, head, scale
            )
            outs.append(
                jnp.dot(
                    probs.astype(jnp.bfloat16), v_ref[...], preferred_element_type=jnp.float32
                )
            )
        out_ref[...] = jnp.where(lanes < HEAD_DIM, outs[0], outs[1]).astype(jnp.bfloat16)

    return pl.pallas_call(
        body,
        grid=(micros, HEADS // 2),
        out_shape=low_shape(micros * length, D),
        in_specs=[col, row, wide, wide, wide],
        out_specs=wide,
        compiler_params=pltpu.CompilerParams(vmem_limit_bytes=24 * MIB),
        cost_estimate=cost(15.0),
    )(ids.reshape(-1, 1), ids[:, None], queries, key_rows, value_rows)


def attention_back(queries, key_rows, value_rows, grad_mixed, ids, which, before):
    micros, length = ids.shape
    scale = HEAD_DIM ** (-0.5)
    wide, col, row = attention_specs(micros, length, which)

    def body(col_ref, row_ref, q_ref, k_ref, v_ref, g_ref, *outs):
        lanes = lax.broadcasted_iota(jnp.int32, (1, 2 * HEAD_DIM), 1)
        q, k, v, g = q_ref[...], k_ref[...], v_ref[...], g_ref[...]
        parts = []
        for head in range(2):
            wanted, probs = attend(col_ref[...], row_ref[0], q, k, lanes, head, scale)
            grad_probs = dot1(jnp.where(wanted, g, 0), v)
            delta = jnp.sum(grad_probs * probs, axis=-1, keepdims=True)
            grad_scores = (probs * (grad_probs - delta)).astype(jnp.bfloat16)
            parts.append(
                (
                    jnp.dot(grad_scores, k, preferred_element_type=jnp.float32) * scale,
                    dot0(grad_scores, q) * scale,
                    dot0(probs.astype(jnp.bfloat16), g),
                )
            )
        for out, one, two in zip(outs[-3:], *parts):
            out[...] = jnp.where(lanes < HEAD_DIM, one, two).astype(jnp.bfloat16)

    return pl.pallas_call(
        body,
        grid=(1, HEADS // 2),
        out_shape=[low_shape(micros * length, D)] * 3,
        in_specs=[col, row, wide, wide, wide, wide]
        + [pl.BlockSpec(memory_space=pl.ANY)] * len(before or ()),
        out_specs=[wide] * 3,
        input_output_aliases={6 + i: i for i in range(len(before or ()))},
        compiler_params=pltpu.CompilerParams(vmem_limit_bytes=60 * MIB),
        cost_estimate=cost(12.0),
    )(ids.reshape(-1, 1), ids[:, None], queries, key_rows, value_rows, grad_mixed, *(before or ()))


def pack_head_grads(pairs, core, dp_size, copy_size, kernels, others=(), plan=None):
    world = dp_size * copy_size
    count, mids = dp_size // 2, 2 * copy_size
    width = pairs[0][1].shape[1]
    half = width // 2
    sizes = [p[0].shape[1] // world for p in pairs]
    total = sum(sizes)
    if not kernels:
        packs = []
        for c in (1 - core, core):
            parts = []
            for left_side, right_side in pairs:
                part = lax.dynamic_slice_in_dim(right_side, c * half, half, 1)
                part = weight_grad(left_side, part).astype(jnp.bfloat16)
                parts.append(part.reshape(count, mids, -1, half))
            packs.append(jnp.concatenate(parts, axis=2))
        given = [jnp.stack([column_sum(p[1]) for p in pairs]), *others]
        if plan is None:
            return packs + given
        return packs + [jnp.concatenate([given[i][at : at + n] for i, at, n in plan])]

    lefts, which = [], []
    for left_side, _ in pairs:
        seen = [i for i, other in enumerate(lefts) if other is left_side]
        which.append(seen[0] if seen else len(lefts))
        lefts += [] if seen else [left_side]
    rights = [p[1] for p in pairs]
    narrow = [v.shape[1] // count % 128 == 0 for v in lefts]
    held = [i for i, w in enumerate(which) if not narrow[w]]

    where, height = list(range(len(pairs))), len(pairs)
    if plan is not None:
        at_row = 0
        for source, row, n in plan:
            if not source:
                where[row : row + n] = range(at_row, at_row + n)
            at_row += n
        height = at_row

    def body(at, *refs):
        left_refs = refs[: len(lefts)]
        right_refs = refs[len(lefts) : len(lefts) + len(rights)]
        other_refs, refs = refs[len(lefts) + len(rights) :][: len(others)], refs[len(others) :]
        sent, kept, sums = refs[len(lefts) + len(rights) :][:3]
        scratch = refs[len(lefts) + len(rights) + 3 :]
        first = at[0] == 0
        step = pl.program_id(0)

        @pl.when(step == 0)
        def _():
            for i, right in enumerate(right_refs):
                ones = jnp.ones((8, right.shape[0]), jnp.bfloat16)
                row = jnp.dot(ones, right[...], preferred_element_type=jnp.float32)
                sums[where[i] : where[i] + 1] = row[:1]
            at = 0
            for source, row, n in plan or ():
                if source:
                    sums[at : at + n] = other_refs[source - 1][row : row + n]
                at += n
            for i, buffer in zip(held, scratch):
                buffer[...] = dot0(left_refs[which[i]][...], right_refs[i][...])

        at_row = 0
        for i, n in enumerate(sizes):
            if i in held:
                rows = mids * n
                whole = scratch[held.index(i)][pl.ds(pl.multiple_of(step * rows, 8), rows)]
            else:
                whole = dot0(left_refs[which[i]][...], right_refs[i][...])
            left, right = whole[:, :half], whole[:, half:]
            for out, part in (
                (sent, jnp.where(first, right, left)),
                (kept, jnp.where(first, left, right)),
            ):
                out[0, :, at_row : at_row + n] = part.reshape(mids, n, half).astype(jnp.bfloat16)
            at_row += n

    in_specs = [pl.BlockSpec(memory_space=pltpu.SMEM)]
    for v, cut_up in zip(lefts, narrow):
        if cut_up:
            in_specs.append(pl.BlockSpec((v.shape[0], v.shape[1] // count), lambda p: (0, p)))
        else:
            in_specs.append(pl.BlockSpec(v.shape, lambda p: (0, 0)))
    in_specs += [pl.BlockSpec(v.shape, lambda p: (0, 0)) for v in [*rights, *others]]
    out_spec = pl.BlockSpec((1, mids, total, half), lambda p: (p, 0, 0, 0))
    return pl.pallas_call(
        body,
        grid=(count,),
        out_shape=[low_shape(count, mids, total, half)] * 2
        + [jax.ShapeDtypeStruct((height, width), jnp.float32)],
        in_specs=in_specs,
        out_specs=[out_spec] * 2 + [pl.BlockSpec((height, width), lambda p: (0, 0))],
        scratch_shapes=[
            pltpu.VMEM((lefts[which[i]].shape[1], width), jnp.float32) for i in held
        ],
        compiler_params=pltpu.CompilerParams(vmem_limit_bytes=40 * MIB),
        cost_estimate=cost(13.0),
    )(jnp.asarray(core, jnp.int32)[None], *lefts, *rights, *others)


def assemble(pieces, scalars, copy_size, rows):
    width = pieces[0][0].shape[-1]
    total = rows

    def body(at, *refs):
        ins, out, sems = refs[: len(pieces)], refs[len(pieces)], refs[len(pieces) + 1]
        copies = []
        for ref, (value, first, flip, vary) in zip(ins, pieces):
            for d in range(2):
                for j in range(copy_size):
                    dp = at[0] ^ (flip | (vary if d else 0))
                    owner = dp * copy_size + lax.rem(at[1] + j, copy_size)
                    copy = pltpu.make_async_copy(
                        ref.at[d, j],
                        out.at[owner, pl.ds(first, value.shape[2])],
                        sems.at[len(copies)],
                    )
                    copy.start()
                    copies.append(copy)
        for copy in copies:
            copy.wait()

    return pl.pallas_call(
        body,
        out_shape=low_shape(8 * copy_size, total, width),
        in_specs=[pl.BlockSpec(memory_space=pltpu.SMEM)]
        + [pl.BlockSpec(memory_space=pl.ANY)] * len(pieces),
        out_specs=pl.BlockSpec(memory_space=pl.ANY),
        scratch_shapes=[pltpu.SemaphoreType.DMA((len(pieces) * 2 * copy_size,))],
        compiler_params=pltpu.CompilerParams(vmem_limit_bytes=4 * MIB),
        cost_estimate=cost(8.0),
    )(jnp.stack([jnp.asarray(v, jnp.int32) for v in scalars]), *[p[0] for p in pieces])


def gather(pack, rows, arrived):
    total = pack.shape[0]
    along = [pack, *arrived]
    pieces = []
    for first, last, bits in ((0, rows, (2, 1)), (rows, total, (1, 2))):
        held = jnp.stack([v[first:last] for v in along])
        held = jnp.stack([held, swap_bit(held, 8, bits[0])])
        got = swap_bit(held, 8, bits[1])
        vary = 1 << bits[0]
        other = 1 << bits[1]
        pieces += [(held, first, 0, vary), (got, first, other, vary)]
        pieces += [
            (swap_bit(held, 8, 0), first, 1, vary),
            (swap_bit(got, 8, 0), first, other | 1, vary),
        ]
    return assemble(pieces, (lax.axis_index("dp"), lax.axis_index("copy")), 4, total)


LANES = 128


def padded_lanes(values):
    return jnp.pad(values, ((0, 0), (0, LANES - values.shape[1]))).reshape(-1)


def lay(ins, shape, plan, vectors):
    height, width = shape
    start = max(p[5] + p[3] for p in plan)

    def body(*refs):
        out = refs[-1]
        for which, row, column, rows, columns, there in plan:
            out[there : there + rows] = refs[which][row : row + rows, column : column + columns]
        values = []
        for which, turned in vectors:
            value = refs[which][...].astype(jnp.float32)
            value = value.T if turned else value
            values += [value[i : i + 1] for i in range(value.shape[0])]
        zero = jnp.zeros((1, LANES), jnp.float32)
        values = [
            jnp.concatenate([v, zero[:, : LANES - v.shape[1]]], axis=1) for v in values
        ]
        values += [zero] * ((height - start) * width // LANES - len(values))
        per = width // LANES
        lines = [
            jnp.concatenate(values[i : i + per], axis=1) for i in range(0, len(values), per)
        ]
        if lines:
            out[start:] = jnp.concatenate(lines, axis=0).astype(jnp.bfloat16)

    return pl.pallas_call(
        body,
        out_shape=low_shape(height, width),
        in_specs=[pl.BlockSpec(memory_space=pltpu.VMEM)] * len(ins),
        out_specs=pl.BlockSpec(memory_space=pltpu.VMEM),
        compiler_params=pltpu.CompilerParams(vmem_limit_bytes=16 * MIB),
        cost_estimate=cost(2.0),
    )(*ins)


def spread(packed, sizes):
    world = packed.shape[0]
    total = sum(count for count, _ in sizes)

    def body(packed_ref, *outs):
        at = 0
        for (count, k), out in zip(sizes, outs):
            width = world * k
            column = lax.broadcasted_iota(jnp.int32, (LANES, width), 1)
            row = lax.broadcasted_iota(jnp.int32, (LANES, width), 0)
            tile = (row == column % k).astype(jnp.bfloat16)
            owner = lax.broadcasted_iota(jnp.int32, (world, width), 0)
            own = owner == lax.broadcasted_iota(jnp.int32, (world, width), 1) // k
            for i in range(count):
                block = packed_ref[:, (at + i) * LANES : (at + i + 1) * LANES]
                values = jnp.dot(block, tile, preferred_element_type=jnp.float32)
                out[i : i + 1] = jnp.sum(jnp.where(own, values, 0.0), axis=0, keepdims=True)
            at += count

    return pl.pallas_call(
        body,
        out_shape=[
            jax.ShapeDtypeStruct((count, world * k), jnp.float32) for count, k in sizes
        ],
        in_specs=[pl.BlockSpec(memory_space=pltpu.VMEM)],
        out_specs=[pl.BlockSpec(memory_space=pltpu.VMEM)] * len(sizes),
        compiler_params=pltpu.CompilerParams(vmem_limit_bytes=16 * MIB),
        cost_estimate=cost(0.7),
    )(packed[:, : total * LANES])


def head_step(weight, head_bias, gain, out_bias, embedded, values):
    bf16, f32 = jnp.bfloat16, jnp.float32
    condition, noisy, noise, slot = values
    out, sums = {}, {}
    valid = (slot >= 0).astype(f32)
    cond = product(condition, weight("cond")) + head_bias(0)
    chosen = jnp.zeros_like(cond)
    for i in range(embedded.shape[0]):
        chosen = jnp.where(slot == i, embedded[i : i + 1], chosen)
    cond = cond + chosen
    gated = jax.nn.silu(cond).astype(bf16)
    out["gated"] = gated
    entry = product(noisy, weight("input")) + head_bias(3)
    norm_head, inv_head = normalize(entry)
    affine = norm_head * gain + head_bias(4)
    shift = product(gated, weight("shift")) + head_bias(7)
    scale = product(gated, weight("scale")) + head_bias(8)
    mlp_in = (affine * (1.0 + scale) + shift).astype(bf16)
    out["mlp_in"] = mlp_in
    inner_one = product(mlp_in, weight("one")) + head_bias(5)
    inner_act = jax.nn.silu(inner_one).astype(bf16)
    out["inner_act"] = inner_act
    inner_two = product(inner_act, weight("two")) + head_bias(6)
    gate = product(gated, weight("gate")) + head_bias(9)
    residual = entry + gate * inner_two
    fshift = product(gated, weight("fshift")) + head_bias(10)
    fscale = product(gated, weight("fscale")) + head_bias(11)
    norm_final, inv_final = normalize(residual)
    final_in = (norm_final * (1.0 + fscale) + fshift).astype(bf16)
    predicted = input_back(final_in, weight("output")) + out_bias
    grad_pred = ((predicted - noise) * valid).astype(bf16)
    sums["output"] = weight_grad(grad_pred, final_in)
    sums["out_bias"] = jnp.sum(grad_pred.astype(f32), axis=0, keepdims=True)
    grad_final_in = product(grad_pred, weight("output"))
    out["fshift"] = grad_final_in.astype(bf16)
    out["fscale"] = (grad_final_in * norm_final).astype(bf16)
    grad_residual = norm_back(grad_final_in * (1.0 + fscale), norm_final, inv_final)
    out["two"] = (grad_residual * gate).astype(bf16)
    grad_one = input_back(out["two"], weight("two")) * silu_slope(inner_one)
    out["one"] = grad_one.astype(bf16)
    grad_mlp_in = input_back(out["one"], weight("one"))
    out["shift"] = grad_mlp_in.astype(bf16)
    out["scale"] = (grad_mlp_in * affine).astype(bf16)
    out["gate"] = (grad_residual * inner_two).astype(bf16)
    grad_gated = input_back(out["shift"], weight("shift"))
    for name in ("scale", "gate", "fshift", "fscale"):
        grad_gated = grad_gated + input_back(out[name], weight(name))
    grad_cond = grad_gated * silu_slope(cond)
    out["cond"] = grad_cond.astype(bf16)
    out["condition"] = input_back(out["cond"], weight("cond")).astype(bf16)
    grad_affine = grad_mlp_in * (1.0 + scale)
    grad_entry = grad_residual + norm_back(grad_affine * gain, norm_head, inv_head)
    grad_entry = grad_entry.astype(bf16)
    sums["input"] = weight_grad(noisy, grad_entry)
    sums["gain"] = jnp.sum(grad_affine * norm_head, axis=0, keepdims=True)
    sums["entry"] = jnp.sum(grad_entry.astype(f32), axis=0, keepdims=True)
    sums["affine"] = jnp.sum(grad_affine, axis=0, keepdims=True)
    lanes = lax.broadcasted_iota(jnp.int32, (slot.shape[0], embedded.shape[0]), 1)
    onehot = (slot == lanes).astype(bf16)
    low_part = (grad_cond - out["cond"].astype(f32)).astype(bf16)
    sums["embedded"] = weight_grad(onehot, out["cond"]) + weight_grad(onehot, low_part)
    return out, sums


SQUARES = ("shift", "scale", "gate", "time2", "one", "two", "fshift", "fscale")
HEAD_OUT = (
    "gated", "mlp_in", "inner_act", "fshift", "fscale", "two", "one", "shift", "scale", "gate",
    "cond",
)
HEAD_SUMS = (
    ("input", CHANNELS), ("output", CHANNELS), ("embedded", 8), ("gain", 1), ("entry", 1),
    ("affine", 1), ("out_bias", 1),
)


def head_kernel(pack, w_cond, w_input, w_output, head_bias, gain, out_bias, embedded, values, k, cut):
    rows = values[0].shape[0]
    micros, own = cut
    step = rows // micros
    world = pack.shape[0]
    used = [i for i, name in enumerate(SQUARES) if name != "time2"]
    height = sum(n for _, n in HEAD_SUMS)
    height += -height % 8
    smalls = [w_cond, w_input, w_output, head_bias, gain, out_bias, embedded]

    def body(*refs):
        ins = refs[: len(smalls)]
        pack_ref = refs[len(smalls)]
        tiles = refs[len(smalls) + 1 :][:4]
        outs = refs[len(smalls) + 5 :][: len(HEAD_OUT)]
        rest = refs[len(smalls) + 5 + len(HEAD_OUT) :]
        chunks, (sums_ref, buffer, sems) = rest[:-3], rest[-3:]
        first = pl.program_id(0) == 0

        def fetch(n):
            return pltpu.make_async_copy(
                pack_ref.at[:, pl.ds(used[n] * k, k)], buffer.at[n], sems.at[n]
            )

        @pl.when(first)
        def _():
            for n in range(len(used)):
                fetch(n).start()

        ready = set()

        def weight(name):
            if name in ("cond", "input", "output"):
                return ins[("cond", "input", "output").index(name)][...]
            n = used.index(SQUARES.index(name))
            if n not in ready:
                ready.add(n)

                @pl.when(first)
                def _():
                    fetch(n).wait()

            return buffer[n].reshape(WIDTH, WIDTH)

        out, sums = head_step(
            weight,
            lambda i: ins[3][i : i + 1],
            ins[4][...],
            ins[5][...],
            ins[6][...],
            [t[...] for t in tiles],
        )
        for name, ref in zip(HEAD_OUT, outs):
            ref[...] = out[name]
        for n, ref in enumerate(chunks):
            ref[0] = out["condition"][n * own : (n + 1) * own]

        @pl.when(first)
        def _():
            sums_ref[...] = jnp.zeros((height, WIDTH), jnp.float32)

        at = 0
        for name, n in HEAD_SUMS:
            width = sums[name].shape[1]
            sums_ref[at : at + n, :width] += sums[name]
            at += n

    def tall(width):
        return pl.BlockSpec((step, width), lambda i: (i, 0))

    count = step // own
    *outs, sums = pl.pallas_call(
        body,
        grid=(rows // step,),
        out_shape=[low_shape(rows, WIDTH)] * len(HEAD_OUT)
        + [low_shape(micros, own, D)] * count
        + [jax.ShapeDtypeStruct((height, WIDTH), jnp.float32)],
        in_specs=[
            pl.BlockSpec(v.shape, lambda i: (0, 0), pipeline_mode=pl.Buffered(1)) for v in smalls
        ]
        + [pl.BlockSpec(memory_space=pl.ANY)]
        + [tall(v.shape[1]) for v in values],
        out_specs=[tall(WIDTH)] * len(HEAD_OUT)
        + [pl.BlockSpec((1, own, D), lambda i: (i, 0, 0))] * count
        + [pl.BlockSpec((height, WIDTH), lambda i: (0, 0))],
        scratch_shapes=[
            pltpu.VMEM((len(used), world, k, WIDTH), jnp.bfloat16),
            pltpu.SemaphoreType.DMA((len(used),)),
        ],
        compiler_params=pltpu.CompilerParams(vmem_limit_bytes=60 * MIB),
        cost_estimate=cost(45.0),
    )(*smalls, pack, *values)
    return dict(zip(HEAD_OUT, outs)), outs[len(HEAD_OUT) :], sums


def pack_block_grads(pairs, core, dp_size):
    count = dp_size // 2
    half = D // 2
    packs = []
    for c in (1 - core, core):
        parts = []
        for left_side, right_side in pairs:
            for at in range(0, right_side.shape[1], D):
                part = lax.dynamic_slice_in_dim(right_side, at + c * half, half, 1)
                part = product(left_side, part).astype(jnp.bfloat16)
                parts.append(part.reshape(count, 2, -1, half))
        packs.append(jnp.concatenate(parts, axis=2))
    return packs


def put_halves(first, sent, kept, at_row, whole):
    half = D // 2
    count = sent.shape[0]
    n = whole.shape[0] // (2 * count)
    left, right = whole[:, :half], whole[:, half:]
    for out, part in (
        (sent, jnp.where(first, right, left)),
        (kept, jnp.where(first, left, right)),
    ):
        part = part.reshape(count, 2, n, half).astype(jnp.bfloat16)
        out[:, :, at_row : at_row + n] = part


def feed_forward(second_in, middle, ups, up_bias, w_down, down_bias, place, copy_size, kernels):
    bf16, f32 = jnp.bfloat16, jnp.float32
    rows = middle.shape[0]
    steps = len(ups)

    def step_of(hidden):
        half = 0.5 * (1.0 + lax.erf(hidden * 2.0 ** (-0.5)))
        bell = jnp.exp(-0.5 * hidden * hidden) * (2.0 * math.pi) ** (-0.5)
        return (hidden * half).astype(bf16), (half + hidden * bell).astype(bf16)

    if not kernels:
        hidden = product(second_in, jnp.concatenate(ups, axis=1)) + up_bias
        active, slope = step_of(hidden)
        output = middle + product(active, w_down) + down_bias
        return output.astype(bf16), slope, None, active

    per = w_down.shape[0] // steps
    k = per // (2 * copy_size)
    width = per // copy_size

    def body(at, *refs):
        up_refs, refs = refs[:steps], refs[steps:]
        in_ref, middle_ref, bias_ref, down_ref, down_bias_ref = refs[:5]
        out_ref, slope_ref, chosen_ref, total, hidden = refs[5:]
        step = pl.program_id(0)
        for n in range(steps):

            @pl.when(step == n)
            def _():
                hidden[...] = product(in_ref[...], up_refs[n][...])

        active, slope = step_of(hidden[...] + bias_ref[...])
        slope_ref[...] = slope
        part = product(active, down_ref[...])
        source = lax.broadcasted_iota(jnp.int32, (width, per), 1)
        target = lax.broadcasted_iota(jnp.int32, (width, per), 0)
        wanted = (target // k * copy_size + at[0]) * k + target % k
        one_hot = (source == wanted).astype(bf16)
        chosen_ref[0] = dot1(one_hot, active).astype(bf16)

        @pl.when(step == 0)
        def _():
            total[...] = middle_ref[...] + down_bias_ref[...] + part

        @pl.when(step > 0)
        def _():
            total[...] += part

        @pl.when(step == steps - 1)
        def _():
            out_ref[...] = total[...].astype(bf16)

    def full(v):
        return pl.BlockSpec(v.shape, lambda j: (0,) * len(v.shape), pipeline_mode=pl.Buffered(1))

    out, slope, chosen = pl.pallas_call(
        body,
        grid=(steps,),
        out_shape=[low_shape(rows, D), low_shape(rows, per * steps), low_shape(steps, width, rows)],
        in_specs=[pl.BlockSpec(memory_space=pltpu.SMEM)]
        + [full(v) for v in (*ups, second_in, middle)]
        + [
            pl.BlockSpec((1, per), lambda j: (0, j)),
            pl.BlockSpec((per, D), lambda j: (j, 0)),
            full(down_bias),
        ],
        out_specs=[
            pl.BlockSpec((rows, D), lambda j: (0, 0)),
            pl.BlockSpec((rows, per), lambda j: (0, j)),
            pl.BlockSpec((1, width, rows), lambda j: (j, 0, 0)),
        ],
        scratch_shapes=[pltpu.VMEM((rows, D), f32), pltpu.VMEM((rows, per), f32)],
        compiler_params=pltpu.CompilerParams(vmem_limit_bytes=48 * MIB),
        cost_estimate=cost(18.0),
    )(place[None], *ups, second_in, middle, up_bias, w_down, down_bias)
    return out, slope, chosen, None


def block_back_one(pieces, slope, ups, w_down, w_proj, lefts, norm, inverse, gain, core, dp_size, kernels):
    bf16, f32 = jnp.bfloat16, jnp.float32
    micros, own, _ = pieces[0].shape
    rows = micros * own * len(pieces)
    steps = len(ups)
    k = lefts[0].shape[0] // dp_size
    k_down = w_down.shape[0] // (dp_size * len(pieces))
    if not kernels:
        grad = jnp.stack(pieces, axis=1).reshape(rows, D)
        hidden = (input_back(grad, w_down) * slope.astype(f32)).astype(bf16)
        second = input_back(hidden, jnp.concatenate(ups, axis=1))
        middle = grad.astype(f32) + norm_back(second * gain, norm, inverse)
        low = middle.astype(bf16)
        sums = [jnp.sum(second * norm, axis=0), jnp.sum(second, axis=0)]
        sums = jnp.stack(sums + [column_sum(low), column_sum(grad)])
        packs = pack_block_grads([(lefts[0], hidden), (lefts[1], grad)], core, dp_size)
        mixed = input_back(low, w_proj).astype(bf16)
        return *packs, middle, low, mixed, sums, column_sum(hidden).reshape(steps, 1, D)

    def body(at, *refs):
        piece_refs, refs = refs[: len(pieces)], refs[len(pieces) :]
        up_refs, refs = refs[:steps], refs[steps:]
        slope_ref, down_ref, proj_ref, left_up, left_down, norm_ref, inv_ref, gain_ref = refs[:8]
        sent, kept, middle_ref, low_ref, mixed_ref, sums_ref, hidden_sums, grad, total = refs[8:]
        step = pl.program_id(0)
        first = at[0] == 0

        @pl.when(step == 0)
        def _():
            for m in range(micros):
                for n, ref in enumerate(piece_refs):
                    start = (m * len(pieces) + n) * own
                    grad[start : start + own] = ref[m]
            for n in range(steps):
                here = pl.ds(n * dp_size // (2 * steps), dp_size // (2 * steps))
                part = product(left_down[n], grad[...])
                put_halves(first, sent.at[here], kept.at[here], steps * k, part)
            total[...] = jnp.zeros_like(total)

        hidden = dot1(grad[...], down_ref[...]) * slope_ref[...].astype(f32)
        hidden = hidden.astype(bf16)
        ones = jnp.ones((8, rows), bf16)
        hidden_sums[0] = jnp.dot(ones, hidden, preferred_element_type=f32)
        up_grad = product(left_up[...], hidden)
        for n in range(steps):

            @pl.when(step == n)
            def _():
                total[...] += dot1(hidden, up_refs[n][...])
                put_halves(first, sent, kept, n * k, up_grad)

        @pl.when(step == steps - 1)
        def _():
            second, norm_now = total[...], norm_ref[...]
            given = grad[...].astype(f32)
            middle = given + norm_back(second * gain_ref[...], norm_now, inv_ref[...])
            low = middle.astype(bf16)
            middle_ref[...] = middle
            low_ref[...] = low
            mixed_ref[...] = dot1(low, proj_ref[...]).astype(bf16)
            for n, values in enumerate((second * norm_now, second, low.astype(f32), given)):
                sums_ref[n : n + 1] = jnp.sum(values, axis=0, keepdims=True)

    def full(v):
        return pl.BlockSpec(v.shape, lambda j: (0,) * len(v.shape), pipeline_mode=pl.Buffered(1))

    pack = low_shape(dp_size // 2, 2, steps * k + k_down, D // 2)
    tall = jax.ShapeDtypeStruct((rows, D), f32)
    outs = [pack, pack, tall, low_shape(rows, D), low_shape(rows, D)]
    outs += [jax.ShapeDtypeStruct((8, D), f32)]
    ins = [*pieces, *ups, slope, w_down, w_proj, *lefts, norm, inverse, gain]
    in_specs = [full(v) for v in ins]
    in_specs[len(pieces) + steps] = pl.BlockSpec((rows, D), lambda j: (0, j))
    in_specs[len(pieces) + steps + 1] = pl.BlockSpec((D, D), lambda j: (j, 0))
    return pl.pallas_call(
        body,
        grid=(steps,),
        out_shape=outs + [jax.ShapeDtypeStruct((steps, 8, D), f32)],
        in_specs=[pl.BlockSpec(memory_space=pltpu.SMEM)] + in_specs,
        out_specs=[pl.BlockSpec(v.shape, lambda j, n=len(v.shape): (0,) * n) for v in outs]
        + [pl.BlockSpec((1, 8, D), lambda j: (j, 0, 0))],
        scratch_shapes=[pltpu.VMEM((rows, D), bf16), pltpu.VMEM((rows, D), f32)],
        compiler_params=pltpu.CompilerParams(vmem_limit_bytes=60 * MIB),
        cost_estimate=cost(24.0),
    )(jnp.asarray(core, jnp.int32)[None], *ins)


def block_back_two(grads, weights, lefts, low, middle, norm, inverse, gain, sums, hidden_sums, own, micros, core, dp_size, kernels):
    f32 = jnp.float32
    rows = low.shape[0]
    length = rows // micros
    steps = hidden_sums.shape[0]

    def smalls(first, norm_now, q, v):
        return [
            jnp.sum(first * norm_now, axis=0, keepdims=True),
            None,
            jnp.sum(first, axis=0, keepdims=True),
            jnp.sum(q.astype(f32), axis=0, keepdims=True),
            jnp.sum(v.astype(f32), axis=0, keepdims=True),
        ]

    if not kernels:
        first = sum(input_back(g, w) for g, w in zip(grads, weights))
        input_grad = middle + norm_back(first * gain, norm, inverse)
        input_grad = input_grad.reshape(micros, length, D)[:, :own]
        rows_of = smalls(first, norm, grads[0], grads[2])
        rows_of[1] = sums[:1]
        small = jnp.concatenate([*rows_of, sums[2:3], sums[1:2], sums[3:4], hidden_sums[:, 0]])
        pairs = [(lefts[0], g) for g in grads] + [(lefts[1], low)]
        return *pack_block_grads(pairs, core, dp_size), input_grad, small

    k = lefts[0].shape[0] // dp_size

    def body(at, *refs):
        grad_refs, weight_refs, refs = refs[:3], refs[3:6], refs[6:]
        left_in, left_mixed, low_ref, middle_ref, norm_ref, inv_ref, gain_ref = refs[:7]
        sums_ref, hidden_ref, sent, kept, out_ref, small_ref = refs[7:]
        flag = at[0] == 0
        for n, ref in enumerate(grad_refs):
            put_halves(flag, sent, kept, n * k, product(left_in[...], ref[...]))
        put_halves(flag, sent, kept, 3 * k, product(left_mixed[...], low_ref[...]))
        first = dot1(grad_refs[0][...], weight_refs[0][...])
        for g, w in zip(grad_refs[1:], weight_refs[1:]):
            first = first + dot1(g[...], w[...])
        for n, value in enumerate(
            smalls(first, norm_ref[...], grad_refs[0][...], grad_refs[2][...])
        ):
            if value is not None:
                small_ref[n : n + 1] = value
        small_ref[1:2] = sums_ref[0:1]
        small_ref[5:6] = sums_ref[2:3]
        small_ref[6:7] = sums_ref[1:2]
        small_ref[7:8] = sums_ref[3:4]
        for n in range(steps):
            small_ref[8 + n : 9 + n] = hidden_ref[n, 0:1]
        for m in range(micros):
            here = pl.ds(m * length, own)
            back = norm_back(
                first[m * length : m * length + own] * gain_ref[...], norm_ref[here], inv_ref[here]
            )
            out_ref[m] = middle_ref[here] + back

    pack = low_shape(dp_size // 2, 2, 4 * k, D // 2)
    outs = [pack, pack, jax.ShapeDtypeStruct((micros, own, D), f32)]
    outs += [jax.ShapeDtypeStruct((8 + steps, D), f32)]
    ins = [*grads, *weights, *lefts, low, middle, norm, inverse, gain, sums, hidden_sums]
    return small_call(body, outs, [core], ins)


def shards(
    block_input,
    image_ids,
    latents,
    noise,
    timesteps,
    norm_gains,
    block_biases,
    w_qkv,
    w_proj,
    w_up,
    up_bias,
    w_down,
    head_gain,
    head_biases,
    w_cond,
    w_time1,
    w_time2,
    w_input,
    w_ada,
    w_mlp1,
    w_mlp2,
    w_final,
    w_output,
    output_bias,
):
    bf16, f32 = jnp.bfloat16, jnp.float32
    dp_size, copy_size = lax.axis_size("dp"), lax.axis_size("copy")
    world = dp_size * copy_size
    place = lax.axis_index("copy")
    micros, _, own, _ = block_input.shape
    length = image_ids.shape[2]
    total = micros * length
    k_d, k_ff, k_w, k_t = D // world, w_down.shape[0], WIDTH // world, w_time1.shape[0]
    ff = k_ff * world
    kernels = k_d % 8 == 0 and k_w % 16 == 0 and k_t % 8 == 0
    score_scale = HEAD_DIM ** (-0.5)

    def cut(matrix, width):
        return [matrix[:, i : i + width] for i in range(0, matrix.shape[1], width)]

    def pad_flat(parts, width):
        flat = jnp.concatenate([padded_lanes(p) for p in parts])
        count = -(-flat.shape[0] // (16 * width)) * 16 * width
        return jnp.pad(flat, (0, count - flat.shape[0])).reshape(-1, width)

    groups = [
        (cut(w_qkv, D) + [w_proj, pad_flat([norm_gains, block_biases, up_bias[None]], D)], 2),
        (cut(w_up, D) + [w_down], 4),
        (
            cut(w_ada, WIDTH)
            + [w_time2, w_mlp1, w_mlp2]
            + cut(w_final, WIDTH)
            + [w_cond, w_time1]
            + [pad_flat([w_input, w_output.T, head_gain[None], head_biases], WIDTH)],
            0,
        ),
    ]

    def everyone(pack):
        return [shift_copy(pack, copy_size, copy_size - j) for j in range(1, copy_size)]

    def unpack(pack, parts):
        out, at = [], 0
        for part in parts:
            out.append(pack[:, at : at + part.shape[0]].reshape(-1, pack.shape[2]))
            at += part.shape[0]
        return out

    own_rows = block_input[:, 0]
    if kernels:
        square = range(3)
        packs = [
            lay(
                [w_qkv, w_proj, norm_gains, block_biases, up_bias[None]],
                (4 * k_d + 16, D),
                [(0, 0, i * D, k_d, D, i * k_d) for i in square] + [(1, 0, 0, k_d, D, 3 * k_d)],
                [(2, False), (3, False), (4, False)],
            ),
            lay(
                [w_up, w_down],
                (ff // D * k_d + k_ff, D),
                [(0, 0, i * D, k_d, D, i * k_d) for i in range(ff // D)]
                + [(1, 0, 0, k_ff, D, ff // D * k_d)],
                [],
            ),
            lay(
                [w_ada, w_time2, w_mlp1, w_mlp2, w_final, w_cond, w_time1]
                + [w_input, w_output, head_gain[None], head_biases],
                (8 * k_w + k_d + k_t + 16, WIDTH),
                [(0, 0, i * WIDTH, k_w, WIDTH, i * k_w) for i in square]
                + [(i, 0, 0, k_w, WIDTH, (2 + i) * k_w) for i in (1, 2, 3)]
                + [(4, 0, i * WIDTH, k_w, WIDTH, (6 + i) * k_w) for i in range(2)]
                + [(5, 0, 0, k_d, WIDTH, 8 * k_w), (6, 0, 0, k_t, WIDTH, 8 * k_w + k_d)],
                [(7, False), (8, True), (9, False), (10, False)],
            ),
        ]
    else:
        packs = [jnp.concatenate(parts, 0) for parts, _ in groups]
    if kernels and dp_size == 8 and copy_size == 4:
        head_own = packs[2]
        arrived = [everyone(packs[0])]
        *arrived[0], packs[1] = tie(*arrived[0], packs[1])
        arrived.append(everyone(packs[1]))
        *arrived[1], own_rows, head_own = tie(*arrived[1], own_rows, head_own)
        rows_arrived = everyone(own_rows)
        full = [
            gather(pack, sum(p.shape[0] for p in parts[:n]), got)
            for pack, (parts, n), got in zip(packs[:2], groups[:2], arrived[:2])
        ]
        head = lax.all_gather(head_own, ("dp", "copy"), axis=0)
        full.append(head)
    else:
        rows_arrived = everyone(own_rows)
        full = [lax.all_gather(pack, ("dp", "copy"), axis=0) for pack in packs]
    head_pack = full[2]
    full = [unpack(pack, parts) for pack, (parts, _) in zip(full, groups)]

    rows = jnp.stack([own_rows, *rows_arrived], axis=1).reshape(total, D).astype(f32)

    def turned(values):
        twice = jnp.concatenate([values, values], axis=1)
        return lax.dynamic_slice_in_dim(twice, place * own, length, 1)

    ids = turned(image_ids[:, 0])
    latent_rows = turned(latents[:, 0]).reshape(total, CHANNELS)
    noise_rows = turned(noise[:, 0, 0]).reshape(total, CHANNELS)

    w_q, w_k, w_v, w_proj_full, small = full[0]
    w_down_full = full[1][4]
    small = small.reshape(world, -1)
    gains, biases, up_bias_full = spread(small, [(2, k_d), (6, k_d), (1, k_ff)])

    norm_one, inv_one = normalize(rows)
    first_in = (norm_one * gains[0] + biases[0]).astype(bf16)
    queries = (product(first_in, w_q) + biases[1]).astype(bf16)
    key_rows = product(first_in, w_k).astype(bf16)
    value_rows = (product(first_in, w_v) + biases[2]).astype(bf16)
    mixed = attention(queries, key_rows, value_rows, ids)
    middle = rows + product(mixed, w_proj_full) + biases[3]
    norm_two, inv_two = normalize(middle)
    second_in = (norm_two * gains[1] + biases[4]).astype(bf16)
    condition, slope, active_z, active = feed_forward(
        second_in,
        middle,
        full[1][:4],
        up_bias_full,
        w_down_full,
        biases[5:6],
        place,
        copy_size,
        kernels,
    )

    def chosen(values):
        width = values.shape[1]
        k = width // world
        source = jnp.arange(width, dtype=jnp.int32)[None, :]
        target = jnp.arange(dp_size * k, dtype=jnp.int32)[:, None]
        wanted = (target // k * copy_size + place) * k + target % k
        return input_back((source == wanted).astype(bf16), values).astype(bf16)

    condition, first_z, mixed_z, second_z, active_z, slope, norm_one, inv_one, norm_two, inv_two = tie(
        condition,
        chosen(first_in),
        chosen(mixed),
        chosen(second_in),
        chosen(active) if active_z is None else active_z,
        slope,
        norm_one,
        inv_one,
        norm_two,
        inv_two,
    )
    core = lax.axis_index("dp") & 1

    def split_pack(pack, parts):
        out, at = [], 0
        for rows_of in parts:
            out.append(pack[at : at + rows_of])
            at += rows_of
        return out

    def after(first, *values):
        first = list(first)
        return list(tie(*first, *values)[len(first) :])

    def send_after(reduction, first):
        reduction.sent = after(first, *reduction.sent)
        return reduction.receive()

    def form_after(reduction, first):
        reduction.got = after(first, *reduction.got)
        reduction.advance()
        return [*reduction.sent, *reduction.kept]

    def to_copies(reduction, first):
        reduction.got = after(first, *reduction.got)
        chunks = cut_copies(reduction.kept, reduction.got, place, copy_size, kernels)
        arriving = [shift_copy(chunks[j], copy_size, j) for j in range(1, copy_size)]
        return [chunks[0], *arriving]

    def whole(other, mine):
        got = swap_bit(other, dp_size, 0)
        left = jnp.where(core == 0, mine, got)
        right = jnp.where(core == 0, got, mine)
        return jnp.concatenate([left, right], axis=1).astype(f32)

    def finish(reduction):
        while reduction.left:
            reduction.advance().receive()
        parts = [
            jnp.concatenate([v[0] for v in values], axis=1)
            for values in (reduction.kept, reduction.got)
        ]
        return whole(*own_and_other(parts, (0, core), kernels))

    squares = dict(zip(SQUARES, full[2][:8]))
    w_cond_full, w_time1_full, small = full[2][8:]
    w_time2_full = squares["time2"]
    small = small.reshape(world, -1)
    w_input_full, w_output_t, head_gain_f, head_bias = spread(
        small, [(CHANNELS, k_w), (CHANNELS, k_w), (1, k_w), (12, k_w)]
    )
    w_input_full, w_output_t = w_input_full.astype(bf16), w_output_t.astype(bf16)

    row_slot = ids + IMAGES * jnp.arange(micros, dtype=jnp.int32)[:, None]
    row_slot = jnp.where(ids >= 0, row_slot, -1).reshape(total, 1)
    step_vals = timesteps[:, 0, 0].reshape(micros * IMAGES).astype(f32)
    sinusoid_in = sinusoid(step_vals).astype(bf16)
    time_one = product(sinusoid_in, w_time1_full) + head_bias[1]
    time_act = jax.nn.silu(time_one).astype(bf16)
    embedded = product(time_act, w_time2_full) + head_bias[2]
    factors = plan(step_vals)
    slots = jnp.arange(micros * IMAGES, dtype=jnp.int32)[None, :]
    mixing = [
        jnp.sum(jnp.where(row_slot == slots, factors[None, :, i], 0.0), axis=1, keepdims=True)
        for i in range(2)
    ]
    noisy = (latent_rows * mixing[0] + noise_rows * mixing[1]).astype(bf16)
    values = (condition, noisy, noise_rows, row_slot)
    out_bias = output_bias.astype(f32)[None]
    if kernels:
        out, chunks, sums = head_kernel(
            head_pack,
            w_cond_full,
            w_input_full,
            w_output_t,
            head_bias,
            head_gain_f,
            out_bias,
            embedded,
            values,
            k_w,
            (micros, own),
        )
    else:
        others = {"cond": w_cond_full, "input": w_input_full, "output": w_output_t, **squares}
        out, sums = head_step(
            others.get,
            lambda i: head_bias[i : i + 1],
            head_gain_f,
            out_bias,
            embedded,
            values,
        )
        chunks = out["condition"].reshape(micros, copy_size, own, D)
        chunks = [chunks[:, j] for j in range(copy_size)]
        sums = [jnp.pad(sums[n], ((0, 0), (0, WIDTH - sums[n].shape[1]))) for n, _ in HEAD_SUMS]
        sums = jnp.concatenate(sums)
        sums = jnp.pad(sums, ((0, -sums.shape[0] % 8), (0, 0)))
    at_embedded = 2 * CHANNELS
    grad_embedded = sums[at_embedded : at_embedded + micros * IMAGES].astype(bf16)
    grad_time_one = (input_back(grad_embedded, w_time2_full) * silu_slope(time_one)).astype(bf16)
    arriving = [shift_copy(chunks[j], copy_size, j) for j in range(1, copy_size)]
    (gated,) = after(chunks, out["gated"])
    send, keep, sums_one = pack_head_grads(
        [
            (gated, out["fshift"]),
            (gated, out["fscale"]),
            (out["inner_act"], out["two"]),
            (out["mlp_in"], out["one"]),
        ],
        core,
        dp_size,
        copy_size,
        kernels,
    )
    pack_one = Reduction([send], [keep], 2 * k_w, dp_size, kernels)
    arriving = after([keep], *arriving)
    grad_z_own = sum_low([chunks[0], *arriving], kernels)
    arriving = [shift_copy(grad_z_own, copy_size, copy_size - j) for j in range(1, copy_size)]
    send_after(pack_one, [grad_z_own])
    (gated,) = after([grad_z_own], gated)
    of_head = 2 * CHANNELS + 8
    send, keep, small_grads = pack_head_grads(
        [
            (gated, out["shift"]),
            (gated, out["scale"]),
            (gated, out["gate"]),
            (time_act, grad_embedded),
            (condition, out["cond"]),
            (sinusoid_in, grad_time_one),
        ],
        core,
        dp_size,
        copy_size,
        kernels,
        (sums_one, sums),
        (
            (2, 0, 2 * CHANNELS),
            (2, of_head, 1),
            (0, 4, 2),
            (0, 3, 1),
            (2, of_head + 1, 2),
            (1, 3, 1),
            (1, 2, 1),
            (0, 0, 3),
            (1, 0, 2),
            (2, of_head + 3, 1),
            (2, of_head + 4, 2),
        ),
    )
    pack_two = Reduction([send], [keep], 3 * k_w, dp_size, kernels)
    formed = form_after(pack_one, [keep])
    arriving = after(formed, *arriving)
    send_after(pack_one, arriving)
    send_after(pack_two, arriving)

    def swap_copies(values, shift, first):
        return values + after(first, swap_copy(values, copy_size, shift))[0]

    send, keep, grad_middle, grad_branch, grad_mixed, block_sums, hidden_sums = block_back_one(
        [grad_z_own, *arriving],
        slope,
        full[1][:4],
        w_down_full,
        w_proj_full,
        (second_z, active_z),
        norm_two,
        inv_two,
        gains[1:2],
        core,
        dp_size,
        kernels,
    )
    sent, kept = [send], [keep]
    formed = form_after(pack_one, [grad_mixed])
    send_after(pack_one, formed)
    small_grads = swap_copies(small_grads, 1, formed)
    formed = form_after(pack_two, [small_grads])
    send_after(pack_two, formed)
    (grad_mixed,) = after(formed, grad_mixed)
    back = attention_back(queries, key_rows, value_rows, grad_mixed, ids, 0, None)
    pack_one.got = after(back, *pack_one.got)
    send, one_half = cut_copy_halves(pack_one.kept, pack_one.got, place, copy_size, kernels)
    one_got = swap_copy(send, copy_size, copy_size // 2)
    small_grads = swap_copies(small_grads, 2, [one_half])
    (grad_mixed,) = after([small_grads], grad_mixed)
    for m in range(1, micros):
        back = attention_back(queries, key_rows, value_rows, grad_mixed, ids, m, back)
    formed = form_after(pack_two, back)
    send_after(pack_two, formed)
    (one_got,) = after(formed, one_got)
    send, one_last = cut_copy_last(one_half, one_got, place, kernels)
    one_got = swap_copy(send, copy_size, 1)
    back = after([one_last], *back)
    send, keep, input_grad, block_small = block_back_two(
        back,
        (w_q, w_k, w_v),
        (first_z, mixed_z),
        grad_branch,
        grad_middle,
        norm_one,
        inv_one,
        gains[:1],
        block_sums,
        hidden_sums,
        own,
        micros,
        core,
        dp_size,
        kernels,
    )
    sent, kept = sent + [send], kept + [keep]
    pack_three = Reduction(sent, kept, 6 * k_d, dp_size, kernels)
    two_parts = to_copies(pack_two, [keep])
    (one_got,) = after([two_parts[0]], one_got)
    own_one_parts = own_and_other([one_last, one_got], (0, core), kernels)
    send_after(pack_three, own_one_parts)
    head_rows = small_grads.shape[0]
    block_small = jnp.pad(block_small, ((0, -block_small.shape[0] % 8), (0, WIDTH - D)))
    small_grads = jnp.concatenate([small_grads, block_small], axis=0)
    everywhere = lax.all_gather(small_grads, "dp", axis=0)
    small_grads = everywhere[0]
    for n in range(1, dp_size):
        small_grads = small_grads + everywhere[n]
    block_small = small_grads[head_rows:, :D]
    formed = form_after(pack_three, own_one_parts)
    send_after(pack_three, formed)
    while pack_three.left:
        formed = form_after(pack_three, [two_parts[0]])
        send_after(pack_three, formed)
    two_parts = after(formed, *two_parts)
    own_two_parts = own_and_other(two_parts, (place, core), kernels)
    own_all = finish(pack_three)
    own_up = jnp.concatenate(split_pack(own_all, [k_d] * 4), axis=1)
    own_down = own_all[4 * k_d : 4 * k_d + k_ff]
    own_four = own_all[4 * k_d + k_ff :]
    own_q, own_k, own_v, own_proj = split_pack(own_four, [k_d] * 4)
    own_fshift, own_fscale, own_two, own_one = split_pack(
        whole(*own_one_parts), [k_w] * 4
    )
    own_shift, own_scale, own_gate, own_time2, own_cond, own_time1 = split_pack(
        whole(*own_two_parts), [k_w] * 4 + [k_d, k_t]
    )
    me = lax.axis_index("dp") * copy_size + place
    own_rest = lax.dynamic_slice_in_dim(block_small[:8], me * k_d, k_d, 1)
    own_gains, own_biases = own_rest[:2], own_rest[2:]
    own_up_bias = lax.dynamic_slice_in_dim(block_small[8 : 8 + ff // D].reshape(ff), me * k_ff, k_ff)
    own_small = lax.dynamic_slice_in_dim(small_grads, me * k_w, k_w, 1)
    own_w_input = own_small[:CHANNELS]
    own_w_output = own_small[CHANNELS : 2 * CHANNELS].T
    own_head_gain = own_small[2 * CHANNELS]
    own_head_biases = own_small[2 * CHANNELS + 1 : 2 * CHANNELS + 13]
    grad_out_bias = small_grads[2 * CHANNELS + 13, :CHANNELS]

    input_grad = input_grad.reshape(micros, 1, own, D)
    block_output = condition.reshape(micros, length, D)[:, :own].reshape(micros, 1, own, D)
    return (
        block_output,
        input_grad,
        own_gains,
        own_biases,
        jnp.concatenate([own_q, own_k, own_v], axis=1),
        own_proj,
        own_up,
        own_up_bias,
        own_down,
        own_head_gain,
        own_head_biases,
        own_cond,
        own_time1,
        own_time2,
        own_w_input,
        jnp.concatenate([own_shift, own_scale, own_gate], axis=1),
        own_one,
        own_two,
        jnp.concatenate([own_fshift, own_fscale], axis=1),
        own_w_output,
        grad_out_bias,
    )


def solution(mesh):
    in_specs = (
        P(None, "dp", "copy", None),
        P(None, "dp", None),
        P(None, "dp", None, None),
        P(None, "copy", "dp", None, None),
        P(None, "copy", "dp", None),
        P(None, ("dp", "copy")),
        P(None, ("dp", "copy")),
        P(("dp", "copy"), None),
        P(("dp", "copy"), None),
        P(("dp", "copy"), None),
        P(("dp", "copy")),
        P(("dp", "copy"), None),
        P(("dp", "copy")),
        P(None, ("dp", "copy")),
        P(("dp", "copy"), None),
        P(("dp", "copy"), None),
        P(("dp", "copy"), None),
        P(None, ("dp", "copy")),
        P(("dp", "copy"), None),
        P(("dp", "copy"), None),
        P(("dp", "copy"), None),
        P(("dp", "copy"), None),
        P(("dp", "copy"), None),
        P(),
    )
    out_specs = (
        P(None, "dp", "copy", None),
        P(None, "dp", "copy", None),
        P(None, ("dp", "copy")),
        P(None, ("dp", "copy")),
        P(("dp", "copy"), None),
        P(("dp", "copy"), None),
        P(("dp", "copy"), None),
        P(("dp", "copy")),
        P(("dp", "copy"), None),
        P(("dp", "copy")),
        P(None, ("dp", "copy")),
        P(("dp", "copy"), None),
        P(("dp", "copy"), None),
        P(("dp", "copy"), None),
        P(None, ("dp", "copy")),
        P(("dp", "copy"), None),
        P(("dp", "copy"), None),
        P(("dp", "copy"), None),
        P(("dp", "copy"), None),
        P(("dp", "copy"), None),
        P(),
    )
    return jax.shard_map(shards, mesh=mesh, in_specs=in_specs, out_specs=out_specs, check_vma=False)
```
